128 devices in a mesh: group: 8 (over y, core), tensor: 16 (over x, z).
Axes of the slice: x: 4, y: 4, z: 4, core: 2. Of those that a mesh axis runs over, the one named last changes fastest.
Arguments:
- hidden_states: bfloat16 [2048, 8192], P('group', 'tensor'), may hold values from -6 to 6
- norm_gain: bfloat16 [8192], replicated, may hold values from 0.25 to 1.75
- w_query: bfloat16 [8192, 8192], P(None, 'tensor'), may hold values from -0.0625 to 0.0625
- b_query: bfloat16 [8192], P('tensor'), may hold values from -4 to 4
- w_key: bfloat16 [8192, 1024], P(None, 'tensor'), may hold values from -0.0625 to 0.0625
- b_key: bfloat16 [1024], P('tensor'), may hold values from -4 to 4
- w_value: bfloat16 [8192, 1024], P(None, 'tensor'), may hold values from -0.0625 to 0.0625
- b_value: bfloat16 [1024], P('tensor'), may hold values from -4 to 4
- w_out: bfloat16 [8192, 8192], P('tensor'), may hold values from -0.0625 to 0.0625
- pool_keys: bfloat16 [2048, 8, 64, 128], P(('group', 'tensor')), may hold values from -80 to 80
- pool_values: bfloat16 [2048, 8, 64, 128], P(('group', 'tensor')), may hold values from -6 to 6
- conv_slots: int32 [32], replicated, may hold values from 0 to 31, as said below
- page_table: int32 [32, 64], replicated, may hold values from 0 to 2047, as said below
- prefix_len: int32 [32], replicated, may hold values from 1 to 4096, as said below
- suffix_len: int32 [32], replicated, may hold values from 1 to 64, as said below
- new_dest: int32 [32], replicated, may hold values from 0 to 127, as said below
Outputs:
- attn_out: bfloat16 [2048, 8192], P('group', 'tensor')
- new_keys: bfloat16 [128, 8, 64, 128], P(('group', 'tensor'))
- new_values: bfloat16 [128, 8, 64, 128], P(('group', 'tensor'))
The draws below stay inside these ranges and needn't reach their ends.
Inputs may be any that keep to these rules, and one draw needn't show every extreme that they name: A permutation: slot s, of group s // 4, holds conversation conv_slots[s]. `page_table`: entry = device * 16 + local slot, with device = group index * 16 + tensor index; the pages of a conversation held by group g lie in local slots g * 2 to (g + 1) * 2 - 1; every pool slot holds exactly one page. `prefix_len`: some conversation has exactly 4096. `suffix_len`: some conversation has exactly 64. `new_dest`: all distinct.
All inputs are finite; a program needn't handle non-finite values.
Results may differ from the reference program's by a relative error of at most 0.02.
Values may be sent and summed in bfloat16 or wider, within the bound.
A program may use at most 128 MiB of HBM per device.

```python
import jax
import jax.numpy as jnp
from jax import lax

D = 8192
HD = 128
SUF = 64
CONV_GRP = 4
PPC = 64
H = 64
KVH = 8
PAGE = 64
PRE = 4096
CONV = 32
TOKENS = 2048
SPG = 2
POOL_DEV = 16
POOL = 2048
N_GROUP = 8
DEVICES = 128


def place_tables(key):
    slots_conv = jax.random.permutation(jax.random.fold_in(key, 101), CONV)
    group_keys = jax.random.split(jax.random.fold_in(key, 102), N_GROUP)
    spread = jax.vmap(lambda group_key: jax.random.permutation(group_key, CONV_GRP * PPC))(group_keys)
    groups = jnp.arange(N_GROUP, dtype=jnp.int32)[:, None]
    slot_ids = spread // SPG * POOL_DEV + groups * SPG + spread % SPG
    by_slot = slot_ids.reshape(CONV, PPC).astype(jnp.int32)
    table = jnp.zeros((CONV, PPC), jnp.int32).at[slots_conv].set(by_slot)
    return (slots_conv.astype(jnp.int32), table)


def draw_conv_slots(key, part):
    shared = place_tables(key)
    return shared[0]


def draw_page_table(key, part):
    shared = place_tables(key)
    return shared[1]


def draw_prefix_len(key, part):
    key = jax.random.fold_in(key, 3)
    lengths = jax.random.randint(jax.random.fold_in(key, 1), (CONV,), 1, PRE + 1)
    chosen = jax.random.randint(jax.random.fold_in(key, 2), (), 0, CONV)
    return lengths.at[chosen].set(PRE).astype(jnp.int32)


def draw_suffix_len(key, part):
    key = jax.random.fold_in(key, 4)
    lengths = jax.random.randint(jax.random.fold_in(key, 1), (CONV,), 1, SUF + 1)
    chosen = jax.random.randint(jax.random.fold_in(key, 2), (), 0, CONV)
    return lengths.at[chosen].set(SUF).astype(jnp.int32)


def draw_new_dest(key, part):
    key = jax.random.fold_in(key, 5)
    return jax.random.permutation(key, DEVICES)[:CONV].astype(jnp.int32)


def draw_pool_keys(key, part):
    key = jax.random.fold_in(key, 7)
    shape = (POOL, KVH, PAGE, HD)
    base = jnp.clip(jax.random.normal(jax.random.fold_in(key, 1), shape, jnp.float32), -6.0, 6.0)
    return base.astype(jnp.bfloat16)


def steps_of(own_key, dims, cuts, least, largest):
    factor_of = 1.0
    for axis_at, shards_of in cuts:
        draws = jax.random.uniform(jax.random.fold_in(jax.random.fold_in(own_key, 6), axis_at), (shards_of,), jnp.float32, least / len(cuts), largest / len(cuts))
        factor_of = factor_of * jnp.repeat(jnp.exp(draws), dims[axis_at] // shards_of).reshape((-1,) + (1,) * (len(dims) - 1 - axis_at))
    return factor_of


def gaussian(rng, extent, scale, bound, cuts=(), held_as=jnp.bfloat16):
    drawn = jax.random.normal(rng, extent, jnp.float32) * scale
    if len(cuts) > 0:
        drawn = steps_of(rng, extent, cuts, -0.22, 0.18) * drawn
    return jnp.clip(drawn, min=-bound, max=bound).astype(held_as)


def setup_inputs(seed: int = 0) -> dict:
    key_of = jax.random.split(jax.random.key(seed), 17)
    hidden_states = gaussian(key_of[0], (TOKENS, D), 1.0, 6.0, ((0, 8), (1, 16)))
    norm_gain = jnp.clip(1.0 + 0.15 * jax.random.normal(key_of[1], (D,), jnp.float32), 0.25, 1.75).astype(jnp.bfloat16)
    w_query = gaussian(key_of[2], (D, H * HD), D ** -0.5, 0.0625, ((1, 16),))
    b_query = gaussian(key_of[3], (H * HD,), 1.0, 4.0, ((0, 16),))
    w_key = gaussian(key_of[4], (D, KVH * HD), D ** -0.5, 0.0625, ((1, 16),))
    b_key = gaussian(key_of[5], (KVH * HD,), 1.0, 4.0, ((0, 16),))
    w_value = gaussian(key_of[6], (D, KVH * HD), D ** -0.5, 0.0625, ((1, 16),))
    b_value = gaussian(key_of[7], (KVH * HD,), 1.0, 4.0, ((0, 16),))
    w_out = gaussian(key_of[8], (H * HD, D), (H * HD) ** -0.5, 0.0625, ((0, 16),))
    pool_keys = draw_pool_keys(jax.random.fold_in(key_of[16], 71), 0)
    pool_values = gaussian(key_of[10], (POOL, KVH, PAGE, HD), 1.0, 6.0, ((0, 128),))
    conv_slots = draw_conv_slots(jax.random.fold_in(key_of[16], 71), 0)
    page_table = draw_page_table(jax.random.fold_in(key_of[16], 71), 0)
    prefix_len = draw_prefix_len(jax.random.fold_in(key_of[16], 71), 0)
    suffix_len = draw_suffix_len(jax.random.fold_in(key_of[16], 71), 0)
    new_dest = draw_new_dest(jax.random.fold_in(key_of[16], 71), 0)
    return dict(hidden_states=hidden_states, norm_gain=norm_gain, w_query=w_query, b_query=b_query, w_key=w_key, b_key=b_key, w_value=w_value, b_value=b_value, w_out=w_out, pool_keys=pool_keys, pool_values=pool_values, conv_slots=conv_slots, page_table=page_table, prefix_len=prefix_len, suffix_len=suffix_len, new_dest=new_dest)


THETA = 1000000.0
EPSILON = 1e-06
NEGATIVE = -1e+30

def rotate(values, positions):
    width = values.shape[-1]
    half_width = width // 2
    freq = THETA ** (-(jnp.arange(half_width, dtype=jnp.float32) * 2.0 / width))
    angle = positions.astype(jnp.float32)[:, None] * freq[None, :]
    cosine = jnp.concatenate([jnp.cos(angle), jnp.cos(angle)], axis=1)[:, None, :]
    sine = jnp.concatenate([jnp.sin(angle), jnp.sin(angle)], axis=1)[:, None, :]
    turned = jnp.concatenate([-values[..., half_width:], values[..., :half_width]], axis=-1)
    return values * cosine + turned * sine

def normalize(rows, gain):
    wide = rows.astype(jnp.float32)
    factor = lax.rsqrt(lax.optimization_barrier(jnp.mean(wide * wide, axis=-1, keepdims=True)) + EPSILON)
    return (wide * factor * gain.astype(jnp.float32)).astype(jnp.bfloat16)

def reference(hidden_states, norm_gain, w_query, b_query, w_key, b_key, w_value, b_value, w_out, pool_keys, pool_values, conv_slots, page_table, prefix_len, suffix_len, new_dest):
    heads = w_query.shape[1] // HD
    kv_heads = w_key.shape[1] // HD
    ratio = heads // kv_heads

    def one_slot(slot):
        conv = conv_slots[slot]
        rows = lax.dynamic_slice_in_dim(hidden_states, slot * SUF, SUF, 0)
        normed = normalize(rows, norm_gain)
        offsets = jnp.arange(SUF, dtype=jnp.int32)
        positions = prefix_len[conv] + offsets
        query = jnp.dot(normed, w_query, preferred_element_type=jnp.float32) + b_query.astype(jnp.float32)
        query = rotate(query.reshape(SUF, heads, HD), positions).astype(jnp.bfloat16)
        key_raw = (jnp.dot(normed, w_key, preferred_element_type=jnp.float32) + b_key.astype(jnp.float32)).astype(jnp.bfloat16)
        value_new = (jnp.dot(normed, w_value, preferred_element_type=jnp.float32) + b_value.astype(jnp.float32)).astype(jnp.bfloat16)
        value_new = value_new.reshape(SUF, kv_heads, HD)
        key_new = rotate(key_raw.astype(jnp.float32).reshape(SUF, kv_heads, HD), positions).astype(jnp.bfloat16)
        pages = page_table[conv]
        old_keys = jnp.transpose(jnp.take(pool_keys, pages, axis=0), (1, 0, 2, 3)).reshape(kv_heads, PPC * PAGE, HD)
        old_values = jnp.transpose(jnp.take(pool_values, pages, axis=0), (1, 0, 2, 3)).reshape(kv_heads, PPC * PAGE, HD)
        all_keys = jnp.concatenate([old_keys, jnp.transpose(key_new, (1, 0, 2))], axis=1).astype(jnp.float32)
        all_values = jnp.concatenate([old_values, jnp.transpose(value_new, (1, 0, 2))], axis=1).astype(jnp.float32)
        alive = jnp.arange(PPC * PAGE, dtype=jnp.int32) < prefix_len[conv]
        mask_old = jnp.broadcast_to(alive[None, :], (SUF, PPC * PAGE))
        mask_new = offsets[None, :] <= offsets[:, None]
        mask = jnp.concatenate([mask_old, mask_new], axis=1)
        grouped = query.astype(jnp.float32).reshape(SUF, kv_heads, ratio, HD)
        scores = jnp.einsum('ikgd,kjd->kgij', grouped, all_keys) * HD ** (-0.5)
        scores = jnp.where(mask[None, None], scores, NEGATIVE)
        peak = lax.optimization_barrier(jnp.max(scores, axis=-1, keepdims=True))
        weights = jnp.exp(scores - peak)
        total = lax.optimization_barrier(jnp.sum(weights, axis=-1))
        rounded = lax.optimization_barrier(weights.astype(jnp.bfloat16)).astype(jnp.float32)
        mixed = jnp.einsum('kgij,kjd->ikgd', rounded, all_values)
        mixed = mixed / jnp.transpose(total, (2, 0, 1))[..., None]
        live_rows = offsets < suffix_len[conv]
        mixed = jnp.where(live_rows[:, None, None, None], mixed, jnp.zeros_like(mixed))
        mixed = mixed.astype(jnp.bfloat16).reshape(SUF, heads * HD)
        result = jnp.dot(mixed, w_out, preferred_element_type=jnp.float32).astype(jnp.bfloat16)
        page_keys = jnp.where(live_rows[:, None, None], key_new, jnp.zeros_like(key_new))
        page_values = jnp.where(live_rows[:, None, None], value_new, jnp.zeros_like(value_new))
        return (result, jnp.transpose(page_keys, (1, 0, 2)), jnp.transpose(page_values, (1, 0, 2)), new_dest[conv])
    results, page_keys, page_values, dests = lax.map(one_slot, jnp.arange(CONV, dtype=jnp.int32))
    new_keys = jnp.zeros((DEVICES, kv_heads, SUF, HD), jnp.bfloat16).at[dests].set(page_keys)
    new_values = jnp.zeros((DEVICES, kv_heads, SUF, HD), jnp.bfloat16).at[dests].set(page_values)
    return (results.reshape(CONV * SUF, results.shape[-1]), new_keys, new_values)
```

```python
import jax
import jax.numpy as jnp
import numpy as np
from jax import lax
from jax.experimental import pallas as pl
from jax.experimental.pallas import tpu as pltpu
from jax.sharding import PartitionSpec as P

HD = 128
SUF = 64
CONVS = 4
ROWS = CONVS * SUF
GROUPS = 8
TENSOR = 16
WIDTH = 8192
PART = WIDTH // TENSOR
PAGES = 64
PAGE = 64
HEADS = 4
THETA = 1000000.0
EPSILON = 1e-06
NEGATIVE = -1e30
SCALE = HD**-0.5 * 1.4426950408889634
LN2 = 0.6931471805599453
MESH = pl.DeviceIdType.MESH
BF16 = jnp.bfloat16
F32 = jnp.float32
I32 = jnp.int32


def remote(src, dst, send_sem, recv_sem, group, tensor):
    return pltpu.make_async_remote_copy(
        src_ref=src,
        dst_ref=dst,
        send_sem=send_sem,
        recv_sem=recv_sem,
        device_id=(group, tensor),
        device_id_type=MESH,
    )


def place():
    group = lax.axis_index("group")
    tensor = lax.axis_index("tensor")
    return (
        group,
        tensor,
        lax.div(group, 2),
        lax.rem(group, 2),
        lax.div(tensor, 4),
        lax.rem(tensor, 4),
    )


def offset_device(off, y, core, x, z):
    flip = lax.rem(off, 2)
    other_x = lax.rem(x + lax.rem(lax.div(off, 2), 4), 4)
    other_core = lax.rem(core + lax.rem(lax.div(off, 8), 2), 2)
    other_y = lax.rem(y + lax.div(off, 16), 4)
    other_z = z + flip * (3 - 2 * z)
    return other_y * 2 + other_core, other_x, other_z


def lane_iota(shape):
    return lax.broadcasted_iota(I32, shape, len(shape) - 1)


def row_iota(shape):
    return lax.broadcasted_iota(I32, shape, len(shape) - 2)


def gather_kernel(
    conv_ref,
    prefix_ref,
    suffix_ref,
    dest_ref,
    table_ref,
    hidden,
    pool_k,
    pool_v,
    w_query,
    w_key,
    w_value,
    gain_ref,
    b_query,
    b_key,
    b_value,
    freq_ref,
    got_k,
    got_v,
    query_own,
    query_other,
    key_new,
    value_new,
    lists,
    new_pages,
    feat,
    wq,
    wk,
    wv,
    acc_q,
    acc_k,
    acc_v,
    kv_own,
    kv_other,
    new_all,
    new_send,
    local_sem,
    ring_send,
    ring_recv,
    pool_send,
    pool_recv,
    pair_send,
    pair_recv,
    group_send,
    group_recv,
    page_send,
    page_recv,
):
    group, tensor, y, core, x, z = place()
    pair_z = z + 1 - 2 * lax.rem(z, 2)
    parity = lax.rem(z, 2)
    own = pltpu.make_async_copy(hidden, feat.at[x, z], local_sem.at[0])
    own.start()
    loads = [
        pltpu.make_async_copy(w_query, wq, local_sem.at[1]),
        pltpu.make_async_copy(w_key, wk, local_sem.at[2]),
        pltpu.make_async_copy(w_value, wv, local_sem.at[3]),
    ]
    for load in loads:
        load.start()
    my_head = 2 * x + lax.div(z, 2)
    keep = [
        pltpu.make_async_copy(
            pool_k.at[pl.ds(2 * group, 2), my_head], got_k.at[0], local_sem.at[4]
        ),
        pltpu.make_async_copy(
            pool_v.at[pl.ds(2 * group, 2), my_head], got_v.at[0], local_sem.at[5]
        ),
    ]
    for copy in keep:
        copy.start()

    barrier = pltpu.get_barrier_semaphore()

    def greet(off, carry):
        to_group, to_x, to_z = offset_device(off, y, core, x, z)
        pl.semaphore_signal(
            barrier, inc=1, device_id=(to_group, to_x * 4 + to_z), device_id_type=MESH
        )
        return carry

    lax.fori_loop(1, 64, greet, 0)

    def greet_rest(off, carry):
        to_x = lax.div(off, 2)
        to_z = pair_z + lax.rem(off, 2) * (3 - 2 * pair_z)
        pl.semaphore_signal(
            barrier, inc=1, device_id=(group, to_x * 4 + to_z), device_id_type=MESH
        )
        return carry

    lax.fori_loop(0, 8, greet_rest, 0)
    pl.semaphore_wait(barrier, 71)

    own.wait()
    x_up, x_down = lax.rem(x + 1, 4), lax.rem(x + 3, 4)
    z_up, z_down = lax.rem(z + 1, 4), lax.rem(z + 3, 4)
    to_x_up, to_x_down = x_up * 4 + z, x_down * 4 + z
    to_z_up, to_z_down = x * 4 + z_up, x * 4 + z_down
    sent = []

    def ring(index, ref, to):
        copy = remote(ref, ref, ring_send.at[index], ring_recv.at[index], group, to)
        copy.start()
        sent.append(copy)
        return copy

    half_a, half_b = pl.ds(0, 128), pl.ds(128, 128)
    a0 = ring(0, feat.at[x, z, half_a], to_x_up)
    a1 = ring(1, feat.at[x, z, half_a], to_x_down)
    b0 = ring(2, feat.at[x, z, half_b], to_z_up)
    b1 = ring(3, feat.at[x, z, half_b], to_z_down)

    def pool_copies(off):
        to_group, to_x, to_z = offset_device(off, y, core, x, z)
        to = to_x * 4 + to_z
        head = 2 * to_x + lax.div(to_z, 2)
        slots = pl.ds(2 * to_group, 2)
        return (
            remote(
                pool_k.at[slots, head],
                got_k.at[off],
                pool_send.at[0, off],
                pool_recv.at[0, off],
                to_group,
                to,
            ),
            remote(
                pool_v.at[slots, head],
                got_v.at[off],
                pool_send.at[1, off],
                pool_recv.at[1, off],
                to_group,
                to,
            ),
        )

    def push(off, carry):
        first, second = pool_copies(off)
        first.start()
        second.start()
        return carry

    lax.fori_loop(1, 64, push, 0)

    a0.wait_recv()
    a2 = ring(4, feat.at[x_down, z, pl.ds(0, 64)], to_x_up)
    a1.wait_recv()
    a3 = ring(5, feat.at[x_up, z, pl.ds(64, 64)], to_x_down)
    b0.wait_recv()
    b2 = ring(6, feat.at[x, z_down, pl.ds(128, 64)], to_z_up)
    b1.wait_recv()
    b3 = ring(7, feat.at[x, z_up, pl.ds(192, 64)], to_z_down)
    a2.wait_recv()
    a3.wait_recv()
    a4 = ring(8, feat.at[:, z, half_a], to_z_up)
    a5 = ring(9, feat.at[:, z, half_a], to_z_down)
    b2.wait_recv()
    b3.wait_recv()
    b4 = ring(10, feat.at[x, :, half_b], to_x_up)
    b5 = ring(11, feat.at[x, :, half_b], to_x_down)

    prefix = [prefix_ref[conv_ref[group * CONVS + i]] for i in range(CONVS)]
    suffix = [suffix_ref[conv_ref[group * CONVS + i]] for i in range(CONVS)]

    offsets = row_iota((SUF, HD))
    positions = jnp.concatenate([offsets + prefix[i] for i in range(CONVS)], axis=0)
    angle = positions.astype(F32) * freq_ref[...]
    cosine = jnp.cos(angle)
    sine = jnp.sin(angle)
    sine = jnp.where(lane_iota((ROWS, HD)) < HD // 2, -sine, sine)

    page_ids = lane_iota((1, PAGES))
    below = (row_iota((PAGES, PAGES)) < lane_iota((PAGES, PAGES))).astype(F32)
    lane = lane_iota((PAGES, HD))
    table = jnp.zeros((PAGES, HD), F32)
    counts = jnp.zeros((8, HD), F32)
    for i in range(CONVS):
        entry = table_ref[pl.ds(conv_ref[group * CONVS + i], 1), :]
        source = entry >> 4
        source_y, source_core = source >> 5, (source >> 4) & 1
        source_x, source_z = (source >> 2) & 3, source & 3
        live = jnp.clip(prefix[i] - page_ids * PAGE, 0, PAGE)
        here = ((source_z == z) | (source_z == 3 - z)) & (live > 0)
        off = (((y - source_y) & 3) * 2 + ((core - source_core) & 1)) * 4
        off = (off + ((x - source_x) & 3)) * 2 + jnp.where(source_z == z, 0, 1)
        value = ((off * 2 + (entry & 1)) * 128 + live).astype(F32)
        here_f = here.astype(F32)
        order = jnp.dot(
            jnp.broadcast_to(here_f, (8, PAGES)), below, preferred_element_type=F32
        )[0:1, :]
        match = (order == row_iota((PAGES, PAGES)).astype(F32)) & (
            jnp.broadcast_to(here_f, (PAGES, PAGES)) > 0.5
        )
        column = jnp.sum(jnp.where(match, value, 0.0), axis=1, keepdims=True)
        table = jnp.where(lane == i, column, table)
        counts = jnp.where(
            lane_iota((8, HD)) == i, jnp.sum(here_f, axis=1, keepdims=True), counts
        )
    lists[pl.ds(0, PAGES), :] = table.astype(I32)
    lists[pl.ds(PAGES, 8), :] = counts.astype(I32)

    a4.wait_recv()
    a6 = ring(12, feat.at[:, z_down, pl.ds(0, 64)], to_z_up)
    a5.wait_recv()
    a7 = ring(13, feat.at[:, z_up, pl.ds(64, 64)], to_z_down)
    b4.wait_recv()
    b6 = ring(14, feat.at[x_down, :, pl.ds(128, 64)], to_x_up)
    b5.wait_recv()
    b7 = ring(15, feat.at[x_up, :, pl.ds(192, 64)], to_x_down)
    for load in loads:
        load.wait()
    for copy in (a6, a7, b6, b7):
        copy.wait_recv()

    def square(bx, total):
        for bz in range(4):
            wide = feat[bx, bz].astype(F32)
            wide = wide * wide
            for part in range(PART // HD):
                total = total + wide[:, part * HD : (part + 1) * HD]
        return total

    total = lax.fori_loop(0, 4, square, jnp.zeros((ROWS, HD), F32))
    factor = lax.rsqrt(jnp.sum(total, axis=1, keepdims=True) * (1.0 / WIDTH) + EPSILON)
    acc_q[...] = jnp.zeros_like(acc_q)
    acc_k[...] = jnp.zeros_like(acc_k)
    acc_v[...] = jnp.zeros_like(acc_v)

    def project(bx, carry):
        for bz in range(4):
            block = bx * 4 + bz
            rows = pl.ds(pl.multiple_of(block * PART, PART), PART)
            wide = feat[bx, bz].astype(F32)
            normed = (wide * factor * gain_ref[block]).astype(BF16)
            acc_q[...] += jnp.dot(normed, wq[rows, :], preferred_element_type=F32)
            acc_k[...] += jnp.dot(normed, wk[rows, :], preferred_element_type=F32)
            acc_v[...] += jnp.dot(normed, wv[rows, :], preferred_element_type=F32)
        return carry

    lax.fori_loop(0, 4, project, 0)

    kv_own[...] = jnp.concatenate(
        [
            acc_k[...] + b_key[...].astype(F32),
            acc_v[...] + b_value[...].astype(F32),
        ],
        axis=1,
    ).astype(BF16)
    pair = x * 4 + pair_z
    kv_copy = remote(kv_own, kv_other, pair_send.at[0], pair_recv.at[0], group, pair)
    kv_copy.start()

    def rotate(values):
        return values * cosine + pltpu.roll(values, HD // 2, 1) * sine

    for head in range(HEADS):
        columns = slice(head * HD, (head + 1) * HD)
        values = acc_q[:, columns] + b_query[:, columns].astype(F32)
        values = rotate(values).astype(BF16)
        for i in range(CONVS):
            query_own[i, head * SUF : (head + 1) * SUF, :] = values[i * SUF : (i + 1) * SUF, :]
    query_copy = remote(
        query_own, query_other, pair_send.at[1], pair_recv.at[1], group, pair
    )
    query_copy.start()

    kv_copy.wait_recv()
    mine = kv_own[...].astype(F32)
    theirs = kv_other[...].astype(F32)
    even = jnp.where(parity == 0, mine, theirs)
    odd = jnp.where(parity == 0, theirs, mine)
    low = lane_iota((ROWS, HD)) < HD // 2
    keys = jnp.where(low, even, pltpu.roll(odd, HD // 2, 1))
    keys = rotate(keys)
    values = jnp.where(low, pltpu.roll(even, HD // 2, 1), odd)
    key_new[...] = keys.astype(BF16)
    value_new[...] = values.astype(BF16)

    page = jnp.where(parity == 0, keys.astype(BF16).astype(F32), values)
    live_row = jnp.concatenate([offsets < suffix[i] for i in range(CONVS)], axis=0)
    page = jnp.where(live_row, page, 0.0).astype(BF16)
    new_all[pl.ds(group * CONVS, CONVS)] = page.reshape(CONVS, SUF, HD)

    def group_copy(off):
        to_y = lax.rem(y + lax.div(off, 2), 4)
        to_core = lax.rem(core + lax.rem(off, 2), 2)
        ref = new_all.at[pl.ds(group * CONVS, CONVS)]
        return remote(
            ref, ref, group_send.at[off], group_recv.at[off], to_y * 2 + to_core, tensor
        )

    def group_start(off, carry):
        group_copy(off).start()
        return carry

    lax.fori_loop(1, 8, group_start, 0)

    def group_wait(off, carry):
        group_copy(off).wait_recv()
        return carry

    lax.fori_loop(1, 8, group_wait, 0)

    def choose(to, carry):
        target = group * TENSOR + to
        index = jnp.int32(0)
        found = jnp.float32(0)
        for slot in range(GROUPS * CONVS):
            hit = dest_ref[conv_ref[slot]] == target
            index = jnp.where(hit, slot, index)
            found = jnp.where(hit, 1.0, found)
        new_send[to] = (new_all[index].astype(F32) * found).astype(BF16)
        return carry

    lax.fori_loop(0, TENSOR, choose, 0)
    mine_copy = pltpu.make_async_copy(
        new_send.at[tensor], new_pages.at[tensor], local_sem.at[6]
    )
    mine_copy.start()

    def page_copy(off):
        to = lax.rem(tensor + off, TENSOR)
        return remote(
            new_send.at[to],
            new_pages.at[tensor],
            page_send.at[off],
            page_recv.at[off],
            group,
            to,
        )

    def page_start(off, carry):
        page_copy(off).start()
        return carry

    lax.fori_loop(1, TENSOR, page_start, 0)

    mine_copy.wait()
    for copy in keep:
        copy.wait()
    for copy in sent:
        copy.wait_send()
    kv_copy.wait_send()
    query_copy.wait()

    def group_end(off, carry):
        group_copy(off).wait_send()
        return carry

    lax.fori_loop(1, 8, group_end, 0)

    def page_end(off, carry):
        page_copy(off).wait()
        return carry

    lax.fori_loop(1, TENSOR, page_end, 0)

    def pool_end(off, carry):
        first, second = pool_copies(off)
        first.wait()
        second.wait()
        return carry

    lax.fori_loop(1, 64, pool_end, 0)


def attend_kernel(
    lists,
    got_k,
    got_v,
    query_own,
    query_other,
    key_new,
    value_new,
    mixed_own,
    mixed_other,
    lse_own,
    lse_other,
):
    half = HEADS * SUF
    token = row_iota((SUF, 2 * half))
    causal = row_iota((SUF, half)) <= (lane_iota((SUF, half)) & (SUF - 1))
    step = 4

    def one(i, carry):
        first = query_own[i]
        both = jnp.concatenate([first, query_other[i]], axis=0)
        rows = pl.ds(pl.multiple_of(i * SUF, SUF), SUF)
        scores = lax.dot_general(
            key_new[rows, :], first, (((1,), (1,)), ((), ())), preferred_element_type=F32
        )
        scores = jnp.where(causal, scores * SCALE, NEGATIVE)
        peak = jnp.max(scores, axis=0, keepdims=True)
        weights = jnp.exp2(scores - peak)
        total = jnp.sum(weights, axis=0, keepdims=True)
        accum = lax.dot_general(
            value_new[rows, :],
            weights.astype(BF16),
            (((0,), (0,)), ((), ())),
            preferred_element_type=F32,
        )
        peak = jnp.concatenate([peak, jnp.full((1, half), NEGATIVE, F32)], axis=1)
        total = jnp.concatenate([total, jnp.zeros((1, half), F32)], axis=1)
        accum = jnp.concatenate([accum, jnp.zeros((HD, half), F32)], axis=1)
        count = lists[PAGES, i]

        def block(b, state):
            peak, total, accum = state
            codes = [lists[b * step + p, i] for p in range(step)]
            where = [code >> 7 for code in codes]
            keys = jnp.concatenate([got_k[w] for w in where], axis=0)
            values = jnp.concatenate([got_v[w] for w in where], axis=0)
            scores = lax.dot_general(
                keys, both, (((1,), (1,)), ((), ())), preferred_element_type=F32
            )
            scores = jnp.concatenate(
                [
                    jnp.where(
                        token < (codes[p] & 127),
                        scores[p * PAGE : (p + 1) * PAGE] * SCALE,
                        NEGATIVE,
                    )
                    for p in range(step)
                ],
                axis=0,
            )
            fresh = jnp.maximum(peak, jnp.max(scores, axis=0, keepdims=True))
            shrink = jnp.exp2(peak - fresh)
            weights = jnp.exp2(scores - fresh)
            total = total * shrink + jnp.sum(weights, axis=0, keepdims=True)
            accum = accum * shrink + lax.dot_general(
                values,
                weights.astype(BF16),
                (((0,), (0,)), ((), ())),
                preferred_element_type=F32,
            )
            return fresh, total, accum

        peak, total, accum = lax.fori_loop(
            0, (count + step - 1) >> 2, block, (peak, total, accum)
        )
        some = total > 0.0
        safe = jnp.where(some, total, 1.0)
        mixed = (accum / safe).astype(BF16)
        lse = jnp.where(some, peak + jnp.log(safe) * (1.0 / LN2), NEGATIVE)
        lse = jnp.broadcast_to(lse, (8, 2 * half))
        mixed_own[i] = mixed[:, :half]
        mixed_other[i] = mixed[:, half:]
        lse_own[i] = lse[:, :half]
        lse_other[i] = lse[:, half:]
        return carry

    lax.fori_loop(0, CONVS, one, 0)


def reduce_kernel(
    conv_ref,
    suffix_ref,
    mixed_own,
    mixed_other,
    lse_own,
    lse_other,
    w_out,
    out_ref,
    weights,
    mixed_got,
    lse_got,
    mixed,
    part,
    ring_a,
    ring_b,
    small_a,
    small_b,
    local_sem,
    pair_send,
    pair_recv,
    ring_send,
    ring_recv,
):
    group, tensor, y, core, x, z = place()
    pair_z = z + 1 - 2 * lax.rem(z, 2)
    load = pltpu.make_async_copy(w_out, weights, local_sem.at[0])
    load.start()
    x_up, x_down = lax.rem(x + 1, 4), lax.rem(x + 3, 4)
    z_up, z_down = lax.rem(z + 1, 4), lax.rem(z + 3, 4)
    x_far, z_far = lax.rem(x + 2, 4), lax.rem(z + 2, 4)
    to_x_up, to_x_down = x_up * 4 + z, x_down * 4 + z
    to_z_up, to_z_down = x * 4 + z_up, x * 4 + z_down
    barrier = pltpu.get_barrier_semaphore()
    for to in (to_x_up, to_x_down, to_z_up, to_z_down):
        pl.semaphore_signal(barrier, inc=1, device_id=(group, to), device_id_type=MESH)
    pl.semaphore_wait(barrier, 4)

    pair = x * 4 + pair_z
    mixed_copy = remote(mixed_other, mixed_got, pair_send.at[0], pair_recv.at[0], group, pair)
    lse_copy = remote(lse_other, lse_got, pair_send.at[1], pair_recv.at[1], group, pair)
    lse_copy.start()
    mixed_copy.start()
    lse_copy.wait()
    mixed_copy.wait()
    half = HEADS * SUF
    row_of = lane_iota((1, half)) & (SUF - 1)
    for i in range(CONVS):
        first, second = lse_own[i, 0:1, :], lse_got[i, 0:1, :]
        peak = jnp.maximum(first, second)
        first, second = jnp.exp2(first - peak), jnp.exp2(second - peak)
        scale = jnp.where(row_of < suffix_ref[conv_ref[group * CONVS + i]], 1.0, 0.0)
        scale = scale / (first + second)
        joined = mixed_own[i].astype(F32) * (first * scale) + mixed_got[i].astype(F32) * (
            second * scale
        )
        turned = jnp.transpose(joined).astype(BF16)
        for head in range(HEADS):
            mixed[i * SUF : (i + 1) * SUF, head * HD : (head + 1) * HD] = turned[
                head * SUF : (head + 1) * SUF, :
            ]
    load.wait()

    def project(bx, carry):
        for bz in range(4):
            columns = pl.ds(pl.multiple_of((bx * 4 + bz) * PART, PART), PART)
            part[bx, bz] = jnp.dot(
                mixed[...], weights[:, columns], preferred_element_type=F32
            ).astype(BF16)
        return carry

    lax.fori_loop(0, 4, project, 0)

    pending = []

    class Ring:
        def __init__(self, base, first_sem, pick, buffers, ups):
            self.base, self.sem, self.pick, self.buffers = base, first_sem, pick, buffers
            self.up, self.down, self.me, self.far, self.to_up, self.to_down = ups
            self.top, self.bottom = pl.ds(base, 64), pl.ds(base + 64, 64)

        def send(self, index, ref, to):
            sem = self.sem + index
            copy = remote(
                ref,
                self.buffers.at[index],
                ring_send.at[sem],
                ring_recv.at[sem],
                group,
                to,
            )
            copy.start()
            pending.append(copy)
            return copy

        def start(self):
            pick = self.pick
            self.c0 = self.send(0, pick(self.far, self.top), self.to_up)
            self.c1 = self.send(1, pick(self.far, self.bottom), self.to_down)
            self.c2 = self.send(2, pick(self.up, self.bottom), self.to_up)
            self.c3 = self.send(3, pick(self.down, self.top), self.to_down)

        def add(self, ref, *indices):
            total = ref[...].astype(F32)
            for index in indices:
                total = total + self.buffers[index].astype(F32)
            ref[...] = total.astype(BF16)

        def relay(self):
            pick = self.pick
            self.c0.wait_recv()
            self.add(pick(self.up, self.top), 0)
            self.c4 = self.send(4, pick(self.up, self.top), self.to_up)
            self.c1.wait_recv()
            self.add(pick(self.down, self.bottom), 1)
            self.c5 = self.send(5, pick(self.down, self.bottom), self.to_down)

        def finish(self):
            pick = self.pick
            self.c3.wait_recv()
            self.c4.wait_recv()
            self.add(pick(self.me, self.top), 3, 4)
            self.c2.wait_recv()
            self.c5.wait_recv()
            self.add(pick(self.me, self.bottom), 2, 5)

    along_x = (x_up, x_down, x, x_far, to_x_up, to_x_down)
    along_z = (z_up, z_down, z, z_far, to_z_up, to_z_down)
    big_a = Ring(0, 0, lambda j, rows: part.at[:, j, rows], ring_a, along_z)
    big_b = Ring(128, 6, lambda j, rows: part.at[j, :, rows], ring_b, along_x)
    end_a = Ring(0, 12, lambda j, rows: part.at[j, z, rows], small_a, along_x)
    end_b = Ring(128, 18, lambda j, rows: part.at[x, j, rows], small_b, along_z)
    big_a.start()
    big_b.start()
    big_a.relay()
    big_b.relay()
    big_a.finish()
    end_a.start()
    big_b.finish()
    end_b.start()
    end_a.relay()
    end_b.relay()
    end_a.finish()
    end_b.finish()
    out_ref[...] = part[x, z]
    for copy in pending:
        copy.wait_send()


def any_spec():
    return pl.BlockSpec(memory_space=pl.ANY)


def vmem_spec():
    return pl.BlockSpec(memory_space=pltpu.VMEM)


def smem_spec():
    return pl.BlockSpec(memory_space=pltpu.SMEM)


def shards(
    hidden_states,
    norm_gain,
    w_query,
    b_query,
    w_key,
    b_key,
    w_value,
    b_value,
    w_out,
    pool_keys,
    pool_values,
    conv_slots,
    page_table,
    prefix_len,
    suffix_len,
    new_dest,
):
    dma = pltpu.SemaphoreType.DMA
    freq = THETA ** (-(np.arange(HD // 2, dtype=np.float64) * 2.0 / HD))
    freq = jnp.asarray(np.concatenate([freq, freq])[None, :], F32)
    shape = jax.ShapeDtypeStruct
    got_k, got_v, query_own, query_other, key_new, value_new, lists, new_pages = pl.pallas_call(
        gather_kernel,
        out_shape=[
            shape((64, 2, PAGE, HD), BF16),
            shape((64, 2, PAGE, HD), BF16),
            shape((CONVS, HEADS * SUF, HD), BF16),
            shape((CONVS, HEADS * SUF, HD), BF16),
            shape((ROWS, HD), BF16),
            shape((ROWS, HD), BF16),
            shape((PAGES + 8, HD), I32),
            shape((TENSOR, SUF, HD), BF16),
        ],
        in_specs=[smem_spec()] * 4
        + [vmem_spec()]
        + [any_spec()] * 6
        + [vmem_spec()] * 5,
        out_specs=[
            any_spec(),
            any_spec(),
            vmem_spec(),
            any_spec(),
            vmem_spec(),
            vmem_spec(),
            vmem_spec(),
            any_spec(),
        ],
        scratch_shapes=[
            pltpu.VMEM((4, 4, ROWS, PART), BF16),
            pltpu.VMEM((WIDTH, HEADS * HD), BF16),
            pltpu.VMEM((WIDTH, HD // 2), BF16),
            pltpu.VMEM((WIDTH, HD // 2), BF16),
            pltpu.VMEM((ROWS, HEADS * HD), F32),
            pltpu.VMEM((ROWS, HD // 2), F32),
            pltpu.VMEM((ROWS, HD // 2), F32),
            pltpu.VMEM((ROWS, HD), BF16),
            pltpu.VMEM((ROWS, HD), BF16),
            pltpu.VMEM((GROUPS * CONVS, SUF, HD), BF16),
            pltpu.VMEM((TENSOR, SUF, HD), BF16),
            dma((8,)),
            dma((16,)),
            dma((16,)),
            dma((2, 64)),
            dma((2, 64)),
            dma((2,)),
            dma((2,)),
            dma((8,)),
            dma((8,)),
            dma((16,)),
            dma((16,)),
        ],
        compiler_params=pltpu.CompilerParams(
            collective_id=0, has_side_effects=True, vmem_limit_bytes=48 * 1024 * 1024
        ),
        name="gather",
    )(
        conv_slots,
        prefix_len,
        suffix_len,
        new_dest,
        page_table,
        hidden_states,
        pool_keys,
        pool_values,
        w_query,
        w_key,
        w_value,
        norm_gain.astype(F32).reshape(TENSOR, 1, PART),
        b_query.reshape(1, HEADS * HD),
        b_key.reshape(1, HD // 2),
        b_value.reshape(1, HD // 2),
        freq,
    )
    mixed_own, mixed_other, lse_own, lse_other = pl.pallas_call(
        attend_kernel,
        out_shape=[
            shape((CONVS, HD, HEADS * SUF), BF16),
            shape((CONVS, HD, HEADS * SUF), BF16),
            shape((CONVS, 8, HEADS * SUF), F32),
            shape((CONVS, 8, HEADS * SUF), F32),
        ],
        in_specs=[smem_spec()] + [vmem_spec()] * 6,
        out_specs=[vmem_spec()] * 4,
        compiler_params=pltpu.CompilerParams(vmem_limit_bytes=32 * 1024 * 1024),
        name="attend",
    )(
        lists,
        got_k.reshape(128, PAGE, HD),
        got_v.reshape(128, PAGE, HD),
        query_own,
        query_other,
        key_new,
        value_new,
    )
    attn_out = pl.pallas_call(
        reduce_kernel,
        out_shape=shape((ROWS, PART), BF16),
        in_specs=[smem_spec()] * 2 + [vmem_spec()] * 4 + [any_spec()],
        out_specs=vmem_spec(),
        scratch_shapes=[
            pltpu.VMEM((HEADS * HD, WIDTH), BF16),
            pltpu.VMEM((CONVS, HD, HEADS * SUF), BF16),
            pltpu.VMEM((CONVS, 8, HEADS * SUF), F32),
            pltpu.VMEM((ROWS, HEADS * HD), BF16),
            pltpu.VMEM((4, 4, ROWS, PART), BF16),
            pltpu.VMEM((6, 4, 64, PART), BF16),
            pltpu.VMEM((6, 4, 64, PART), BF16),
            pltpu.VMEM((6, 64, PART), BF16),
            pltpu.VMEM((6, 64, PART), BF16),
            dma((1,)),
            dma((2,)),
            dma((2,)),
            dma((24,)),
            dma((24,)),
        ],
        compiler_params=pltpu.CompilerParams(
            collective_id=1, has_side_effects=True, vmem_limit_bytes=40 * 1024 * 1024
        ),
        name="reduce",
    )(conv_slots, suffix_len, mixed_own, mixed_other, lse_own, lse_other, w_out)
    pages = new_pages.reshape(TENSOR // 2, 2, SUF, HD)
    return (attn_out, pages[None, :, 0], pages[None, :, 1])


def solution(mesh):
    in_specs = (
        P("group", "tensor"),
        P(),
        P(None, "tensor"),
        P("tensor"),
        P(None, "tensor"),
        P("tensor"),
        P(None, "tensor"),
        P("tensor"),
        P("tensor", None),
        P(("group", "tensor"), None, None, None),
        P(("group", "tensor"), None, None, None),
        P(),
        P(),
        P(),
        P(),
        P(),
    )
    out_specs = (
        P("group", "tensor"),
        P(("group", "tensor"), None, None, None),
        P(("group", "tensor"), None, None, None),
    )
    return jax.shard_map(shards, mesh=mesh, in_specs=in_specs, out_specs=out_specs, check_vma=False)
```

```python
import jax
import jax.numpy as jnp
import numpy as np
from jax import lax
from jax.experimental import pallas as pl
from jax.experimental.pallas import tpu as pltpu
from jax.sharding import PartitionSpec as P

HD = 128
SUF = 64
CONVS = 4
ROWS = CONVS * SUF
GROUPS = 8
TENSOR = 16
WIDTH = 8192
PART = WIDTH // TENSOR
PAGES = 64
PAGE = 64
HEADS = 4
THETA = 1000000.0
EPSILON = 1e-06
NEGATIVE = -1e30
SCALE = HD**-0.5 * 1.4426950408889634
LN2 = 0.6931471805599453
MESH = pl.DeviceIdType.MESH
BF16 = jnp.bfloat16
F32 = jnp.float32
I32 = jnp.int32


def remote(src, dst, send_sem, recv_sem, group, tensor):
    return pltpu.make_async_remote_copy(
        src_ref=src,
        dst_ref=dst,
        send_sem=send_sem,
        recv_sem=recv_sem,
        device_id=(group, tensor),
        device_id_type=MESH,
    )


def place():
    group = lax.axis_index("group")
    tensor = lax.axis_index("tensor")
    return (
        group,
        tensor,
        lax.div(group, 2),
        lax.rem(group, 2),
        lax.div(tensor, 4),
        lax.rem(tensor, 4),
    )


def lane_iota(shape):
    return lax.broadcasted_iota(I32, shape, len(shape) - 1)


def row_iota(shape):
    return lax.broadcasted_iota(I32, shape, len(shape) - 2)


def gather_kernel(
    conv_ref,
    prefix_ref,
    suffix_ref,
    dest_ref,
    table_ref,
    hidden,
    pool_k,
    pool_v,
    w_query,
    w_key,
    w_value,
    gain_ref,
    b_query,
    b_key,
    b_value,
    freq_ref,
    got_k,
    got_v,
    queries,
    key_new,
    value_new,
    lists,
    new_pages,
    feat,
    wq,
    wkv,
    acc_q,
    acc_kv,
    squares,
    stage_k,
    stage_v,
    query_own,
    kv_own,
    kv_other,
    new_all,
    new_send,
    load_sem,
    keep_sem,
    feat_send,
    feat_recv,
    y_send,
    y_recv,
    x_send,
    x_recv,
    pair_send,
    pair_recv,
    group_send,
    group_recv,
    page_send,
    page_recv,
):
    group, tensor, y, core, x, z = place()
    parity = lax.rem(z, 2)
    partner_z = [z, z + 1 - 2 * parity, lax.rem(z + 2, 4), 3 - z]
    own = pltpu.make_async_copy(hidden, feat.at[x, z], load_sem.at[0])
    own.start()
    loads = [
        pltpu.make_async_copy(w_query, wq, load_sem.at[1]),
        pltpu.make_async_copy(w_key, wkv.at[pl.ds(0, HD // 2)], load_sem.at[2]),
        pltpu.make_async_copy(w_value, wkv.at[pl.ds(HD // 2, HD // 2)], load_sem.at[3]),
    ]
    for load in loads:
        load.start()

    def group_at(shift):
        to_y = lax.rem(y + shift // 2, 4)
        to_core = lax.rem(core + shift % 2, 2)
        return to_y * 2 + to_core

    barrier = pltpu.get_barrier_semaphore()
    for shift in range(1, GROUPS):
        pl.semaphore_signal(
            barrier, inc=1, device_id=(group_at(shift), tensor), device_id_type=MESH
        )

    def greet(off, carry):
        to = lax.rem(tensor + off, TENSOR)
        pl.semaphore_signal(barrier, inc=1, device_id=(group, to), device_id_type=MESH)
        return carry

    lax.fori_loop(1, TENSOR, greet, 0)
    pl.semaphore_wait(barrier, GROUPS - 1 + TENSOR - 1)

    own.wait()
    x_at = [lax.rem(x + shift, 4) for shift in range(4)]
    z_up, z_far, z_down = (lax.rem(z + shift, 4) for shift in (1, 2, 3))
    to_x_up, to_x_down = x_at[1] * 4 + z, x_at[3] * 4 + z
    to_z_up, to_z_down = x * 4 + z_up, x * 4 + z_down
    half_rows = ROWS // 2
    low_rows, high_rows = pl.ds(0, half_rows), pl.ds(half_rows, half_rows)
    sent = []
    kept = []

    def pass_on(index, ref, to):
        copy = remote(ref, ref, feat_send.at[index], feat_recv.at[index], group, to)
        copy.start()
        sent.append(copy)
        return copy

    def spread(block, shift):
        ref = feat.at[x_at[shift], z]
        return (
            pass_on(4 + 4 * block, ref, to_z_up),
            pass_on(5 + 4 * block, ref, to_z_down),
        )

    def spread_on(block, shift, copies):
        copies[0].wait_recv()
        first = pass_on(6 + 4 * block, feat.at[x_at[shift], z_down, low_rows], to_z_up)
        copies[1].wait_recv()
        second = pass_on(7 + 4 * block, feat.at[x_at[shift], z_up, high_rows], to_z_down)
        return first, second

    pools, stages, gots = (pool_k, pool_v), (stage_k, stage_v), (got_k, got_v)

    def y_copy(kind, shift):
        to_group = group_at(shift)
        return remote(
            pools[kind].at[pl.ds(2 * to_group, 2)],
            stages[kind].at[shift],
            y_send.at[kind, shift],
            y_recv.at[kind, shift],
            to_group,
            tensor,
        )

    def x_copies(kind, shift):
        for step in (1, 3, 2, 0):
            heads = pl.ds(2 * x_at[step], 2)
            if shift == 0:
                source = pools[kind].at[pl.ds(2 * group, 2), heads]
            else:
                source = stages[kind].at[shift, :, heads]
            target = gots[kind].at[step, shift]
            if step == 0:
                copy = pltpu.make_async_copy(source, target, keep_sem.at[kind, shift])
                copy.start()
                kept.append(copy)
            else:
                copy = remote(
                    source,
                    target,
                    x_send.at[kind, shift, step],
                    x_recv.at[kind, shift, step],
                    group,
                    x_at[step] * 4 + z,
                )
                copy.start()
                pages_out.append(copy)

    pages_out = []
    y_out = []
    y_items = [
        (kind, shifts) for shifts in ((2, 6), (3, 7), (4,), (5,)) for kind in range(2)
    ]
    y_running = {}

    def y_start(item):
        if item < len(y_items):
            kind, shifts = y_items[item]
            y_running[item] = [y_copy(kind, shift) for shift in shifts]
            for copy in y_running[item]:
                copy.start()
                y_out.append(copy)

    def y_step(item):
        kind, shifts = y_items[item]
        for copy in y_running[item]:
            copy.wait_recv()
        y_start(item + 2)
        for shift in shifts:
            x_copies(kind, shift)

    f0 = pass_on(0, feat.at[x, z], to_x_up)
    f1 = pass_on(1, feat.at[x, z], to_x_down)
    across = [y_copy(0, 1), y_copy(1, 1)]
    for copy in across:
        copy.start()
        y_out.append(copy)
    y_start(0)
    y_start(1)
    s0 = spread(0, 0)
    x_copies(0, 0)
    x_copies(1, 0)
    f0.wait_recv()
    f2 = pass_on(2, feat.at[x_at[3], z, low_rows], to_x_up)
    s1 = spread(1, 3)
    f1.wait_recv()
    f3 = pass_on(3, feat.at[x_at[1], z, high_rows], to_x_down)
    s2 = spread(2, 1)
    for kind in range(2):
        across[kind].wait_recv()
        x_copies(kind, 1)

    prefix = [prefix_ref[conv_ref[group * CONVS + i]] for i in range(CONVS)]
    suffix = [suffix_ref[conv_ref[group * CONVS + i]] for i in range(CONVS)]

    offsets = row_iota((SUF, HD))
    positions = jnp.concatenate([offsets + prefix[i] for i in range(CONVS)], axis=0)
    angle = positions.astype(F32) * freq_ref[...]
    cosine = jnp.cos(angle)
    sine = jnp.sin(angle)
    sine = jnp.where(lane_iota((ROWS, HD)) < HD // 2, -sine, sine)

    y_step(0)
    r0 = spread_on(0, 0, s0)

    page_ids = lane_iota((1, PAGES))
    below = (row_iota((PAGES, PAGES)) < lane_iota((PAGES, PAGES))).astype(F32)
    lane = lane_iota((PAGES, HD))
    table = jnp.zeros((PAGES, HD), F32)
    counts = jnp.zeros((8, HD), F32)
    for i in range(CONVS):
        entry = table_ref[pl.ds(conv_ref[group * CONVS + i], 1), :]
        source = entry >> 4
        source_y, source_core = source >> 5, (source >> 4) & 1
        source_x, source_z = (source >> 2) & 3, source & 3
        live = jnp.clip(prefix[i] - page_ids * PAGE, 0, PAGE)
        here = (source_z == z) & (live > 0)
        where = ((x - source_x) & 3) * GROUPS
        where = where + ((y - source_y) & 3) * 2 + ((core - source_core) & 1)
        value = ((where * 2 + (entry & 1)) * 128 + live).astype(F32)
        here_f = here.astype(F32)
        order = jnp.dot(
            jnp.broadcast_to(here_f, (8, PAGES)), below, preferred_element_type=F32
        )[0:1, :]
        match = (order == row_iota((PAGES, PAGES)).astype(F32)) & (
            jnp.broadcast_to(here_f, (PAGES, PAGES)) > 0.5
        )
        column = jnp.sum(jnp.where(match, value, 0.0), axis=1, keepdims=True)
        table = jnp.where(lane == i, column, table)
        counts = jnp.where(
            lane_iota((8, HD)) == i, jnp.sum(here_f, axis=1, keepdims=True), counts
        )
    counts = jnp.where(
        lane_iota((8, HD)) == CONVS, lax.div(z, 2).astype(F32), counts
    )
    lists[pl.ds(0, PAGES), :] = table.astype(I32)
    lists[pl.ds(PAGES, 8), :] = counts.astype(I32)

    f2.wait_recv()
    f3.wait_recv()
    s3 = spread(3, 2)
    for load in loads:
        load.wait()
    acc_q[...] = jnp.zeros_like(acc_q)
    acc_kv[...] = jnp.zeros_like(acc_kv)
    squares[...] = jnp.zeros_like(squares)

    def project(bz):
        def one(bx, carry):
            block = bx * 4 + bz
            rows = pl.ds(pl.multiple_of(block * PART, PART), PART)
            wide = feat[bx, bz].astype(F32)
            scaled = (wide * gain_ref[block]).astype(BF16)
            acc_q[...] += jnp.dot(scaled, wq[rows, :], preferred_element_type=F32)
            acc_kv[...] += lax.dot_general(
                scaled,
                wkv[:, rows],
                (((1,), (1,)), ((), ())),
                preferred_element_type=F32,
            )
            wide = wide * wide
            total = squares[...]
            for part in range(PART // HD):
                total = total + wide[:, part * HD : (part + 1) * HD]
            squares[...] = total
            return carry

        lax.fori_loop(0, 4, one, 0)

    project(z)
    y_step(1)
    r1 = spread_on(1, 3, s1)
    r2 = spread_on(2, 1, s2)
    y_step(2)
    r3 = spread_on(3, 2, s3)
    project(z_up)
    y_step(3)
    project(z_down)
    y_step(4)
    for copies in (r0, r1, r2, r3):
        for copy in copies:
            copy.wait_recv()
    project(z_far)
    mean = jnp.sum(squares[...], axis=1, keepdims=True) * (1.0 / WIDTH)
    factor = lax.rsqrt(mean + EPSILON)
    bias = jnp.concatenate([b_key[...], b_value[...]], axis=1).astype(F32)
    kv_own[...] = (acc_kv[...] * factor + bias).astype(BF16)
    kv_copy = remote(
        kv_own,
        kv_other,
        pair_send.at[0],
        pair_recv.at[0],
        group,
        x * 4 + partner_z[1],
    )
    kv_copy.start()

    def rotate(values):
        return values * cosine + pltpu.roll(values, HD // 2, 1) * sine

    for head in range(HEADS):
        columns = slice(head * HD, (head + 1) * HD)
        values = acc_q[:, columns] * factor + b_query[:, columns].astype(F32)
        values = rotate(values).astype(BF16)
        for i in range(CONVS):
            query_own[i, head * SUF : (head + 1) * SUF, :] = values[i * SUF : (i + 1) * SUF, :]
    query_out = [
        remote(
            query_own,
            queries.at[r],
            pair_send.at[r],
            pair_recv.at[r],
            group,
            x * 4 + partner_z[r],
        )
        for r in (1, 2, 3)
    ]
    for copy in query_out:
        copy.start()
    query_keep = pltpu.make_async_copy(query_own, queries.at[0], load_sem.at[4])
    query_keep.start()
    y_step(5)

    kv_copy.wait_recv()
    mine = kv_own[...].astype(F32)
    theirs = kv_other[...].astype(F32)
    even = jnp.where(parity == 0, mine, theirs)
    odd = jnp.where(parity == 0, theirs, mine)
    low = lane_iota((ROWS, HD)) < HD // 2
    keys = jnp.where(low, even, pltpu.roll(odd, HD // 2, 1))
    keys = rotate(keys)
    values = jnp.where(low, pltpu.roll(even, HD // 2, 1), odd)
    key_new[...] = keys.astype(BF16)
    value_new[...] = values.astype(BF16)

    page = jnp.where(parity == 0, keys.astype(BF16).astype(F32), values)
    live_row = jnp.concatenate([offsets < suffix[i] for i in range(CONVS)], axis=0)
    page = jnp.where(live_row, page, 0.0).astype(BF16)
    new_all[pl.ds(group * CONVS, CONVS)] = page.reshape(CONVS, SUF, HD)
    new_ref = new_all.at[pl.ds(group * CONVS, CONVS)]
    group_out = [
        remote(
            new_ref,
            new_ref,
            group_send.at[shift],
            group_recv.at[shift],
            group_at(shift),
            tensor,
        )
        for shift in range(1, GROUPS)
    ]
    for copy in group_out:
        copy.start()
    y_step(6)
    for copy in group_out:
        copy.wait_recv()

    def choose(to, carry):
        target = group * TENSOR + to
        index = jnp.int32(0)
        found = jnp.float32(0)
        for slot in range(GROUPS * CONVS):
            hit = dest_ref[conv_ref[slot]] == target
            index = jnp.where(hit, slot, index)
            found = jnp.where(hit, 1.0, found)
        new_send[to] = (new_all[index].astype(F32) * found).astype(BF16)
        return carry

    lax.fori_loop(0, TENSOR, choose, 0)
    mine_copy = pltpu.make_async_copy(
        new_send.at[tensor], new_pages.at[tensor], load_sem.at[5]
    )
    mine_copy.start()

    def page_copy(off):
        to = lax.rem(tensor + off, TENSOR)
        return remote(
            new_send.at[to],
            new_pages.at[tensor],
            page_send.at[off],
            page_recv.at[off],
            group,
            to,
        )

    def page_start(off, carry):
        page_copy(off).start()
        return carry

    lax.fori_loop(1, TENSOR, page_start, 0)
    y_step(7)

    mine_copy.wait()
    query_keep.wait()
    kv_copy.wait_send()
    for copy in query_out:
        copy.wait()
    for copy in sent + y_out + group_out:
        copy.wait_send()

    def page_end(off, carry):
        page_copy(off).wait()
        return carry

    lax.fori_loop(1, TENSOR, page_end, 0)
    for copy in kept + pages_out:
        copy.wait()


def attend_kernel(lists, got_k, got_v, queries, key_new, value_new, mixed_ref, lse_ref):
    half = HEADS * SUF
    token = row_iota((PAGE, 2 * half))
    causal = row_iota((SUF, half)) <= (lane_iota((SUF, half)) & (SUF - 1))
    step = 4
    own_head = lists[PAGES, CONVS]
    heads = (own_head, 1 - own_head)

    def one(i, carry):
        first = queries[0, i]
        query = [
            jnp.concatenate([first, queries[1, i]], axis=0),
            jnp.concatenate([queries[2, i], queries[3, i]], axis=0),
        ]
        rows = pl.ds(pl.multiple_of(i * SUF, SUF), SUF)
        scores = lax.dot_general(
            key_new[rows, :], first, (((1,), (1,)), ((), ())), preferred_element_type=F32
        )
        scores = jnp.where(causal, scores * SCALE, NEGATIVE)
        peak = jnp.max(scores, axis=0, keepdims=True)
        weights = jnp.exp2(scores - peak)
        total = jnp.sum(weights, axis=0, keepdims=True)
        accum = lax.dot_general(
            value_new[rows, :],
            weights.astype(BF16),
            (((0,), (0,)), ((), ())),
            preferred_element_type=F32,
        )
        peak = jnp.concatenate([peak, jnp.full((1, half), NEGATIVE, F32)], axis=1)
        total = jnp.concatenate([total, jnp.zeros((1, half), F32)], axis=1)
        accum = jnp.concatenate([accum, jnp.zeros((HD, half), F32)], axis=1)
        empty = (
            jnp.full((1, 2 * half), NEGATIVE, F32),
            jnp.zeros((1, 2 * half), F32),
            jnp.zeros((HD, 2 * half), F32),
        )
        count = lists[PAGES, i]

        def block(b, state):
            codes = [lists[b * step + p, i] for p in range(step)]
            scores = []
            for slot in range(2):
                keys = jnp.concatenate([got_k[code >> 7, heads[slot]] for code in codes], axis=0)
                scores.append(
                    lax.dot_general(
                        keys,
                        query[slot],
                        (((1,), (1,)), ((), ())),
                        preferred_element_type=F32,
                    )
                )
            out = []
            for slot in range(2):
                peak, total, accum = state[slot]
                values = jnp.concatenate(
                    [got_v[code >> 7, heads[slot]] for code in codes], axis=0
                )
                score = jnp.concatenate(
                    [
                        jnp.where(
                            token < (codes[p] & 127),
                            scores[slot][p * PAGE : (p + 1) * PAGE] * SCALE,
                            NEGATIVE,
                        )
                        for p in range(step)
                    ],
                    axis=0,
                )
                fresh = jnp.maximum(peak, jnp.max(score, axis=0, keepdims=True))
                shrink = jnp.exp2(peak - fresh)
                weights = jnp.exp2(score - fresh)
                total = total * shrink + jnp.sum(weights, axis=0, keepdims=True)
                accum = accum * shrink + lax.dot_general(
                    values,
                    weights.astype(BF16),
                    (((0,), (0,)), ((), ())),
                    preferred_element_type=F32,
                )
                out.append((fresh, total, accum))
            return tuple(out)

        state = lax.fori_loop(
            0, (count + step - 1) >> 2, block, ((peak, total, accum), empty)
        )
        for slot in range(2):
            peak, total, accum = state[slot]
            some = total > 0.0
            safe = jnp.where(some, total, 1.0)
            mixed = (accum / safe).astype(BF16)
            lse = jnp.where(some, peak + jnp.log(safe) * (1.0 / LN2), NEGATIVE)
            lse = jnp.broadcast_to(lse, (8, 2 * half))
            for side in range(2):
                columns = slice(side * half, (side + 1) * half)
                mixed_ref[2 * slot + side, i] = mixed[:, columns]
                lse_ref[2 * slot + side, i] = lse[:, columns]
        return carry

    lax.fori_loop(0, CONVS, one, 0)


X_FIRST = (True, True, False, True)


def reduce_kernel(
    conv_ref,
    suffix_ref,
    mixed_ref,
    lse_ref,
    w_out,
    out_ref,
    weights,
    mixed_got,
    lse_got,
    mixed,
    part,
    big,
    small,
    load_sem,
    mixed_send,
    mixed_recv,
    lse_send,
    lse_recv,
    ring_send,
    ring_recv,
):
    group, tensor, y, core, x, z = place()
    partner_z = [z, z + 1 - 2 * lax.rem(z, 2), lax.rem(z + 2, 4), 3 - z]
    load = pltpu.make_async_copy(w_out, weights, load_sem.at[0])
    load.start()
    x_up, x_far, x_down = (lax.rem(x + shift, 4) for shift in (1, 2, 3))
    z_up, z_far, z_down = (lax.rem(z + shift, 4) for shift in (1, 2, 3))
    to_x_up, to_x_down = x_up * 4 + z, x_down * 4 + z
    to_z_up, to_z_down = x * 4 + z_up, x * 4 + z_down
    barrier = pltpu.get_barrier_semaphore()
    for to in (to_x_up, to_x_down, to_z_up, to_z_down, x * 4 + z_far):
        pl.semaphore_signal(barrier, inc=1, device_id=(group, to), device_id_type=MESH)
    pl.semaphore_wait(barrier, 5)

    lse_out = [
        remote(
            lse_ref.at[r],
            lse_got.at[r],
            lse_send.at[r],
            lse_recv.at[r],
            group,
            x * 4 + partner_z[r],
        )
        for r in (1, 2, 3)
    ]
    mixed_out = [
        [
            remote(
                mixed_ref.at[r, i],
                mixed_got.at[r, i],
                mixed_send.at[r, i],
                mixed_recv.at[r, i],
                group,
                x * 4 + partner_z[r],
            )
            for r in (1, 2, 3)
        ]
        for i in range(CONVS)
    ]
    for copy in lse_out + mixed_out[0] + mixed_out[1]:
        copy.start()
    row_of = lane_iota((1, HEADS * SUF)) & (SUF - 1)
    pending = []

    def combine(i):
        if i == 0:
            for copy in lse_out:
                copy.wait_recv()
        for copy in mixed_out[i]:
            copy.wait_recv()
        if i + 2 < CONVS:
            for copy in mixed_out[i + 2]:
                copy.start()
        logs = [lse_ref[0, i, 0:1, :]] + [lse_got[r, i, 0:1, :] for r in (1, 2, 3)]
        peak = jnp.maximum(jnp.maximum(logs[0], logs[1]), jnp.maximum(logs[2], logs[3]))
        shares = [jnp.exp2(log - peak) for log in logs]
        scale = jnp.where(row_of < suffix_ref[conv_ref[group * CONVS + i]], 1.0, 0.0)
        scale = scale / (shares[0] + shares[1] + shares[2] + shares[3])
        joined = mixed_ref[0, i].astype(F32) * (shares[0] * scale)
        for r in (1, 2, 3):
            joined = joined + mixed_got[r, i].astype(F32) * (shares[r] * scale)
        turned = jnp.transpose(joined).astype(BF16)
        for head in range(HEADS):
            mixed[i, :, head * HD : (head + 1) * HD] = turned[
                head * SUF : (head + 1) * SUF, :
            ]

    class Ring:
        def __init__(self, conv, first, pick, buffers, way):
            self.conv, self.first, self.pick, self.buffers = conv, first, pick, buffers
            self.up, self.down, self.me, self.far, self.to_up, self.to_down = way
            self.top = pl.ds(conv * SUF, SUF // 2)
            self.bottom = pl.ds(conv * SUF + SUF // 2, SUF // 2)

        def send(self, index, ref, to):
            sem = self.first + index
            copy = remote(
                ref,
                self.buffers.at[self.conv, index],
                ring_send.at[sem],
                ring_recv.at[sem],
                group,
                to,
            )
            copy.start()
            pending.append(copy)
            return copy

        def start(self, ready):
            pick = self.pick
            ready(self.far)
            self.c0 = self.send(0, pick(self.far, self.top), self.to_up)
            self.c1 = self.send(1, pick(self.far, self.bottom), self.to_down)
            ready(self.up)
            self.c2 = self.send(2, pick(self.up, self.bottom), self.to_up)
            ready(self.down)
            self.c3 = self.send(3, pick(self.down, self.top), self.to_down)
            ready(self.me)

        def add(self, ref, *indices):
            total = ref[...].astype(F32)
            for index in indices:
                total = total + self.buffers[self.conv, index].astype(F32)
            ref[...] = total.astype(BF16)

        def relay(self):
            pick = self.pick
            self.c0.wait_recv()
            self.add(pick(self.up, self.top), 0)
            self.c4 = self.send(4, pick(self.up, self.top), self.to_up)
            self.c1.wait_recv()
            self.add(pick(self.down, self.bottom), 1)
            self.c5 = self.send(5, pick(self.down, self.bottom), self.to_down)

        def finish(self):
            pick = self.pick
            self.c3.wait_recv()
            self.c4.wait_recv()
            self.add(pick(self.me, self.top), 3, 4)
            self.c2.wait_recv()
            self.c5.wait_recv()
            self.add(pick(self.me, self.bottom), 2, 5)

    along_x = (x_up, x_down, x, x_far, to_x_up, to_x_down)
    along_z = (z_up, z_down, z, z_far, to_z_up, to_z_down)
    firsts, seconds = [], []
    for i in range(CONVS):
        if X_FIRST[i]:
            firsts.append(Ring(i, 12 * i, lambda j, rows: part.at[j, :, rows], big, along_x))
            seconds.append(
                Ring(i, 12 * i + 6, lambda j, rows: part.at[x, j, rows], small, along_z)
            )
        else:
            firsts.append(Ring(i, 12 * i, lambda j, rows: part.at[:, j, rows], big, along_z))
            seconds.append(
                Ring(i, 12 * i + 6, lambda j, rows: part.at[j, z, rows], small, along_x)
            )

    def begin(i):
        combine(i)
        if i == 0:
            load.wait()
        rows = slice(i * SUF, (i + 1) * SUF)

        def ready(j):
            def one(k, carry):
                bx, bz = (j, k) if X_FIRST[i] else (k, j)
                columns = pl.ds(pl.multiple_of((bx * 4 + bz) * PART, PART), PART)
                part[bx, bz, rows] = jnp.dot(
                    mixed[i], weights[:, columns], preferred_element_type=F32
                ).astype(BF16)
                return carry

            lax.fori_loop(0, 4, one, 0)

        firsts[i].start(ready)

    def turn(i):
        firsts[i].finish()
        seconds[i].start(lambda j: None)

    begin(0)
    begin(1)
    firsts[0].relay()
    begin(2)
    firsts[1].relay()
    turn(0)
    begin(3)
    firsts[2].relay()
    turn(1)
    seconds[0].relay()
    firsts[3].relay()
    turn(2)
    seconds[1].relay()
    seconds[0].finish()
    turn(3)
    seconds[2].relay()
    seconds[1].finish()
    seconds[3].relay()
    seconds[2].finish()
    seconds[3].finish()
    out_ref[...] = part[x, z]
    for copy in lse_out + mixed_out[0] + mixed_out[1] + mixed_out[2] + mixed_out[3] + pending:
        copy.wait_send()


def any_spec():
    return pl.BlockSpec(memory_space=pl.ANY)


def vmem_spec():
    return pl.BlockSpec(memory_space=pltpu.VMEM)


def smem_spec():
    return pl.BlockSpec(memory_space=pltpu.SMEM)


def shards(
    hidden_states,
    norm_gain,
    w_query,
    b_query,
    w_key,
    b_key,
    w_value,
    b_value,
    w_out,
    pool_keys,
    pool_values,
    conv_slots,
    page_table,
    prefix_len,
    suffix_len,
    new_dest,
):
    dma = pltpu.SemaphoreType.DMA
    freq = THETA ** (-(np.arange(HD // 2, dtype=np.float64) * 2.0 / HD))
    freq = jnp.asarray(np.concatenate([freq, freq])[None, :], F32)
    shape = jax.ShapeDtypeStruct
    got_k, got_v, queries, key_new, value_new, lists, new_pages = pl.pallas_call(
        gather_kernel,
        out_shape=[
            shape((4, GROUPS, 2, 2, PAGE, HD), BF16),
            shape((4, GROUPS, 2, 2, PAGE, HD), BF16),
            shape((4, CONVS, HEADS * SUF, HD), BF16),
            shape((ROWS, HD), BF16),
            shape((ROWS, HD), BF16),
            shape((PAGES + 8, HD), I32),
            shape((TENSOR, SUF, HD), BF16),
        ],
        in_specs=[smem_spec()] * 4
        + [vmem_spec()]
        + [any_spec()] * 6
        + [vmem_spec()] * 5,
        out_specs=[any_spec()] * 3 + [vmem_spec()] * 3 + [any_spec()],
        scratch_shapes=[
            pltpu.VMEM((4, 4, ROWS, PART), BF16),
            pltpu.VMEM((WIDTH, HEADS * HD), BF16),
            pltpu.VMEM((HD, WIDTH), BF16),
            pltpu.VMEM((ROWS, HEADS * HD), F32),
            pltpu.VMEM((ROWS, HD), F32),
            pltpu.VMEM((ROWS, HD), F32),
            pltpu.VMEM((GROUPS, 2, 8, PAGE, HD), BF16),
            pltpu.VMEM((GROUPS, 2, 8, PAGE, HD), BF16),
            pltpu.VMEM((CONVS, HEADS * SUF, HD), BF16),
            pltpu.VMEM((ROWS, HD), BF16),
            pltpu.VMEM((ROWS, HD), BF16),
            pltpu.VMEM((GROUPS * CONVS, SUF, HD), BF16),
            pltpu.VMEM((TENSOR, SUF, HD), BF16),
            dma((8,)),
            dma((2, GROUPS)),
            dma((20,)),
            dma((20,)),
            dma((2, GROUPS)),
            dma((2, GROUPS)),
            dma((2, GROUPS, 4)),
            dma((2, GROUPS, 4)),
            dma((4,)),
            dma((4,)),
            dma((GROUPS,)),
            dma((GROUPS,)),
            dma((TENSOR,)),
            dma((TENSOR,)),
        ],
        compiler_params=pltpu.CompilerParams(
            collective_id=0, has_side_effects=True, vmem_limit_bytes=60 * 1024 * 1024
        ),
        name="gather",
    )(
        conv_slots,
        prefix_len,
        suffix_len,
        new_dest,
        page_table,
        hidden_states,
        pool_keys,
        pool_values,
        w_query,
        w_key.T,
        w_value.T,
        norm_gain.astype(F32).reshape(TENSOR, 1, PART),
        b_query.reshape(1, HEADS * HD),
        b_key.reshape(1, HD // 2),
        b_value.reshape(1, HD // 2),
        freq,
    )
    mixed, lse = pl.pallas_call(
        attend_kernel,
        out_shape=[
            shape((4, CONVS, HD, HEADS * SUF), BF16),
            shape((4, CONVS, 8, HEADS * SUF), F32),
        ],
        in_specs=[smem_spec()] + [vmem_spec()] * 5,
        out_specs=[vmem_spec()] * 2,
        compiler_params=pltpu.CompilerParams(vmem_limit_bytes=60 * 1024 * 1024),
        name="attend",
    )(
        lists,
        got_k.reshape(PAGES, 2, PAGE, HD),
        got_v.reshape(PAGES, 2, PAGE, HD),
        queries,
        key_new,
        value_new,
    )
    attn_out = pl.pallas_call(
        reduce_kernel,
        out_shape=shape((ROWS, PART), BF16),
        in_specs=[smem_spec()] * 2 + [vmem_spec()] * 2 + [any_spec()],
        out_specs=vmem_spec(),
        scratch_shapes=[
            pltpu.VMEM((HEADS * HD, WIDTH), BF16),
            pltpu.VMEM((4, CONVS, HD, HEADS * SUF), BF16),
            pltpu.VMEM((4, CONVS, 8, HEADS * SUF), F32),
            pltpu.VMEM((CONVS, SUF, HEADS * HD), BF16),
            pltpu.VMEM((4, 4, ROWS, PART), BF16),
            pltpu.VMEM((CONVS, 6, 4, SUF // 2, PART), BF16),
            pltpu.VMEM((CONVS, 6, SUF // 2, PART), BF16),
            dma((1,)),
            dma((4, CONVS)),
            dma((4, CONVS)),
            dma((4,)),
            dma((4,)),
            dma((12 * CONVS,)),
            dma((12 * CONVS,)),
        ],
        compiler_params=pltpu.CompilerParams(
            collective_id=1, has_side_effects=True, vmem_limit_bytes=60 * 1024 * 1024
        ),
        name="reduce",
    )(conv_slots, suffix_len, mixed, lse, w_out)
    pages = new_pages.reshape(TENSOR // 2, 2, SUF, HD)
    return (attn_out, pages[None, :, 0], pages[None, :, 1])


def solution(mesh):
    in_specs = (
        P("group", "tensor"),
        P(),
        P(None, "tensor"),
        P("tensor"),
        P(None, "tensor"),
        P("tensor"),
        P(None, "tensor"),
        P("tensor"),
        P("tensor", None),
        P(("group", "tensor"), None, None, None),
        P(("group", "tensor"), None, None, None),
        P(),
        P(),
        P(),
        P(),
        P(),
    )
    out_specs = (
        P("group", "tensor"),
        P(("group", "tensor"), None, None, None),
        P(("group", "tensor"), None, None, None),
    )
    return jax.shard_map(shards, mesh=mesh, in_specs=in_specs, out_specs=out_specs, check_vma=False)
```

```python
import jax
import jax.numpy as jnp
import numpy as np
from jax import lax
from jax.experimental import pallas as pl
from jax.experimental.pallas import tpu as pltpu
from jax.sharding import PartitionSpec as P

HD = 128
SUF = 64
CONVS = 4
ROWS = CONVS * SUF
GROUPS = 8
TENSOR = 16
WIDTH = 8192
PART = WIDTH // TENSOR
PAGES = 64
PAGE = 64
HEADS = 4
THETA = 1000000.0
EPSILON = 1e-06
NEGATIVE = -1e30
SCALE = HD**-0.5 * 1.4426950408889634
LN2 = 0.6931471805599453
MESH = pl.DeviceIdType.MESH
BF16 = jnp.bfloat16
F32 = jnp.float32
I32 = jnp.int32


def remote(src, dst, send_sem, recv_sem, group, tensor):
    return pltpu.make_async_remote_copy(
        src_ref=src,
        dst_ref=dst,
        send_sem=send_sem,
        recv_sem=recv_sem,
        device_id=(group, tensor),
        device_id_type=MESH,
    )


def place():
    group = lax.axis_index("group")
    tensor = lax.axis_index("tensor")
    return (
        group,
        tensor,
        lax.div(group, 2),
        lax.rem(group, 2),
        lax.div(tensor, 4),
        lax.rem(tensor, 4),
    )


def lane_iota(shape):
    return lax.broadcasted_iota(I32, shape, len(shape) - 1)


def row_iota(shape):
    return lax.broadcasted_iota(I32, shape, len(shape) - 2)


def gather_kernel(
    conv_ref,
    prefix_ref,
    suffix_ref,
    dest_ref,
    table_ref,
    hidden,
    pool_k,
    pool_v,
    w_query,
    w_key,
    w_value,
    gain_ref,
    b_query,
    b_key,
    b_value,
    freq_ref,
    got_k,
    got_v,
    queries,
    key_new,
    value_new,
    lists,
    new_pages,
    feat,
    wq,
    wkv,
    acc_q,
    acc_kv,
    squares,
    stage_k,
    stage_v,
    query_own,
    kv_own,
    kv_other,
    new_all,
    new_send,
    chosen,
    gain,
    load_sem,
    keep_sem,
    feat_send,
    feat_recv,
    y_send,
    y_recv,
    x_send,
    x_recv,
    v_send,
    v_recv,
    pair_send,
    pair_recv,
    group_send,
    group_recv,
    page_send,
    page_recv,
):
    group, tensor, y, core, x, z = place()
    parity = lax.rem(z, 2)
    partner_z = [z, z + 1 - 2 * parity, lax.rem(z + 2, 4), 3 - z]
    own = pltpu.make_async_copy(hidden, feat.at[x, z], load_sem.at[0])
    own.start()
    loads = [
        pltpu.make_async_copy(w_query, wq, load_sem.at[1]),
        pltpu.make_async_copy(w_key, wkv.at[pl.ds(0, HD // 2)], load_sem.at[2]),
        pltpu.make_async_copy(w_value, wkv.at[pl.ds(HD // 2, HD // 2)], load_sem.at[3]),
    ]
    for load in loads:
        load.start()

    def group_at(shift):
        to_y = lax.rem(y + shift // 2, 4)
        to_core = lax.rem(core + shift % 2, 2)
        return to_y * 2 + to_core

    barrier = pltpu.get_barrier_semaphore()
    for shift in range(1, GROUPS):
        pl.semaphore_signal(
            barrier, inc=1, device_id=(group_at(shift), tensor), device_id_type=MESH
        )

    def greet(off, carry):
        to = lax.rem(tensor + off, TENSOR)
        pl.semaphore_signal(barrier, inc=1, device_id=(group, to), device_id_type=MESH)
        return carry

    lax.fori_loop(1, TENSOR, greet, 0)
    pl.semaphore_wait(barrier, GROUPS - 1 + TENSOR - 1)

    own.wait()
    x_at = [lax.rem(x + shift, 4) for shift in range(4)]
    z_up, z_far, z_down = (lax.rem(z + shift, 4) for shift in (1, 2, 3))
    to_x_up, to_x_down = x_at[1] * 4 + z, x_at[3] * 4 + z
    to_z_up, to_z_down = x * 4 + z_up, x * 4 + z_down
    half_rows = ROWS // 2
    low_rows, high_rows = pl.ds(0, half_rows), pl.ds(half_rows, half_rows)
    sent, kept = [], []

    def pass_on(index, ref, to):
        copy = remote(ref, ref, feat_send.at[index], feat_recv.at[index], group, to)
        copy.start()
        sent.append(copy)
        return copy

    def spread(block, shift):
        ref = feat.at[x_at[shift], z]
        return (
            pass_on(4 + 4 * block, ref, to_z_up),
            pass_on(5 + 4 * block, ref, to_z_down),
        )

    def spread_on(block, shift, copies):
        copies[0].wait_recv()
        first = pass_on(6 + 4 * block, feat.at[x_at[shift], z_down, low_rows], to_z_up)
        copies[1].wait_recv()
        second = pass_on(7 + 4 * block, feat.at[x_at[shift], z_up, high_rows], to_z_down)
        return first, second

    pages_out = []

    def push(source, target, send_sem, recv_sem, to_group, to):
        copy = remote(source, target, send_sem, recv_sem, to_group, to)
        copy.start()
        pages_out.append(copy)
        return copy

    def keep(source, target, sem):
        copy = pltpu.make_async_copy(source, target, sem)
        copy.start()
        kept.append(copy)

    def slots(shift):
        return pl.ds(2 * group_at(shift), 2)

    def heads(step):
        return pl.ds(2 * x_at[step], 2)

    def keys_first(shift):
        return push(
            pool_k.at[slots(shift)],
            stage_k.at[shift],
            y_send.at[0, shift],
            y_recv.at[0, shift],
            group_at(shift),
            tensor,
        )

    def keys_second(shift):
        for step in (1, 3, 2, 0):
            if shift == 0:
                source = pool_k.at[slots(0), heads(step)]
            else:
                source = stage_k.at[shift, :, heads(step)]
            target = got_k.at[step, shift]
            if step == 0:
                keep(source, target, keep_sem.at[0, shift])
            else:
                keys_last.append(
                    push(
                        source,
                        target,
                        x_send.at[0, shift, step],
                        x_recv.at[0, shift, step],
                        group,
                        x_at[step] * 4 + z,
                    )
                )

    def values_first(step):
        return push(
            pool_v.at[:, heads(step)],
            stage_v.at[step],
            v_send.at[step],
            v_recv.at[step],
            group,
            x_at[step] * 4 + z,
        )

    def values_second(step):
        for shift in (1, 2, 6, 3, 7, 4, 5, 0):
            if step == 0:
                source = pool_v.at[slots(shift), heads(0)]
            else:
                source = stage_v.at[step, slots(shift)]
            target = got_v.at[step, shift]
            if shift == 0:
                keep(source, target, keep_sem.at[1, step])
            else:
                keys_last.append(
                    push(
                        source,
                        target,
                        x_send.at[1, shift, step],
                        x_recv.at[1, shift, step],
                        group_at(shift),
                        tensor,
                    )
                )

    keys_last = []
    f0 = pass_on(0, feat.at[x, z], to_x_up)
    f1 = pass_on(1, feat.at[x, z], to_x_down)
    s0 = spread(0, 0)
    key_first = {shift: keys_first(shift) for shift in (1, 2, 6, 3, 7, 4, 5)}
    value_first = {step: values_first(step) for step in (1, 3, 2)}
    keys_second(0)
    values_second(0)
    f0.wait_recv()
    f2 = pass_on(2, feat.at[x_at[3], z, low_rows], to_x_up)
    s1 = spread(1, 3)
    f1.wait_recv()
    f3 = pass_on(3, feat.at[x_at[1], z, high_rows], to_x_down)
    s2 = spread(2, 1)
    key_first[1].wait_recv()
    keys_second(1)

    prefix = [prefix_ref[conv_ref[group * CONVS + i]] for i in range(CONVS)]
    suffix = [suffix_ref[conv_ref[group * CONVS + i]] for i in range(CONVS)]

    offsets = row_iota((SUF, HD))
    positions = jnp.concatenate([offsets + prefix[i] for i in range(CONVS)], axis=0)
    angle = positions.astype(F32) * freq_ref[...]
    cosine = jnp.cos(angle)
    sine = jnp.sin(angle)
    sine = jnp.where(lane_iota((ROWS, HD)) < HD // 2, -sine, sine)

    r0 = spread_on(0, 0, s0)

    page_ids = lane_iota((1, PAGES))
    below = (row_iota((PAGES, PAGES)) < lane_iota((PAGES, PAGES))).astype(F32)
    lane = lane_iota((PAGES, HD))
    table = jnp.zeros((PAGES, HD), F32)
    counts = jnp.zeros((8, HD), F32)
    for i in range(CONVS):
        entry = table_ref[pl.ds(conv_ref[group * CONVS + i], 1), :]
        source = entry >> 4
        source_y, source_core = source >> 5, (source >> 4) & 1
        source_x, source_z = (source >> 2) & 3, source & 3
        live = jnp.clip(prefix[i] - page_ids * PAGE, 0, PAGE)
        here = (source_z == z) & (live > 0)
        where = ((x - source_x) & 3) * GROUPS
        where = where + ((y - source_y) & 3) * 2 + ((core - source_core) & 1)
        value = ((where * 2 + (entry & 1)) * 128 + live).astype(F32)
        here_f = here.astype(F32)
        order = jnp.dot(
            jnp.broadcast_to(here_f, (8, PAGES)), below, preferred_element_type=F32
        )[0:1, :]
        match = (order == row_iota((PAGES, PAGES)).astype(F32)) & (
            jnp.broadcast_to(here_f, (PAGES, PAGES)) > 0.5
        )
        column = jnp.sum(jnp.where(match, value, 0.0), axis=1, keepdims=True)
        table = jnp.where(lane == i, column, table)
        counts = jnp.where(
            lane_iota((8, HD)) == i, jnp.sum(here_f, axis=1, keepdims=True), counts
        )
    counts = jnp.where(
        lane_iota((8, HD)) == CONVS, lax.div(z, 2).astype(F32), counts
    )
    lists[pl.ds(0, PAGES), :] = table.astype(I32)
    lists[pl.ds(PAGES, 8), :] = counts.astype(I32)

    def find(to, carry):
        target = group * TENSOR + to
        index = jnp.int32(0)
        found = jnp.int32(0)
        for slot in range(GROUPS * CONVS):
            hit = dest_ref[conv_ref[slot]] == target
            index = jnp.where(hit, slot, index)
            found = jnp.where(hit, 1, found)
        chosen[0, to] = index
        chosen[1, to] = found
        return carry

    f2.wait_recv()
    f3.wait_recv()
    s3 = spread(3, 2)
    for load in loads:
        load.wait()
    gain[...] = gain_ref[...].astype(F32).reshape(1, WIDTH)
    query_bias = b_query[...].astype(F32).reshape(1, HEADS * HD)
    acc_q[...] = jnp.zeros_like(acc_q)
    acc_kv[...] = jnp.zeros_like(acc_kv)
    squares[...] = jnp.zeros_like(squares)

    def project(bz):
        def one(bx, carry):
            block = bx * 4 + bz
            rows = pl.ds(pl.multiple_of(block * PART, PART), PART)
            wide = feat[bx, bz].astype(F32)
            scaled = (wide * gain[:, rows]).astype(BF16)
            acc_q[...] += jnp.dot(scaled, wq[rows, :], preferred_element_type=F32)
            acc_kv[...] += lax.dot_general(
                scaled,
                wkv[:, rows],
                (((1,), (1,)), ((), ())),
                preferred_element_type=F32,
            )
            wide = wide * wide
            total = squares[...]
            for part in range(PART // HD):
                total = total + wide[:, part * HD : (part + 1) * HD]
            squares[...] = total
            return carry

        lax.fori_loop(0, 4, one, 0)

    project(z)
    lax.fori_loop(0, TENSOR, find, 0)
    r1 = spread_on(1, 3, s1)
    r2 = spread_on(2, 1, s2)
    r3 = spread_on(3, 2, s3)
    for shift in (2, 6, 3, 7, 4, 5):
        key_first[shift].wait_recv()
        keys_second(shift)
    for step in (1, 3, 2):
        value_first[step].wait_recv()
        values_second(step)
    project(z_up)
    project(z_down)
    for copies in (r0, r1, r2, r3):
        for copy in copies:
            copy.wait_recv()
    project(z_far)
    mean = jnp.sum(squares[...], axis=1, keepdims=True) * (1.0 / WIDTH)
    factor = lax.rsqrt(mean + EPSILON)
    bias = jnp.concatenate(
        [ref[...].astype(F32).reshape(1, HD // 2) for ref in (b_key, b_value)], axis=1
    )
    kv_own[...] = (acc_kv[...] * factor + bias).astype(BF16)
    kv_copy = remote(
        kv_own,
        kv_other,
        pair_send.at[0],
        pair_recv.at[0],
        group,
        x * 4 + partner_z[1],
    )
    kv_copy.start()

    def rotate(values):
        return values * cosine + pltpu.roll(values, HD // 2, 1) * sine

    for head in range(HEADS):
        columns = slice(head * HD, (head + 1) * HD)
        values = acc_q[:, columns] * factor + query_bias[:, columns]
        values = rotate(values).astype(BF16)
        for i in range(CONVS):
            query_own[i, head * SUF : (head + 1) * SUF, :] = values[i * SUF : (i + 1) * SUF, :]
    query_out = [
        remote(
            query_own,
            queries.at[r],
            pair_send.at[r],
            pair_recv.at[r],
            group,
            x * 4 + partner_z[r],
        )
        for r in (1, 2, 3)
    ]
    for copy in query_out:
        copy.start()
    query_keep = pltpu.make_async_copy(query_own, queries.at[0], load_sem.at[4])
    query_keep.start()

    kv_copy.wait_recv()
    mine = kv_own[...].astype(F32)
    theirs = kv_other[...].astype(F32)
    even = jnp.where(parity == 0, mine, theirs)
    odd = jnp.where(parity == 0, theirs, mine)
    low = lane_iota((ROWS, HD)) < HD // 2
    keys = jnp.where(low, even, pltpu.roll(odd, HD // 2, 1))
    keys = rotate(keys)
    values = jnp.where(low, pltpu.roll(even, HD // 2, 1), odd)
    key_new[...] = keys.astype(BF16)
    value_new[...] = values.astype(BF16)

    page = jnp.where(parity == 0, keys.astype(BF16).astype(F32), values)
    live_row = jnp.concatenate([offsets < suffix[i] for i in range(CONVS)], axis=0)
    page = jnp.where(live_row, page, 0.0).astype(BF16)
    new_all[pl.ds(group * CONVS, CONVS)] = page.reshape(CONVS, SUF, HD)
    new_ref = new_all.at[pl.ds(group * CONVS, CONVS)]
    group_out = [
        remote(
            new_ref,
            new_ref,
            group_send.at[shift],
            group_recv.at[shift],
            group_at(shift),
            tensor,
        )
        for shift in range(1, GROUPS)
    ]
    for copy in group_out:
        copy.start()
    for copy in group_out:
        copy.wait_recv()

    def choose(to, carry):
        page = new_all[chosen[0, to]].astype(F32)
        new_send[to] = (page * chosen[1, to].astype(F32)).astype(BF16)
        return carry

    lax.fori_loop(0, TENSOR, choose, 0)
    mine_copy = pltpu.make_async_copy(
        new_send.at[tensor], new_pages.at[tensor], load_sem.at[5]
    )
    mine_copy.start()

    def page_copy(off):
        to = lax.rem(tensor + off, TENSOR)
        return remote(
            new_send.at[to],
            new_pages.at[tensor],
            page_send.at[off],
            page_recv.at[off],
            group,
            to,
        )

    def page_start(off, carry):
        page_copy(off).start()
        return carry

    lax.fori_loop(1, TENSOR, page_start, 0)

    mine_copy.wait()
    query_keep.wait()
    kv_copy.wait_send()
    for copy in query_out:
        copy.wait()
    for copy in sent + pages_out + group_out:
        copy.wait_send()

    def page_end(off, carry):
        page_copy(off).wait()
        return carry

    lax.fori_loop(1, TENSOR, page_end, 0)
    for copy in kept:
        copy.wait()
    for copy in keys_last:
        copy.wait_recv()


def attend_kernel(lists, got_k, got_v, queries, key_new, value_new, mixed_ref, lse_ref):
    half = HEADS * SUF
    token = row_iota((PAGE, 2 * half))
    causal = row_iota((SUF, half)) <= (lane_iota((SUF, half)) & (SUF - 1))
    step = 4
    own_head = lists[PAGES, CONVS]
    heads = (own_head, 1 - own_head)

    def one(i, carry):
        first = queries[0, i]
        query = [
            jnp.concatenate([first, queries[1, i]], axis=0),
            jnp.concatenate([queries[2, i], queries[3, i]], axis=0),
        ]
        rows = pl.ds(pl.multiple_of(i * SUF, SUF), SUF)
        scores = lax.dot_general(
            key_new[rows, :], first, (((1,), (1,)), ((), ())), preferred_element_type=F32
        )
        scores = jnp.where(causal, scores * SCALE, NEGATIVE)
        peak = jnp.max(scores, axis=0, keepdims=True)
        weights = jnp.exp2(scores - peak)
        total = jnp.sum(weights, axis=0, keepdims=True)
        accum = lax.dot_general(
            value_new[rows, :],
            weights.astype(BF16),
            (((0,), (0,)), ((), ())),
            preferred_element_type=F32,
        )
        peak = jnp.concatenate([peak, jnp.full((1, half), NEGATIVE, F32)], axis=1)
        total = jnp.concatenate([total, jnp.zeros((1, half), F32)], axis=1)
        accum = jnp.concatenate([accum, jnp.zeros((HD, half), F32)], axis=1)
        empty = (
            jnp.full((1, 2 * half), NEGATIVE, F32),
            jnp.zeros((1, 2 * half), F32),
            jnp.zeros((HD, 2 * half), F32),
        )
        count = lists[PAGES, i]

        def block(b, state):
            codes = [lists[b * step + p, i] for p in range(step)]
            scores = []
            for slot in range(2):
                keys = jnp.concatenate([got_k[code >> 7, heads[slot]] for code in codes], axis=0)
                scores.append(
                    lax.dot_general(
                        keys,
                        query[slot],
                        (((1,), (1,)), ((), ())),
                        preferred_element_type=F32,
                    )
                )
            out = []
            for slot in range(2):
                peak, total, accum = state[slot]
                values = jnp.concatenate(
                    [got_v[code >> 7, heads[slot]] for code in codes], axis=0
                )
                score = jnp.concatenate(
                    [
                        jnp.where(
                            token < (codes[p] & 127),
                            scores[slot][p * PAGE : (p + 1) * PAGE] * SCALE,
                            NEGATIVE,
                        )
                        for p in range(step)
                    ],
                    axis=0,
                )
                fresh = jnp.maximum(peak, jnp.max(score, axis=0, keepdims=True))
                shrink = jnp.exp2(peak - fresh)
                weights = jnp.exp2(score - fresh)
                total = total * shrink + jnp.sum(weights, axis=0, keepdims=True)
                accum = accum * shrink + lax.dot_general(
                    values,
                    weights.astype(BF16),
                    (((0,), (0,)), ((), ())),
                    preferred_element_type=F32,
                )
                out.append((fresh, total, accum))
            return tuple(out)

        state = lax.fori_loop(
            0, (count + step - 1) >> 2, block, ((peak, total, accum), empty)
        )
        for slot in range(2):
            peak, total, accum = state[slot]
            some = total > 0.0
            safe = jnp.where(some, total, 1.0)
            mixed = (accum * (1.0 / safe)).astype(BF16)
            lse = jnp.where(some, peak + jnp.log(safe) * (1.0 / LN2), NEGATIVE)
            lse = jnp.broadcast_to(lse, (8, 2 * half))
            for side in range(2):
                columns = slice(side * half, (side + 1) * half)
                mixed_ref[2 * slot + side, i] = mixed[:, columns]
                lse_ref[2 * slot + side, i] = lse[:, columns]
        return carry

    lax.fori_loop(0, CONVS, one, 0)


def reduce_kernel(
    conv_ref,
    suffix_ref,
    mixed_ref,
    lse_ref,
    w_out,
    out_ref,
    weights,
    mixed_got,
    lse_got,
    mixed,
    part,
    big,
    small,
    load_sem,
    mixed_send,
    mixed_recv,
    lse_send,
    lse_recv,
    ring_send,
    ring_recv,
):
    group, tensor, y, core, x, z = place()
    partner_z = [z, z + 1 - 2 * lax.rem(z, 2), lax.rem(z + 2, 4), 3 - z]
    load = pltpu.make_async_copy(w_out, weights, load_sem.at[0])
    load.start()
    x_up, x_far, x_down = (lax.rem(x + shift, 4) for shift in (1, 2, 3))
    z_up, z_far, z_down = (lax.rem(z + shift, 4) for shift in (1, 2, 3))
    to_x_up, to_x_down = x_up * 4 + z, x_down * 4 + z
    to_z_up, to_z_down = x * 4 + z_up, x * 4 + z_down
    barrier = pltpu.get_barrier_semaphore()
    for to in (to_x_up, to_x_down, to_z_up, to_z_down, x * 4 + z_far):
        pl.semaphore_signal(barrier, inc=1, device_id=(group, to), device_id_type=MESH)
    pl.semaphore_wait(barrier, 5)

    lse_out = [
        remote(
            lse_ref.at[r],
            lse_got.at[r],
            lse_send.at[r],
            lse_recv.at[r],
            group,
            x * 4 + partner_z[r],
        )
        for r in (1, 2, 3)
    ]
    mixed_out = [
        [
            remote(
                mixed_ref.at[r, i],
                mixed_got.at[r, i],
                mixed_send.at[r, i],
                mixed_recv.at[r, i],
                group,
                x * 4 + partner_z[r],
            )
            for r in (1, 2, 3)
        ]
        for i in range(CONVS)
    ]
    for copy in lse_out + mixed_out[0] + mixed_out[1]:
        copy.start()
    row_of = lane_iota((1, HEADS * SUF)) & (SUF - 1)
    pending = []

    def combine(i):
        if i == 0:
            for copy in lse_out:
                copy.wait_recv()
        for copy in mixed_out[i]:
            copy.wait_recv()
        if i + 2 < CONVS:
            for copy in mixed_out[i + 2]:
                copy.start()
        logs = [lse_ref[0, i, 0:1, :]] + [lse_got[r, i, 0:1, :] for r in (1, 2, 3)]
        peak = jnp.maximum(jnp.maximum(logs[0], logs[1]), jnp.maximum(logs[2], logs[3]))
        shares = [jnp.exp2(log - peak) for log in logs]
        scale = jnp.where(row_of < suffix_ref[conv_ref[group * CONVS + i]], 1.0, 0.0)
        scale = scale / (shares[0] + shares[1] + shares[2] + shares[3])
        joined = mixed_ref[0, i].astype(F32) * (shares[0] * scale)
        for r in (1, 2, 3):
            joined = joined + mixed_got[r, i].astype(F32) * (shares[r] * scale)
        turned = jnp.transpose(joined).astype(BF16)
        for head in range(HEADS):
            mixed[i * SUF : (i + 1) * SUF, head * HD : (head + 1) * HD] = turned[
                head * SUF : (head + 1) * SUF, :
            ]

    class Ring:
        def __init__(self, side, first, pick, buffers, way):
            self.side, self.first, self.pick, self.buffers = side, first, pick, buffers
            self.up, self.down, self.me, self.far, self.to_up, self.to_down = way
            self.top = pl.ds(side * 2 * SUF, SUF)
            self.bottom = pl.ds(side * 2 * SUF + SUF, SUF)

        def send(self, index, ref, to):
            sem = self.first + index
            copy = remote(
                ref,
                self.buffers.at[self.side, index],
                ring_send.at[sem],
                ring_recv.at[sem],
                group,
                to,
            )
            copy.start()
            pending.append(copy)
            return copy

        def start(self, ready):
            pick = self.pick
            ready(self.far)
            self.c0 = self.send(0, pick(self.far, self.top), self.to_up)
            self.c1 = self.send(1, pick(self.far, self.bottom), self.to_down)
            ready(self.up)
            self.c2 = self.send(2, pick(self.up, self.bottom), self.to_up)
            ready(self.down)
            self.c3 = self.send(3, pick(self.down, self.top), self.to_down)
            ready(self.me)

        def add(self, ref, *indices):
            total = ref[...].astype(F32)
            for index in indices:
                total = total + self.buffers[self.side, index].astype(F32)
            ref[...] = total.astype(BF16)

        def relay(self):
            pick = self.pick
            self.c0.wait_recv()
            self.add(pick(self.up, self.top), 0)
            self.c4 = self.send(4, pick(self.up, self.top), self.to_up)
            self.c1.wait_recv()
            self.add(pick(self.down, self.bottom), 1)
            self.c5 = self.send(5, pick(self.down, self.bottom), self.to_down)

        def finish(self):
            pick = self.pick
            self.c3.wait_recv()
            self.c4.wait_recv()
            self.add(pick(self.me, self.top), 3, 4)
            self.c2.wait_recv()
            self.c5.wait_recv()
            self.add(pick(self.me, self.bottom), 2, 5)

    along_x = (x_up, x_down, x, x_far, to_x_up, to_x_down)
    along_z = (z_up, z_down, z, z_far, to_z_up, to_z_down)
    firsts = (
        Ring(0, 0, lambda j, rows: part.at[j, :, rows], big, along_x),
        Ring(1, 6, lambda j, rows: part.at[:, j, rows], big, along_z),
    )
    seconds = (
        Ring(0, 12, lambda j, rows: part.at[x, j, rows], small, along_z),
        Ring(1, 18, lambda j, rows: part.at[j, z, rows], small, along_x),
    )

    def begin(side):
        combine(2 * side)
        combine(2 * side + 1)
        if side == 0:
            load.wait()
        rows = slice(side * 2 * SUF, (side + 1) * 2 * SUF)

        def ready(j):
            def one(k, carry):
                bx, bz = (j, k) if side == 0 else (k, j)
                columns = pl.ds(pl.multiple_of((bx * 4 + bz) * PART, PART), PART)
                part[bx, bz, rows] = jnp.dot(
                    mixed[rows], weights[:, columns], preferred_element_type=F32
                ).astype(BF16)
                return carry

            lax.fori_loop(0, 4, one, 0)

        firsts[side].start(ready)

    def turn(side):
        firsts[side].finish()
        seconds[side].start(lambda j: None)

    begin(0)
    begin(1)
    firsts[0].relay()
    firsts[1].relay()
    turn(0)
    turn(1)
    seconds[0].relay()
    seconds[1].relay()
    seconds[0].finish()
    seconds[1].finish()
    out_ref[...] = part[x, z]
    for copy in lse_out + mixed_out[0] + mixed_out[1] + mixed_out[2] + mixed_out[3] + pending:
        copy.wait_send()


def any_spec():
    return pl.BlockSpec(memory_space=pl.ANY)


def vmem_spec():
    return pl.BlockSpec(memory_space=pltpu.VMEM)


def smem_spec():
    return pl.BlockSpec(memory_space=pltpu.SMEM)


def shards(
    hidden_states,
    norm_gain,
    w_query,
    b_query,
    w_key,
    b_key,
    w_value,
    b_value,
    w_out,
    pool_keys,
    pool_values,
    conv_slots,
    page_table,
    prefix_len,
    suffix_len,
    new_dest,
):
    dma = pltpu.SemaphoreType.DMA
    freq = THETA ** (-(np.arange(HD // 2, dtype=np.float64) * 2.0 / HD))
    freq = jnp.asarray(np.concatenate([freq, freq])[None, :], F32)
    shape = jax.ShapeDtypeStruct
    got_k, got_v, queries, key_new, value_new, lists, new_pages = pl.pallas_call(
        gather_kernel,
        out_shape=[
            shape((4, GROUPS, 2, 2, PAGE, HD), BF16),
            shape((4, GROUPS, 2, 2, PAGE, HD), BF16),
            shape((4, CONVS, HEADS * SUF, HD), BF16),
            shape((ROWS, HD), BF16),
            shape((ROWS, HD), BF16),
            shape((PAGES + 8, HD), I32),
            shape((TENSOR, SUF, HD), BF16),
        ],
        in_specs=[smem_spec()] * 4
        + [vmem_spec()]
        + [any_spec()] * 6
        + [vmem_spec()] * 5,
        out_specs=[any_spec()] * 3 + [vmem_spec()] * 3 + [any_spec()],
        scratch_shapes=[
            pltpu.VMEM((4, 4, ROWS, PART), BF16),
            pltpu.VMEM((WIDTH, HEADS * HD), BF16),
            pltpu.VMEM((HD, WIDTH), BF16),
            pltpu.VMEM((ROWS, HEADS * HD), F32),
            pltpu.VMEM((ROWS, HD), F32),
            pltpu.VMEM((ROWS, HD), F32),
            pltpu.VMEM((GROUPS, 2, 8, PAGE, HD), BF16),
            pltpu.VMEM((4, 2 * GROUPS, 2, PAGE, HD), BF16),
            pltpu.VMEM((CONVS, HEADS * SUF, HD), BF16),
            pltpu.VMEM((ROWS, HD), BF16),
            pltpu.VMEM((ROWS, HD), BF16),
            pltpu.VMEM((GROUPS * CONVS, SUF, HD), BF16),
            pltpu.VMEM((TENSOR, SUF, HD), BF16),
            pltpu.SMEM((2, TENSOR), I32),
            pltpu.VMEM((1, WIDTH), F32),
            dma((8,)),
            dma((2, GROUPS)),
            dma((20,)),
            dma((20,)),
            dma((2, GROUPS)),
            dma((2, GROUPS)),
            dma((2, GROUPS, 4)),
            dma((2, GROUPS, 4)),
            dma((4,)),
            dma((4,)),
            dma((4,)),
            dma((4,)),
            dma((GROUPS,)),
            dma((GROUPS,)),
            dma((TENSOR,)),
            dma((TENSOR,)),
        ],
        compiler_params=pltpu.CompilerParams(
            collective_id=0, has_side_effects=True, vmem_limit_bytes=60 * 1024 * 1024
        ),
        name="gather",
    )(
        conv_slots,
        prefix_len,
        suffix_len,
        new_dest,
        page_table,
        hidden_states,
        pool_keys,
        pool_values,
        w_query,
        w_key.T,
        w_value.T,
        norm_gain,
        b_query,
        b_key,
        b_value,
        freq,
    )
    mixed, lse = pl.pallas_call(
        attend_kernel,
        out_shape=[
            shape((4, CONVS, HD, HEADS * SUF), BF16),
            shape((4, CONVS, 8, HEADS * SUF), F32),
        ],
        in_specs=[smem_spec()] + [vmem_spec()] * 5,
        out_specs=[vmem_spec()] * 2,
        compiler_params=pltpu.CompilerParams(vmem_limit_bytes=60 * 1024 * 1024),
        name="attend",
    )(
        lists,
        got_k.reshape(PAGES, 2, PAGE, HD),
        got_v.reshape(PAGES, 2, PAGE, HD),
        queries,
        key_new,
        value_new,
    )
    attn_out = pl.pallas_call(
        reduce_kernel,
        out_shape=shape((ROWS, PART), BF16),
        in_specs=[smem_spec()] * 2 + [vmem_spec()] * 2 + [any_spec()],
        out_specs=vmem_spec(),
        scratch_shapes=[
            pltpu.VMEM((HEADS * HD, WIDTH), BF16),
            pltpu.VMEM((4, CONVS, HD, HEADS * SUF), BF16),
            pltpu.VMEM((4, CONVS, 8, HEADS * SUF), F32),
            pltpu.VMEM((ROWS, HEADS * HD), BF16),
            pltpu.VMEM((4, 4, ROWS, PART), BF16),
            pltpu.VMEM((2, 6, 4, SUF, PART), BF16),
            pltpu.VMEM((2, 6, SUF, PART), BF16),
            dma((1,)),
            dma((4, CONVS)),
            dma((4, CONVS)),
            dma((4,)),
            dma((4,)),
            dma((24,)),
            dma((24,)),
        ],
        compiler_params=pltpu.CompilerParams(
            collective_id=1, has_side_effects=True, vmem_limit_bytes=60 * 1024 * 1024
        ),
        name="reduce",
    )(conv_slots, suffix_len, mixed, lse, w_out)
    pages = new_pages.reshape(TENSOR // 2, 2, SUF, HD)
    return (attn_out, pages[None, :, 0], pages[None, :, 1])


def solution(mesh):
    in_specs = (
        P("group", "tensor"),
        P(),
        P(None, "tensor"),
        P("tensor"),
        P(None, "tensor"),
        P("tensor"),
        P(None, "tensor"),
        P("tensor"),
        P("tensor", None),
        P(("group", "tensor"), None, None, None),
        P(("group", "tensor"), None, None, None),
        P(),
        P(),
        P(),
        P(),
        P(),
    )
    out_specs = (
        P("group", "tensor"),
        P(("group", "tensor"), None, None, None),
        P(("group", "tensor"), None, None, None),
    )
    return jax.shard_map(shards, mesh=mesh, in_specs=in_specs, out_specs=out_specs, check_vma=False)
```

```python
import jax
import jax.numpy as jnp
import numpy as np
from jax import lax
from jax.experimental import pallas as pl
from jax.experimental.pallas import tpu as pltpu
from jax.sharding import PartitionSpec as P

HD = 128
SUF = 64
CONVS = 4
ROWS = CONVS * SUF
GROUPS = 8
TENSOR = 16
WIDTH = 8192
PART = WIDTH // TENSOR
PAGES = 64
PAGE = 64
HEADS = 4
THETA = 1000000.0
EPSILON = 1e-06
NEGATIVE = -1e30
SCALE = HD**-0.5 * 1.4426950408889634
STEP = 4
BLOCKS = (PAGES + CONVS * (STEP - 1)) // STEP
LIST = 80
LN2 = 0.6931471805599453
MESH = pl.DeviceIdType.MESH
BF16 = jnp.bfloat16
F32 = jnp.float32
I32 = jnp.int32


def remote(src, dst, send_sem, recv_sem, group, tensor):
    return pltpu.make_async_remote_copy(
        src_ref=src,
        dst_ref=dst,
        send_sem=send_sem,
        recv_sem=recv_sem,
        device_id=(group, tensor),
        device_id_type=MESH,
    )


def place():
    group = lax.axis_index("group")
    tensor = lax.axis_index("tensor")
    return (
        group,
        tensor,
        lax.div(group, 2),
        lax.rem(group, 2),
        lax.div(tensor, 4),
        lax.rem(tensor, 4),
    )


def lane_iota(shape):
    return lax.broadcasted_iota(I32, shape, len(shape) - 1)


def row_iota(shape):
    return lax.broadcasted_iota(I32, shape, len(shape) - 2)


def gather_kernel(
    conv_ref,
    prefix_ref,
    suffix_ref,
    dest_ref,
    table_ref,
    hidden,
    pool_k,
    pool_v,
    w_query,
    w_key,
    w_value,
    gain_ref,
    b_query,
    b_key,
    b_value,
    freq_ref,
    got_k,
    got_v,
    queries,
    key_new,
    value_new,
    lists,
    new_pages,
    feat,
    wq,
    wkv,
    acc_q,
    acc_kv,
    squares,
    stage_k,
    stage_v,
    query_own,
    kv_own,
    kv_other,
    new_all,
    new_send,
    chosen,
    gain,
    load_sem,
    keep_sem,
    feat_send,
    feat_recv,
    y_send,
    y_recv,
    x_send,
    x_recv,
    v_send,
    v_recv,
    pair_send,
    pair_recv,
    group_send,
    group_recv,
    page_send,
    page_recv,
):
    group, tensor, y, core, x, z = place()
    parity = lax.rem(z, 2)
    partner_z = [z, z + 1 - 2 * parity, lax.rem(z + 2, 4), 3 - z]
    own = pltpu.make_async_copy(hidden, feat.at[x, z], load_sem.at[0])
    own.start()
    loads = [
        pltpu.make_async_copy(w_query, wq, load_sem.at[1]),
        pltpu.make_async_copy(w_key, wkv.at[pl.ds(0, HD // 2)], load_sem.at[2]),
        pltpu.make_async_copy(w_value, wkv.at[pl.ds(HD // 2, HD // 2)], load_sem.at[3]),
    ]
    for load in loads:
        load.start()

    def group_at(shift):
        to_y = lax.rem(y + shift // 2, 4)
        to_core = lax.rem(core + shift % 2, 2)
        return to_y * 2 + to_core

    barrier = pltpu.get_barrier_semaphore()
    for shift in range(1, GROUPS):
        pl.semaphore_signal(
            barrier, inc=1, device_id=(group_at(shift), tensor), device_id_type=MESH
        )

    def greet(off, carry):
        to = lax.rem(tensor + off, TENSOR)
        pl.semaphore_signal(barrier, inc=1, device_id=(group, to), device_id_type=MESH)
        return carry

    lax.fori_loop(1, TENSOR, greet, 0)
    pl.semaphore_wait(barrier, GROUPS - 1 + TENSOR - 1)

    own.wait()
    x_at = [lax.rem(x + shift, 4) for shift in range(4)]
    z_up, z_far, z_down = (lax.rem(z + shift, 4) for shift in (1, 2, 3))
    to_x_up, to_x_down = x_at[1] * 4 + z, x_at[3] * 4 + z
    to_z_up, to_z_down = x * 4 + z_up, x * 4 + z_down
    half_rows = ROWS // 2
    low_rows, high_rows = pl.ds(0, half_rows), pl.ds(half_rows, half_rows)
    sent, kept = [], []

    def pass_on(index, ref, to):
        copy = remote(ref, ref, feat_send.at[index], feat_recv.at[index], group, to)
        copy.start()
        sent.append(copy)
        return copy

    def spread(block, shift):
        ref = feat.at[x_at[shift], z]
        return (
            pass_on(4 + 4 * block, ref, to_z_up),
            pass_on(5 + 4 * block, ref, to_z_down),
        )

    def spread_on(block, shift, copies):
        copies[0].wait_recv()
        first = pass_on(6 + 4 * block, feat.at[x_at[shift], z_down, low_rows], to_z_up)
        copies[1].wait_recv()
        second = pass_on(7 + 4 * block, feat.at[x_at[shift], z_up, high_rows], to_z_down)
        return first, second

    pages_out = []

    def push(source, target, send_sem, recv_sem, to_group, to):
        copy = remote(source, target, send_sem, recv_sem, to_group, to)
        copy.start()
        pages_out.append(copy)
        return copy

    def keep(source, target, sem):
        copy = pltpu.make_async_copy(source, target, sem)
        copy.start()
        kept.append(copy)

    def slots(shift):
        return pl.ds(2 * group_at(shift), 2)

    def heads(step):
        return pl.ds(2 * x_at[step], 2)

    def keys_first(shift):
        return push(
            pool_k.at[slots(shift)],
            stage_k.at[shift],
            y_send.at[0, shift],
            y_recv.at[0, shift],
            group_at(shift),
            tensor,
        )

    def keys_second(shift):
        for step in (1, 3, 2, 0):
            if shift == 0:
                source = pool_k.at[slots(0), heads(step)]
            else:
                source = stage_k.at[shift, :, heads(step)]
            target = got_k.at[step, shift]
            if step == 0:
                keep(source, target, keep_sem.at[0, shift])
            else:
                keys_last.append(
                    push(
                        source,
                        target,
                        x_send.at[0, shift, step],
                        x_recv.at[0, shift, step],
                        group,
                        x_at[step] * 4 + z,
                    )
                )

    def values_first(step):
        return push(
            pool_v.at[:, heads(step)],
            stage_v.at[step],
            v_send.at[step],
            v_recv.at[step],
            group,
            x_at[step] * 4 + z,
        )

    def values_second(step):
        for shift in (1, 2, 6, 3, 7, 4, 5, 0):
            if step == 0:
                source = pool_v.at[slots(shift), heads(0)]
            else:
                source = stage_v.at[step, slots(shift)]
            target = got_v.at[step, shift]
            if shift == 0:
                keep(source, target, keep_sem.at[1, step])
            else:
                keys_last.append(
                    push(
                        source,
                        target,
                        x_send.at[1, shift, step],
                        x_recv.at[1, shift, step],
                        group_at(shift),
                        tensor,
                    )
                )

    keys_last = []
    f0 = pass_on(0, feat.at[x, z], to_x_up)
    f1 = pass_on(1, feat.at[x, z], to_x_down)
    s0 = spread(0, 0)
    key_first = {shift: keys_first(shift) for shift in (1, 2, 6, 3, 7, 4, 5)}
    f0.wait_recv()
    f2 = pass_on(2, feat.at[x_at[3], z, low_rows], to_x_up)
    s1 = spread(1, 3)
    f1.wait_recv()
    f3 = pass_on(3, feat.at[x_at[1], z, high_rows], to_x_down)
    s2 = spread(2, 1)
    prefix = [prefix_ref[conv_ref[group * CONVS + i]] for i in range(CONVS)]
    suffix = [suffix_ref[conv_ref[group * CONVS + i]] for i in range(CONVS)]

    offsets = row_iota((SUF, HD))
    positions = jnp.concatenate([offsets + prefix[i] for i in range(CONVS)], axis=0)
    angle = positions.astype(F32) * freq_ref[...]
    cosine = jnp.cos(angle)
    sine = jnp.sin(angle)
    sine = jnp.where(lane_iota((ROWS, HD)) < HD // 2, -sine, sine)

    f2.wait_recv()
    f3.wait_recv()
    s3 = spread(3, 2)
    value_first = {step: values_first(step) for step in (1, 3, 2)}
    keys_second(0)
    values_second(0)
    key_first[1].wait_recv()
    keys_second(1)
    r0 = spread_on(0, 0, s0)

    page_ids = lane_iota((1, PAGES))
    below = (row_iota((PAGES, PAGES)) < lane_iota((PAGES, PAGES))).astype(F32)
    lane = lane_iota((LIST, HD))
    place_id = row_iota((LIST, PAGES)).astype(F32)
    row_id = row_iota((LIST, 1)).astype(F32)
    codes = jnp.zeros((LIST, 1), F32)
    block_conv = jnp.zeros((LIST, 1), F32)
    block_first = jnp.zeros((LIST, 1), F32)
    last_block = jnp.zeros((LIST, 1), F32)
    has_block = jnp.zeros((LIST, 1), F32)
    begin = jnp.zeros((1, 1), F32)
    for i in range(CONVS):
        entry = table_ref[pl.ds(conv_ref[group * CONVS + i], 1), :]
        source = entry >> 4
        source_y, source_core = source >> 5, (source >> 4) & 1
        source_x, source_z = (source >> 2) & 3, source & 3
        live = jnp.clip(prefix[i] - page_ids * PAGE, 0, PAGE)
        here = (source_z == z) & (live > 0)
        where = ((x - source_x) & 3) * GROUPS
        where = where + ((y - source_y) & 3) * 2 + ((core - source_core) & 1)
        value = ((where * 2 + (entry & 1)) * 128 + live).astype(F32)
        here_f = here.astype(F32)
        order = jnp.dot(
            jnp.broadcast_to(here_f, (8, PAGES)), below, preferred_element_type=F32
        )[0:1, :]
        count = jnp.sum(here_f, axis=1, keepdims=True)
        blocks = jnp.floor((count + (STEP - 1)) * (1.0 / STEP))
        match = (order + begin * STEP == place_id) & (
            jnp.broadcast_to(here_f, (LIST, PAGES)) > 0.5
        )
        codes = codes + jnp.sum(jnp.where(match, value, 0.0), axis=1, keepdims=True)
        block_first = jnp.where(row_id == begin, 1.0, block_first)
        begin = begin + blocks
        if i < CONVS - 1:
            block_conv = block_conv + jnp.where(row_id >= begin, 1.0, 0.0)
        last_block = jnp.where(row_id == i, jnp.maximum(begin - 1.0, 0.0), last_block)
        has_block = jnp.where(row_id == i, jnp.minimum(count, 1.0), has_block)
    table = jnp.zeros((LIST, HD), F32)
    for column, data in enumerate((codes, block_conv, block_first, last_block, has_block)):
        table = jnp.where(lane == column, data, table)
    lists[...] = table.astype(I32)

    def find(to, carry):
        target = group * TENSOR + to
        index = jnp.int32(0)
        found = jnp.int32(0)
        for slot in range(GROUPS * CONVS):
            hit = dest_ref[conv_ref[slot]] == target
            index = jnp.where(hit, slot, index)
            found = jnp.where(hit, 1, found)
        chosen[0, to] = index
        chosen[1, to] = found
        return carry

    for load in loads:
        load.wait()
    gain[...] = gain_ref[...].astype(F32).reshape(1, WIDTH)
    query_bias = b_query[...].astype(F32).reshape(1, HEADS * HD)
    acc_q[...] = jnp.zeros_like(acc_q)
    acc_kv[...] = jnp.zeros_like(acc_kv)
    squares[...] = jnp.zeros_like(squares)

    def project(bz):
        def one(bx, carry):
            block = bx * 4 + bz
            rows = pl.ds(pl.multiple_of(block * PART, PART), PART)
            wide = feat[bx, bz].astype(F32)
            scaled = (wide * gain[:, rows]).astype(BF16)
            acc_q[...] += jnp.dot(scaled, wq[rows, :], preferred_element_type=F32)
            acc_kv[...] += lax.dot_general(
                scaled,
                wkv[:, rows],
                (((1,), (1,)), ((), ())),
                preferred_element_type=F32,
            )
            wide = wide * wide
            total = squares[...]
            for part in range(PART // HD):
                total = total + wide[:, part * HD : (part + 1) * HD]
            squares[...] = total
            return carry

        lax.fori_loop(0, 4, one, 0)

    project(z)
    lax.fori_loop(0, TENSOR, find, 0)
    r1 = spread_on(1, 3, s1)
    r2 = spread_on(2, 1, s2)
    for shift in (2, 6, 3, 7, 4, 5):
        key_first[shift].wait_recv()
        keys_second(shift)
    r3 = spread_on(3, 2, s3)
    project(z_up)
    project(z_down)
    for step in (1, 3, 2):
        value_first[step].wait_recv()
        values_second(step)
    for copies in (r0, r1, r2, r3):
        for copy in copies:
            copy.wait_recv()
    project(z_far)
    mean = jnp.sum(squares[...], axis=1, keepdims=True) * (1.0 / WIDTH)
    factor = lax.rsqrt(mean + EPSILON)
    bias = jnp.concatenate(
        [ref[...].astype(F32).reshape(1, HD // 2) for ref in (b_key, b_value)], axis=1
    )
    kv_own[...] = (acc_kv[...] * factor + bias).astype(BF16)
    kv_copy = remote(
        kv_own,
        kv_other,
        pair_send.at[0],
        pair_recv.at[0],
        group,
        x * 4 + partner_z[1],
    )
    kv_copy.start()

    def rotate(values):
        return values * cosine + pltpu.roll(values, HD // 2, 1) * sine

    for head in range(HEADS):
        columns = slice(head * HD, (head + 1) * HD)
        values = acc_q[:, columns] * factor + query_bias[:, columns]
        values = rotate(values).astype(BF16)
        for i in range(CONVS):
            query_own[i, head * SUF : (head + 1) * SUF, :] = values[i * SUF : (i + 1) * SUF, :]
    query_out = [
        remote(
            query_own,
            queries.at[r],
            pair_send.at[r],
            pair_recv.at[r],
            group,
            x * 4 + partner_z[r],
        )
        for r in (1, 2, 3)
    ]
    for copy in query_out:
        copy.start()
    query_keep = pltpu.make_async_copy(query_own, queries.at[0], load_sem.at[4])
    query_keep.start()

    kv_copy.wait_recv()
    mine = kv_own[...].astype(F32)
    theirs = kv_other[...].astype(F32)
    even = jnp.where(parity == 0, mine, theirs)
    odd = jnp.where(parity == 0, theirs, mine)
    low = lane_iota((ROWS, HD)) < HD // 2
    keys = jnp.where(low, even, pltpu.roll(odd, HD // 2, 1))
    keys = rotate(keys)
    values = jnp.where(low, pltpu.roll(even, HD // 2, 1), odd)
    key_new[...] = keys.astype(BF16)
    value_new[...] = values.astype(BF16)

    page = jnp.where(parity == 0, keys.astype(BF16).astype(F32), values)
    live_row = jnp.concatenate([offsets < suffix[i] for i in range(CONVS)], axis=0)
    page = jnp.where(live_row, page, 0.0).astype(BF16)
    new_all[pl.ds(group * CONVS, CONVS)] = page.reshape(CONVS, SUF, HD)
    new_ref = new_all.at[pl.ds(group * CONVS, CONVS)]
    group_out = [
        remote(
            new_ref,
            new_ref,
            group_send.at[shift],
            group_recv.at[shift],
            group_at(shift),
            tensor,
        )
        for shift in range(1, GROUPS)
    ]
    for copy in group_out:
        copy.start()
    for copy in group_out:
        copy.wait_recv()

    def choose(to, carry):
        page = new_all[chosen[0, to]].astype(F32)
        new_send[to] = (page * chosen[1, to].astype(F32)).astype(BF16)
        return carry

    lax.fori_loop(0, TENSOR, choose, 0)
    mine_copy = pltpu.make_async_copy(
        new_send.at[tensor], new_pages.at[tensor], load_sem.at[5]
    )
    mine_copy.start()

    def page_copy(off):
        to = lax.rem(tensor + off, TENSOR)
        return remote(
            new_send.at[to],
            new_pages.at[tensor],
            page_send.at[off],
            page_recv.at[off],
            group,
            to,
        )

    def page_start(off, carry):
        page_copy(off).start()
        return carry

    lax.fori_loop(1, TENSOR, page_start, 0)

    mine_copy.wait()
    query_keep.wait()
    kv_copy.wait_send()
    for copy in query_out:
        copy.wait()
    for copy in sent + pages_out + group_out:
        copy.wait_send()

    def page_end(off, carry):
        page_copy(off).wait()
        return carry

    lax.fori_loop(1, TENSOR, page_end, 0)
    for copy in kept:
        copy.wait()
    for copy in keys_last:
        copy.wait_recv()


def attend_kernel(
    lists,
    conv_ref,
    suffix_ref,
    key_new,
    value_new,
    queries_hbm,
    got_k_hbm,
    got_v_hbm,
    w_out,
    out_ref,
    queries,
    got_k,
    got_v,
    weights,
    accums,
    stats,
    own_accum,
    own_stats,
    mixed_out,
    lse_out,
    mixed_got,
    lse_got,
    mixed,
    part,
    big,
    small,
    load_sem,
    mixed_send,
    mixed_recv,
    lse_send,
    lse_recv,
    ring_send,
    ring_recv,
):
    group, tensor, y, core, x, z = place()
    partner_z = [z, z + 1 - 2 * lax.rem(z, 2), lax.rem(z + 2, 4), 3 - z]
    load_query = pltpu.make_async_copy(queries_hbm, queries, load_sem.at[0])
    load_k = pltpu.make_async_copy(got_k_hbm, got_k, load_sem.at[1])
    load_v = pltpu.make_async_copy(got_v_hbm, got_v, load_sem.at[2])
    load = pltpu.make_async_copy(w_out, weights, load_sem.at[3])
    for copy in (load_query, load_k, load_v, load):
        copy.start()
    x_up, x_far, x_down = (lax.rem(x + shift, 4) for shift in (1, 2, 3))
    z_up, z_far, z_down = (lax.rem(z + shift, 4) for shift in (1, 2, 3))
    to_x_up, to_x_down = x_up * 4 + z, x_down * 4 + z
    to_z_up, to_z_down = x * 4 + z_up, x * 4 + z_down
    barrier = pltpu.get_barrier_semaphore()
    for to in (to_x_up, to_x_down, to_z_up, to_z_down, x * 4 + z_far):
        pl.semaphore_signal(barrier, inc=1, device_id=(group, to), device_id_type=MESH)

    half = HEADS * SUF
    own_head = lax.div(z, 2)

    def score(keys, query):
        return lax.dot_general(
            keys, query, (((1,), (1,)), ((), ())), preferred_element_type=F32
        )

    def mix(values, shares):
        return lax.dot_general(
            values,
            shares.astype(BF16),
            (((0,), (0,)), ((), ())),
            preferred_element_type=F32,
        )

    causal = row_iota((SUF, half)) <= (lane_iota((SUF, half)) & (SUF - 1))
    load_query.wait()
    for i in range(CONVS):
        rows = slice(i * SUF, (i + 1) * SUF)
        scores = score(key_new[rows], queries[0, i])
        scores = jnp.where(causal, scores * SCALE, NEGATIVE)
        peak = jnp.max(scores, axis=0, keepdims=True)
        shares = jnp.exp2(scores - peak)
        own_accum[i] = mix(value_new[rows], shares)
        own_stats[i, 0:1, :] = peak
        own_stats[i, 1:2, :] = jnp.sum(shares, axis=0, keepdims=True)
    load_k.wait()
    load_v.wait()

    token = row_iota((PAGE, half))

    def attend(head, sides):
        def block(b, state):
            codes = [lists[b * STEP + p, 0] for p in range(STEP)]
            conv = lists[b, 1]
            first = lists[b, 2] == 1
            keys = jnp.concatenate([got_k[code >> 7, head] for code in codes], axis=0)
            values = jnp.concatenate([got_v[code >> 7, head] for code in codes], axis=0)
            out = []
            for side, (peak, total, accum) in zip(sides, state):
                scores = score(keys, queries[side, conv])
                scores = jnp.concatenate(
                    [
                        jnp.where(
                            token < (codes[p] & 127),
                            scores[p * PAGE : (p + 1) * PAGE] * SCALE,
                            NEGATIVE,
                        )
                        for p in range(STEP)
                    ],
                    axis=0,
                )
                peak = jnp.where(first, NEGATIVE, peak)
                fresh = jnp.maximum(peak, jnp.max(scores, axis=0, keepdims=True))
                shrink = jnp.exp2(peak - fresh)
                shares = jnp.exp2(scores - fresh)
                total = total * shrink + jnp.sum(shares, axis=0, keepdims=True)
                accum = accum * shrink + mix(values, shares)
                accums[side, b] = accum
                stats[side, b, 0:1, :] = fresh
                stats[side, b, 1:2, :] = total
                out.append((fresh, total, accum))
            return tuple(out)

        empty = (
            jnp.full((1, half), NEGATIVE, F32),
            jnp.zeros((1, half), F32),
            jnp.zeros((HD, half), F32),
        )
        lax.fori_loop(0, BLOCKS, block, tuple(empty for _ in sides))

    def result(side, i):
        last = lists[i, 3]
        some = lists[i, 4] == 1
        peak = jnp.where(some, stats[side, last, 0:1, :], NEGATIVE)
        total = jnp.where(some, stats[side, last, 1:2, :], 0.0)
        accum = accums[side, last] * jnp.where(some, 1.0, 0.0)
        return peak, total, accum

    def send(side):
        for i in range(CONVS):
            peak, total, accum = result(side, i)
            safe = jnp.where(total > 0.0, total, 1.0)
            mixed_out[side, i] = (accum * (1.0 / safe)).astype(BF16)
            lse = jnp.where(total > 0.0, peak + jnp.log(safe) * (1.0 / LN2), NEGATIVE)
            lse_out[side, i] = jnp.broadcast_to(lse, (8, half))
        copies = [
            remote(
                source.at[side],
                target.at[side],
                send_sem.at[side],
                recv_sem.at[side],
                group,
                x * 4 + partner_z[side],
            )
            for source, target, send_sem, recv_sem in (
                (mixed_out, mixed_got, mixed_send, mixed_recv),
                (lse_out, lse_got, lse_send, lse_recv),
            )
        ]
        for copy in copies:
            copy.start()
        return copies

    attend(1 - own_head, (2, 3))
    pl.semaphore_wait(barrier, 5)
    exchanged = send(2) + send(3)
    attend(own_head, (1,))
    exchanged = exchanged + send(1)
    attend(own_head, (0,))
    for copy in exchanged:
        copy.wait_recv()
    row_of = lane_iota((1, half)) & (SUF - 1)

    def combine(i):
        peak, total, accum = result(0, i)
        own_peak = own_stats[i, 0:1, :]
        logs = [lse_got[r, i, 0:1, :] for r in (1, 2, 3)]
        top = jnp.maximum(
            jnp.maximum(peak, own_peak), jnp.maximum(jnp.maximum(logs[0], logs[1]), logs[2])
        )
        shares = [jnp.exp2(log - top) for log in logs]
        first, second = jnp.exp2(peak - top), jnp.exp2(own_peak - top)
        total = total * first + own_stats[i, 1:2, :] * second
        total = total + shares[0] + shares[1] + shares[2]
        scale = jnp.where(row_of < suffix_ref[conv_ref[group * CONVS + i]], 1.0, 0.0) / total
        joined = accum * (first * scale) + own_accum[i] * (second * scale)
        for r in (1, 2, 3):
            joined = joined + mixed_got[r, i].astype(F32) * (shares[r - 1] * scale)
        turned = jnp.transpose(joined).astype(BF16)
        for head in range(HEADS):
            mixed[i * SUF : (i + 1) * SUF, head * HD : (head + 1) * HD] = turned[
                head * SUF : (head + 1) * SUF, :
            ]

    pending = []

    class Ring:
        def __init__(self, side, first, pick, buffers, way):
            self.side, self.first, self.pick, self.buffers = side, first, pick, buffers
            self.up, self.down, self.me, self.far, self.to_up, self.to_down = way
            self.top = pl.ds(side * 2 * SUF, SUF)
            self.bottom = pl.ds(side * 2 * SUF + SUF, SUF)

        def send(self, index, ref, to):
            sem = self.first + index
            copy = remote(
                ref,
                self.buffers.at[self.side, index],
                ring_send.at[sem],
                ring_recv.at[sem],
                group,
                to,
            )
            copy.start()
            pending.append(copy)
            return copy

        def start(self, ready):
            pick = self.pick
            ready(self.far)
            self.c0 = self.send(0, pick(self.far, self.top), self.to_up)
            self.c1 = self.send(1, pick(self.far, self.bottom), self.to_down)
            ready(self.up)
            self.c2 = self.send(2, pick(self.up, self.bottom), self.to_up)
            ready(self.down)
            self.c3 = self.send(3, pick(self.down, self.top), self.to_down)
            ready(self.me)

        def add(self, ref, *indices):
            total = ref[...].astype(F32)
            for index in indices:
                total = total + self.buffers[self.side, index].astype(F32)
            ref[...] = total.astype(BF16)

        def relay(self):
            pick = self.pick
            self.c0.wait_recv()
            self.add(pick(self.up, self.top), 0)
            self.c4 = self.send(4, pick(self.up, self.top), self.to_up)
            self.c1.wait_recv()
            self.add(pick(self.down, self.bottom), 1)
            self.c5 = self.send(5, pick(self.down, self.bottom), self.to_down)

        def finish(self):
            pick = self.pick
            self.c3.wait_recv()
            self.c4.wait_recv()
            self.add(pick(self.me, self.top), 3, 4)
            self.c2.wait_recv()
            self.c5.wait_recv()
            self.add(pick(self.me, self.bottom), 2, 5)

    along_x = (x_up, x_down, x, x_far, to_x_up, to_x_down)
    along_z = (z_up, z_down, z, z_far, to_z_up, to_z_down)
    firsts = (
        Ring(0, 0, lambda j, rows: part.at[j, :, rows], big, along_x),
        Ring(1, 6, lambda j, rows: part.at[:, j, rows], big, along_z),
    )
    seconds = (
        Ring(0, 12, lambda j, rows: part.at[x, j, rows], small, along_z),
        Ring(1, 18, lambda j, rows: part.at[j, z, rows], small, along_x),
    )

    def begin(side):
        combine(2 * side)
        combine(2 * side + 1)
        if side == 0:
            load.wait()
        rows = slice(side * 2 * SUF, (side + 1) * 2 * SUF)

        def ready(j):
            def one(k, carry):
                bx, bz = (j, k) if side == 0 else (k, j)
                columns = pl.ds(pl.multiple_of((bx * 4 + bz) * PART, PART), PART)
                part[bx, bz, rows] = jnp.dot(
                    mixed[rows], weights[:, columns], preferred_element_type=F32
                ).astype(BF16)
                return carry

            lax.fori_loop(0, 4, one, 0)

        firsts[side].start(ready)

    def turn(side):
        firsts[side].finish()
        seconds[side].start(lambda j: None)

    begin(0)
    begin(1)
    firsts[0].relay()
    firsts[1].relay()
    turn(0)
    turn(1)
    seconds[0].relay()
    seconds[1].relay()
    seconds[0].finish()
    seconds[1].finish()
    out_ref[...] = part[x, z]
    for copy in exchanged + pending:
        copy.wait_send()


def any_spec():
    return pl.BlockSpec(memory_space=pl.ANY)


def vmem_spec():
    return pl.BlockSpec(memory_space=pltpu.VMEM)


def smem_spec():
    return pl.BlockSpec(memory_space=pltpu.SMEM)


def shards(
    hidden_states,
    norm_gain,
    w_query,
    b_query,
    w_key,
    b_key,
    w_value,
    b_value,
    w_out,
    pool_keys,
    pool_values,
    conv_slots,
    page_table,
    prefix_len,
    suffix_len,
    new_dest,
):
    dma = pltpu.SemaphoreType.DMA
    freq = THETA ** (-(np.arange(HD // 2, dtype=np.float64) * 2.0 / HD))
    freq = jnp.asarray(np.concatenate([freq, freq])[None, :], F32)
    shape = jax.ShapeDtypeStruct
    got_k, got_v, queries, key_new, value_new, lists, new_pages = pl.pallas_call(
        gather_kernel,
        out_shape=[
            shape((4, GROUPS, 2, 2, PAGE, HD), BF16),
            shape((4, GROUPS, 2, 2, PAGE, HD), BF16),
            shape((4, CONVS, HEADS * SUF, HD), BF16),
            shape((ROWS, HD), BF16),
            shape((ROWS, HD), BF16),
            shape((LIST, HD), I32),
            shape((TENSOR, SUF, HD), BF16),
        ],
        in_specs=[smem_spec()] * 4
        + [vmem_spec()]
        + [any_spec()] * 6
        + [vmem_spec()] * 5,
        out_specs=[any_spec()] * 3 + [vmem_spec()] * 3 + [any_spec()],
        scratch_shapes=[
            pltpu.VMEM((4, 4, ROWS, PART), BF16),
            pltpu.VMEM((WIDTH, HEADS * HD), BF16),
            pltpu.VMEM((HD, WIDTH), BF16),
            pltpu.VMEM((ROWS, HEADS * HD), F32),
            pltpu.VMEM((ROWS, HD), F32),
            pltpu.VMEM((ROWS, HD), F32),
            pltpu.VMEM((GROUPS, 2, 8, PAGE, HD), BF16),
            pltpu.VMEM((4, 2 * GROUPS, 2, PAGE, HD), BF16),
            pltpu.VMEM((CONVS, HEADS * SUF, HD), BF16),
            pltpu.VMEM((ROWS, HD), BF16),
            pltpu.VMEM((ROWS, HD), BF16),
            pltpu.VMEM((GROUPS * CONVS, SUF, HD), BF16),
            pltpu.VMEM((TENSOR, SUF, HD), BF16),
            pltpu.SMEM((2, TENSOR), I32),
            pltpu.VMEM((1, WIDTH), F32),
            dma((8,)),
            dma((2, GROUPS)),
            dma((20,)),
            dma((20,)),
            dma((2, GROUPS)),
            dma((2, GROUPS)),
            dma((2, GROUPS, 4)),
            dma((2, GROUPS, 4)),
            dma((4,)),
            dma((4,)),
            dma((4,)),
            dma((4,)),
            dma((GROUPS,)),
            dma((GROUPS,)),
            dma((TENSOR,)),
            dma((TENSOR,)),
        ],
        compiler_params=pltpu.CompilerParams(
            collective_id=0, has_side_effects=True, vmem_limit_bytes=60 * 1024 * 1024
        ),
        name="gather",
    )(
        conv_slots,
        prefix_len,
        suffix_len,
        new_dest,
        page_table,
        hidden_states,
        pool_keys,
        pool_values,
        w_query,
        w_key.T,
        w_value.T,
        norm_gain,
        b_query,
        b_key,
        b_value,
        freq,
    )
    attn_out = pl.pallas_call(
        attend_kernel,
        out_shape=shape((ROWS, PART), BF16),
        in_specs=[smem_spec()] * 3 + [vmem_spec()] * 2 + [any_spec()] * 4,
        out_specs=vmem_spec(),
        scratch_shapes=[
            pltpu.VMEM((4, CONVS, HEADS * SUF, HD), BF16),
            pltpu.VMEM((PAGES, 2, PAGE, HD), BF16),
            pltpu.VMEM((PAGES, 2, PAGE, HD), BF16),
            pltpu.VMEM((HEADS * HD, WIDTH), BF16),
            pltpu.VMEM((4, BLOCKS, HD, HEADS * SUF), F32),
            pltpu.VMEM((4, BLOCKS, 8, HEADS * SUF), F32),
            pltpu.VMEM((CONVS, HD, HEADS * SUF), F32),
            pltpu.VMEM((CONVS, 8, HEADS * SUF), F32),
            pltpu.VMEM((4, CONVS, HD, HEADS * SUF), BF16),
            pltpu.VMEM((4, CONVS, 8, HEADS * SUF), F32),
            pltpu.VMEM((4, CONVS, HD, HEADS * SUF), BF16),
            pltpu.VMEM((4, CONVS, 8, HEADS * SUF), F32),
            pltpu.VMEM((ROWS, HEADS * HD), BF16),
            pltpu.VMEM((4, 4, ROWS, PART), BF16),
            pltpu.VMEM((2, 6, 4, SUF, PART), BF16),
            pltpu.VMEM((2, 6, SUF, PART), BF16),
            dma((4,)),
            dma((4,)),
            dma((4,)),
            dma((4,)),
            dma((4,)),
            dma((24,)),
            dma((24,)),
        ],
        compiler_params=pltpu.CompilerParams(
            collective_id=1, has_side_effects=True, vmem_limit_bytes=60 * 1024 * 1024
        ),
        name="attend",
    )(
        lists,
        conv_slots,
        suffix_len,
        key_new,
        value_new,
        queries,
        got_k.reshape(PAGES, 2, PAGE, HD),
        got_v.reshape(PAGES, 2, PAGE, HD),
        w_out,
    )
    pages = new_pages.reshape(TENSOR // 2, 2, SUF, HD)
    return (attn_out, pages[None, :, 0], pages[None, :, 1])


def solution(mesh):
    in_specs = (
        P("group", "tensor"),
        P(),
        P(None, "tensor"),
        P("tensor"),
        P(None, "tensor"),
        P("tensor"),
        P(None, "tensor"),
        P("tensor"),
        P("tensor", None),
        P(("group", "tensor"), None, None, None),
        P(("group", "tensor"), None, None, None),
        P(),
        P(),
        P(),
        P(),
        P(),
    )
    out_specs = (
        P("group", "tensor"),
        P(("group", "tensor"), None, None, None),
        P(("group", "tensor"), None, None, None),
    )
    return jax.shard_map(shards, mesh=mesh, in_specs=in_specs, out_specs=out_specs, check_vma=False)
```

```python
import jax
import jax.numpy as jnp
import numpy as np
from jax import lax
from jax.experimental import pallas as pl
from jax.experimental.pallas import tpu as pltpu
from jax.sharding import PartitionSpec as P

HD = 128
SUF = 64
CONVS = 4
ROWS = CONVS * SUF
GROUPS = 8
TENSOR = 16
WIDTH = 8192
PART = WIDTH // TENSOR
PAGES = 64
PAGE = 64
HEADS = 4
THETA = 1000000.0
EPSILON = 1e-06
NEGATIVE = -1e30
SCALE = HD**-0.5 * 1.4426950408889634
STEP = 4
PACK = 4
BLOCKS = -(-((PAGES + CONVS * (STEP - 1)) // STEP) // PACK) * PACK
LIST = 80
LN2 = 0.6931471805599453
MESH = pl.DeviceIdType.MESH
BF16 = jnp.bfloat16
F32 = jnp.float32
I32 = jnp.int32


def remote(src, dst, send_sem, recv_sem, group, tensor):
    return pltpu.make_async_remote_copy(
        src_ref=src,
        dst_ref=dst,
        send_sem=send_sem,
        recv_sem=recv_sem,
        device_id=(group, tensor),
        device_id_type=MESH,
    )


def place():
    group = lax.axis_index("group")
    tensor = lax.axis_index("tensor")
    return (
        group,
        tensor,
        lax.div(group, 2),
        lax.rem(group, 2),
        lax.div(tensor, 4),
        lax.rem(tensor, 4),
    )


def lane_iota(shape):
    return lax.broadcasted_iota(I32, shape, len(shape) - 1)


def row_iota(shape):
    return lax.broadcasted_iota(I32, shape, len(shape) - 2)


def gather_kernel(
    conv_ref,
    prefix_ref,
    suffix_ref,
    dest_ref,
    table_ref,
    hidden,
    pool_k,
    pool_v,
    w_query,
    w_key,
    w_value,
    gain_ref,
    b_query,
    b_key,
    b_value,
    freq_ref,
    got_k,
    got_v,
    queries,
    key_new,
    value_new,
    lists,
    new_pages,
    feat,
    wq,
    wkv,
    acc_q,
    acc_kv,
    squares,
    stage_k,
    stage_v,
    query_own,
    kv_own,
    kv_other,
    new_all,
    new_send,
    chosen,
    gain,
    load_sem,
    keep_sem,
    feat_send,
    feat_recv,
    y_send,
    y_recv,
    x_send,
    x_recv,
    v_send,
    v_recv,
    pair_send,
    pair_recv,
    group_send,
    group_recv,
    page_send,
    page_recv,
):
    group, tensor, y, core, x, z = place()
    parity = lax.rem(z, 2)
    partner_z = [z, z + 1 - 2 * parity, lax.rem(z + 2, 4), 3 - z]
    own = pltpu.make_async_copy(hidden, feat.at[x, z], load_sem.at[0])
    own.start()
    loads = [
        pltpu.make_async_copy(w_query, wq, load_sem.at[1]),
        pltpu.make_async_copy(w_key, wkv.at[pl.ds(0, HD // 2)], load_sem.at[2]),
        pltpu.make_async_copy(w_value, wkv.at[pl.ds(HD // 2, HD // 2)], load_sem.at[3]),
    ]
    for load in loads:
        load.start()

    def group_at(shift):
        to_y = lax.rem(y + shift // 2, 4)
        to_core = lax.rem(core + shift % 2, 2)
        return to_y * 2 + to_core

    barrier = pltpu.get_barrier_semaphore()
    for shift in range(1, GROUPS):
        pl.semaphore_signal(
            barrier, inc=1, device_id=(group_at(shift), tensor), device_id_type=MESH
        )

    def greet(off, carry):
        to = lax.rem(tensor + off, TENSOR)
        pl.semaphore_signal(barrier, inc=1, device_id=(group, to), device_id_type=MESH)
        return carry

    lax.fori_loop(1, TENSOR, greet, 0)
    pl.semaphore_wait(barrier, GROUPS - 1 + TENSOR - 1)

    own.wait()
    x_at = [lax.rem(x + shift, 4) for shift in range(4)]
    z_up, z_far, z_down = (lax.rem(z + shift, 4) for shift in (1, 2, 3))
    to_x_up, to_x_down = x_at[1] * 4 + z, x_at[3] * 4 + z
    to_z_up, to_z_down = x * 4 + z_up, x * 4 + z_down
    half_rows = ROWS // 2
    low_rows, high_rows = pl.ds(0, half_rows), pl.ds(half_rows, half_rows)
    sent, kept = [], []

    def pass_on(index, ref, to):
        copy = remote(ref, ref, feat_send.at[index], feat_recv.at[index], group, to)
        copy.start()
        sent.append(copy)
        return copy

    def spread(block, shift):
        ref = feat.at[x_at[shift], z]
        return (
            pass_on(4 + 4 * block, ref, to_z_up),
            pass_on(5 + 4 * block, ref, to_z_down),
        )

    def spread_on(block, shift, copies):
        copies[0].wait_recv()
        first = pass_on(6 + 4 * block, feat.at[x_at[shift], z_down, low_rows], to_z_up)
        copies[1].wait_recv()
        second = pass_on(7 + 4 * block, feat.at[x_at[shift], z_up, high_rows], to_z_down)
        return first, second

    pages_out = []

    def push(source, target, send_sem, recv_sem, to_group, to):
        copy = remote(source, target, send_sem, recv_sem, to_group, to)
        copy.start()
        pages_out.append(copy)
        return copy

    def keep(source, target, sem):
        copy = pltpu.make_async_copy(source, target, sem)
        copy.start()
        kept.append(copy)

    def slots(shift):
        return pl.ds(2 * group_at(shift), 2)

    def heads(step):
        return pl.ds(2 * x_at[step], 2)

    def keys_first(shift):
        return push(
            pool_k.at[slots(shift)],
            stage_k.at[shift],
            y_send.at[0, shift],
            y_recv.at[0, shift],
            group_at(shift),
            tensor,
        )

    def keys_second(shift):
        for step in (1, 3, 2, 0):
            if shift == 0:
                source = pool_k.at[slots(0), heads(step)]
            else:
                source = stage_k.at[shift, :, heads(step)]
            target = got_k.at[step, shift]
            if step == 0:
                keep(source, target, keep_sem.at[0, shift])
            else:
                keys_last.append(
                    push(
                        source,
                        target,
                        x_send.at[0, shift, step],
                        x_recv.at[0, shift, step],
                        group,
                        x_at[step] * 4 + z,
                    )
                )

    def values_first(step):
        return push(
            pool_v.at[:, heads(step)],
            stage_v.at[step],
            v_send.at[step],
            v_recv.at[step],
            group,
            x_at[step] * 4 + z,
        )

    def values_second(step):
        for shift in (1, 2, 6, 3, 7, 4, 5, 0):
            if step == 0:
                source = pool_v.at[slots(shift), heads(0)]
            else:
                source = stage_v.at[step, slots(shift)]
            target = got_v.at[step, shift]
            if shift == 0:
                keep(source, target, keep_sem.at[1, step])
            else:
                keys_last.append(
                    push(
                        source,
                        target,
                        x_send.at[1, shift, step],
                        x_recv.at[1, shift, step],
                        group_at(shift),
                        tensor,
                    )
                )

    keys_last = []
    f0 = pass_on(0, feat.at[x, z], to_x_up)
    f1 = pass_on(1, feat.at[x, z], to_x_down)
    s0 = spread(0, 0)
    key_first = {shift: keys_first(shift) for shift in (1, 2, 6, 3, 7, 4, 5)}
    f0.wait_recv()
    f2 = pass_on(2, feat.at[x_at[3], z, low_rows], to_x_up)
    s1 = spread(1, 3)
    f1.wait_recv()
    f3 = pass_on(3, feat.at[x_at[1], z, high_rows], to_x_down)
    s2 = spread(2, 1)
    prefix = [prefix_ref[conv_ref[group * CONVS + i]] for i in range(CONVS)]
    suffix = [suffix_ref[conv_ref[group * CONVS + i]] for i in range(CONVS)]

    offsets = row_iota((SUF, HD))
    positions = jnp.concatenate([offsets + prefix[i] for i in range(CONVS)], axis=0)
    angle = positions.astype(F32) * freq_ref[...]
    cosine = jnp.cos(angle)
    sine = jnp.sin(angle)
    sine = jnp.where(lane_iota((ROWS, HD)) < HD // 2, -sine, sine)

    f2.wait_recv()
    f3.wait_recv()
    s3 = spread(3, 2)
    value_first = {step: values_first(step) for step in (1, 3, 2)}
    keys_second(0)
    values_second(0)
    key_first[1].wait_recv()
    keys_second(1)
    r0 = spread_on(0, 0, s0)

    page_ids = lane_iota((1, PAGES))
    below = (row_iota((PAGES, PAGES)) < lane_iota((PAGES, PAGES))).astype(F32)
    lane = lane_iota((LIST, HD))
    place_id = row_iota((LIST, PAGES)).astype(F32)
    row_id = row_iota((LIST, 1)).astype(F32)
    codes = jnp.zeros((LIST, 1), F32)
    block_conv = jnp.zeros((LIST, 1), F32)
    block_first = jnp.zeros((LIST, 1), F32)
    last_block = jnp.zeros((LIST, 1), F32)
    has_block = jnp.zeros((LIST, 1), F32)
    begin = jnp.zeros((1, 1), F32)
    for i in range(CONVS):
        entry = table_ref[pl.ds(conv_ref[group * CONVS + i], 1), :]
        source = entry >> 4
        source_y, source_core = source >> 5, (source >> 4) & 1
        source_x, source_z = (source >> 2) & 3, source & 3
        live = jnp.clip(prefix[i] - page_ids * PAGE, 0, PAGE)
        here = (source_z == z) & (live > 0)
        where = ((x - source_x) & 3) * GROUPS
        where = where + ((y - source_y) & 3) * 2 + ((core - source_core) & 1)
        value = ((where * 2 + (entry & 1)) * 128 + live).astype(F32)
        here_f = here.astype(F32)
        order = jnp.dot(
            jnp.broadcast_to(here_f, (8, PAGES)), below, preferred_element_type=F32
        )[0:1, :]
        count = jnp.sum(here_f, axis=1, keepdims=True)
        blocks = jnp.floor((count + (STEP - 1)) * (1.0 / STEP))
        match = (order + begin * STEP == place_id) & (
            jnp.broadcast_to(here_f, (LIST, PAGES)) > 0.5
        )
        codes = codes + jnp.sum(jnp.where(match, value, 0.0), axis=1, keepdims=True)
        block_first = jnp.where(row_id == begin, 1.0, block_first)
        begin = begin + blocks
        if i < CONVS - 1:
            block_conv = block_conv + jnp.where(row_id >= begin, 1.0, 0.0)
        last_block = jnp.where(row_id == i, jnp.maximum(begin - 1.0, 0.0), last_block)
        has_block = jnp.where(row_id == i, jnp.minimum(count, 1.0), has_block)
    table = jnp.zeros((LIST, HD), F32)
    for column, data in enumerate((codes, block_conv, block_first, last_block, has_block)):
        table = jnp.where(lane == column, data, table)
    lists[...] = table.astype(I32)

    def find(to, carry):
        target = group * TENSOR + to
        index = jnp.int32(0)
        found = jnp.int32(0)
        for slot in range(GROUPS * CONVS):
            hit = dest_ref[conv_ref[slot]] == target
            index = jnp.where(hit, slot, index)
            found = jnp.where(hit, 1, found)
        chosen[0, to] = index
        chosen[1, to] = found
        return carry

    for load in loads:
        load.wait()
    gain[...] = gain_ref[...].astype(F32).reshape(1, WIDTH)
    query_bias = b_query[...].astype(F32).reshape(1, HEADS * HD)
    acc_q[...] = jnp.zeros_like(acc_q)
    acc_kv[...] = jnp.zeros_like(acc_kv)
    squares[...] = jnp.zeros_like(squares)

    def project(bz):
        def one(bx, carry):
            block = bx * 4 + bz
            rows = pl.ds(pl.multiple_of(block * PART, PART), PART)
            wide = feat[bx, bz].astype(F32)
            scaled = (wide * gain[:, rows]).astype(BF16)
            acc_q[...] += jnp.dot(scaled, wq[rows, :], preferred_element_type=F32)
            acc_kv[...] += lax.dot_general(
                scaled,
                wkv[:, rows],
                (((1,), (1,)), ((), ())),
                preferred_element_type=F32,
            )
            wide = wide * wide
            total = squares[...]
            for part in range(PART // HD):
                total = total + wide[:, part * HD : (part + 1) * HD]
            squares[...] = total
            return carry

        lax.fori_loop(0, 4, one, 0)

    project(z)
    lax.fori_loop(0, TENSOR, find, 0)
    r1 = spread_on(1, 3, s1)
    r2 = spread_on(2, 1, s2)
    for shift in (2, 6, 3, 7, 4, 5):
        key_first[shift].wait_recv()
        keys_second(shift)
    r3 = spread_on(3, 2, s3)
    project(z_up)
    project(z_down)
    for step in (1, 3, 2):
        value_first[step].wait_recv()
        values_second(step)
    for copies in (r0, r1, r2, r3):
        for copy in copies:
            copy.wait_recv()
    project(z_far)
    mean = jnp.sum(squares[...], axis=1, keepdims=True) * (1.0 / WIDTH)
    factor = lax.rsqrt(mean + EPSILON)
    bias = jnp.concatenate(
        [ref[...].astype(F32).reshape(1, HD // 2) for ref in (b_key, b_value)], axis=1
    )
    kv_own[...] = (acc_kv[...] * factor + bias).astype(BF16)
    kv_copy = remote(
        kv_own,
        kv_other,
        pair_send.at[0],
        pair_recv.at[0],
        group,
        x * 4 + partner_z[1],
    )
    kv_copy.start()

    def rotate(values):
        return values * cosine + pltpu.roll(values, HD // 2, 1) * sine

    for head in range(HEADS):
        columns = slice(head * HD, (head + 1) * HD)
        values = acc_q[:, columns] * factor + query_bias[:, columns]
        values = rotate(values).astype(BF16)
        for i in range(CONVS):
            query_own[i, head * SUF : (head + 1) * SUF, :] = values[i * SUF : (i + 1) * SUF, :]
    query_out = [
        remote(
            query_own,
            queries.at[r],
            pair_send.at[r],
            pair_recv.at[r],
            group,
            x * 4 + partner_z[r],
        )
        for r in (1, 2, 3)
    ]
    for copy in query_out:
        copy.start()
    query_keep = pltpu.make_async_copy(query_own, queries.at[0], load_sem.at[4])
    query_keep.start()

    kv_copy.wait_recv()
    mine = kv_own[...].astype(F32)
    theirs = kv_other[...].astype(F32)
    even = jnp.where(parity == 0, mine, theirs)
    odd = jnp.where(parity == 0, theirs, mine)
    low = lane_iota((ROWS, HD)) < HD // 2
    keys = jnp.where(low, even, pltpu.roll(odd, HD // 2, 1))
    keys = rotate(keys)
    values = jnp.where(low, pltpu.roll(even, HD // 2, 1), odd)
    key_new[...] = keys.astype(BF16)
    value_new[...] = values.astype(BF16)

    page = jnp.where(parity == 0, keys.astype(BF16).astype(F32), values)
    live_row = jnp.concatenate([offsets < suffix[i] for i in range(CONVS)], axis=0)
    page = jnp.where(live_row, page, 0.0).astype(BF16)
    new_all[pl.ds(group * CONVS, CONVS)] = page.reshape(CONVS, SUF, HD)
    new_ref = new_all.at[pl.ds(group * CONVS, CONVS)]
    group_out = [
        remote(
            new_ref,
            new_ref,
            group_send.at[shift],
            group_recv.at[shift],
            group_at(shift),
            tensor,
        )
        for shift in range(1, GROUPS)
    ]
    for copy in group_out:
        copy.start()
    for copy in group_out:
        copy.wait_recv()

    def choose(to, carry):
        page = new_all[chosen[0, to]].astype(F32)
        new_send[to] = (page * chosen[1, to].astype(F32)).astype(BF16)
        return carry

    lax.fori_loop(0, TENSOR, choose, 0)
    mine_copy = pltpu.make_async_copy(
        new_send.at[tensor], new_pages.at[tensor], load_sem.at[5]
    )
    mine_copy.start()

    def page_copy(off):
        to = lax.rem(tensor + off, TENSOR)
        return remote(
            new_send.at[to],
            new_pages.at[tensor],
            page_send.at[off],
            page_recv.at[off],
            group,
            to,
        )

    def page_start(off, carry):
        page_copy(off).start()
        return carry

    lax.fori_loop(1, TENSOR, page_start, 0)

    mine_copy.wait()
    query_keep.wait()
    kv_copy.wait_send()
    for copy in query_out:
        copy.wait()
    for copy in sent + pages_out + group_out:
        copy.wait_send()

    def page_end(off, carry):
        page_copy(off).wait()
        return carry

    lax.fori_loop(1, TENSOR, page_end, 0)
    for copy in kept:
        copy.wait()
    for copy in keys_last:
        copy.wait_recv()


def attend_kernel(
    lists,
    conv_ref,
    suffix_ref,
    key_new,
    value_new,
    queries_hbm,
    got_k_hbm,
    got_v_hbm,
    w_out,
    out_ref,
    queries,
    got_k,
    got_v,
    weights,
    accums,
    stats,
    own_accum,
    own_stats,
    mixed_out,
    lse_out,
    mixed_got,
    lse_got,
    mixed,
    part,
    big,
    small,
    load_sem,
    mixed_send,
    mixed_recv,
    lse_send,
    lse_recv,
    ring_send,
    ring_recv,
):
    group, tensor, y, core, x, z = place()
    partner_z = [z, z + 1 - 2 * lax.rem(z, 2), lax.rem(z + 2, 4), 3 - z]
    load_query = pltpu.make_async_copy(queries_hbm, queries, load_sem.at[0])
    load_k = pltpu.make_async_copy(got_k_hbm, got_k, load_sem.at[1])
    load_v = pltpu.make_async_copy(got_v_hbm, got_v, load_sem.at[2])
    load = pltpu.make_async_copy(w_out, weights, load_sem.at[3])
    for copy in (load_query, load_k, load_v):
        copy.start()
    x_up, x_far, x_down = (lax.rem(x + shift, 4) for shift in (1, 2, 3))
    z_up, z_far, z_down = (lax.rem(z + shift, 4) for shift in (1, 2, 3))
    to_x_up, to_x_down = x_up * 4 + z, x_down * 4 + z
    to_z_up, to_z_down = x * 4 + z_up, x * 4 + z_down
    barrier = pltpu.get_barrier_semaphore()
    for to in (to_x_up, to_x_down, to_z_up, to_z_down, x * 4 + z_far):
        pl.semaphore_signal(barrier, inc=1, device_id=(group, to), device_id_type=MESH)

    half = HEADS * SUF
    own_head = lax.div(z, 2)

    def score(keys, query):
        return lax.dot_general(
            keys, query, (((1,), (1,)), ((), ())), preferred_element_type=F32
        )

    def mix(values, shares):
        return lax.dot_general(
            values,
            shares.astype(BF16),
            (((0,), (0,)), ((), ())),
            preferred_element_type=F32,
        )

    causal = row_iota((SUF, half)) <= (lane_iota((SUF, half)) & (SUF - 1))
    load_query.wait()
    for i in range(CONVS):
        rows = slice(i * SUF, (i + 1) * SUF)
        scores = score(key_new[rows], queries[0, i])
        scores = jnp.where(causal, scores * SCALE, NEGATIVE)
        peak = jnp.max(scores, axis=0, keepdims=True)
        shares = jnp.exp2(scores - peak)
        own_accum[i] = mix(value_new[rows], shares)
        own_stats[i, 0:1, :] = peak
        own_stats[i, 1:2, :] = jnp.sum(shares, axis=0, keepdims=True)
    load_k.wait()
    load_v.wait()
    load.start()

    token = row_iota((PAGE, half))

    def attend(head, sides):
        def pack(index, state):
            blocks = [index * PACK + k for k in range(PACK)]
            codes = [[lists[b * STEP + p, 0] for p in range(STEP)] for b in blocks]
            convs = [lists[b, 1] for b in blocks]
            firsts = [lists[b, 2] == 1 for b in blocks]
            keys = [
                jnp.concatenate([got_k[code >> 7, head] for code in row], axis=0)
                for row in codes
            ]
            values = [
                jnp.concatenate([got_v[code >> 7, head] for code in row], axis=0)
                for row in codes
            ]
            pairs = [(k, s) for k in range(PACK) for s in range(len(sides))]
            scores = {
                (k, s): score(keys[k], queries[sides[s], convs[k]]) for k, s in pairs
            }
            for k, s in pairs:
                scores[k, s] = jnp.concatenate(
                    [
                        jnp.where(
                            token < (codes[k][p] & 127),
                            scores[k, s][p * PAGE : (p + 1) * PAGE] * SCALE,
                            NEGATIVE,
                        )
                        for p in range(STEP)
                    ],
                    axis=0,
                )
            tops = {
                key: jnp.max(value, axis=0, keepdims=True) for key, value in scores.items()
            }
            state = list(state)
            fresh, shrink = {}, {}
            for s in range(len(sides)):
                peak = state[s][0]
                for k in range(PACK):
                    peak = jnp.where(firsts[k], NEGATIVE, peak)
                    fresh[k, s] = jnp.maximum(peak, tops[k, s])
                    shrink[k, s] = jnp.exp2(peak - fresh[k, s])
                    peak = fresh[k, s]
            shares = {key: jnp.exp2(scores[key] - fresh[key]) for key in pairs}
            sums = {key: jnp.sum(shares[key], axis=0, keepdims=True) for key in pairs}
            mixes = {(k, s): mix(values[k], shares[k, s]) for k, s in pairs}
            for s, side in enumerate(sides):
                peak, total, accum = state[s]
                for k in range(PACK):
                    total = total * shrink[k, s] + sums[k, s]
                    accum = accum * shrink[k, s] + mixes[k, s]
                    accums[side, blocks[k]] = accum
                    stats[side, blocks[k], 0:1, :] = fresh[k, s]
                    stats[side, blocks[k], 1:2, :] = total
                state[s] = (fresh[PACK - 1, s], total, accum)
            return tuple(state)

        empty = (
            jnp.full((1, half), NEGATIVE, F32),
            jnp.zeros((1, half), F32),
            jnp.zeros((HD, half), F32),
        )
        lax.fori_loop(0, BLOCKS // PACK, pack, tuple(empty for _ in sides))

    def result(side, i):
        last = lists[i, 3]
        some = lists[i, 4] == 1
        peak = jnp.where(some, stats[side, last, 0:1, :], NEGATIVE)
        total = jnp.where(some, stats[side, last, 1:2, :], 0.0)
        accum = accums[side, last] * jnp.where(some, 1.0, 0.0)
        return peak, total, accum

    def send(side):
        for i in range(CONVS):
            peak, total, accum = result(side, i)
            safe = jnp.where(total > 0.0, total, 1.0)
            mixed_out[side, i] = (accum * (1.0 / safe)).astype(BF16)
            lse = jnp.where(total > 0.0, peak + jnp.log(safe) * (1.0 / LN2), NEGATIVE)
            lse_out[side, i] = jnp.broadcast_to(lse, (8, half))
        copies = [
            remote(
                source.at[side],
                target.at[side],
                send_sem.at[side],
                recv_sem.at[side],
                group,
                x * 4 + partner_z[side],
            )
            for source, target, send_sem, recv_sem in (
                (mixed_out, mixed_got, mixed_send, mixed_recv),
                (lse_out, lse_got, lse_send, lse_recv),
            )
        ]
        for copy in copies:
            copy.start()
        return copies

    attend(1 - own_head, (2, 3))
    pl.semaphore_wait(barrier, 5)
    exchanged = send(2) + send(3)
    attend(own_head, (1, 0))
    exchanged = exchanged + send(1)
    for copy in exchanged:
        copy.wait_recv()
    row_of = lane_iota((1, half)) & (SUF - 1)

    def combine(i):
        peak, total, accum = result(0, i)
        own_peak = own_stats[i, 0:1, :]
        logs = [lse_got[r, i, 0:1, :] for r in (1, 2, 3)]
        top = jnp.maximum(
            jnp.maximum(peak, own_peak), jnp.maximum(jnp.maximum(logs[0], logs[1]), logs[2])
        )
        shares = [jnp.exp2(log - top) for log in logs]
        first, second = jnp.exp2(peak - top), jnp.exp2(own_peak - top)
        total = total * first + own_stats[i, 1:2, :] * second
        total = total + shares[0] + shares[1] + shares[2]
        scale = jnp.where(row_of < suffix_ref[conv_ref[group * CONVS + i]], 1.0, 0.0) / total
        joined = accum * (first * scale) + own_accum[i] * (second * scale)
        for r in (1, 2, 3):
            joined = joined + mixed_got[r, i].astype(F32) * (shares[r - 1] * scale)
        turned = jnp.transpose(joined).astype(BF16)
        for head in range(HEADS):
            mixed[i * SUF : (i + 1) * SUF, head * HD : (head + 1) * HD] = turned[
                head * SUF : (head + 1) * SUF, :
            ]

    pending = []

    class Ring:
        def __init__(self, side, first, pick, buffers, way):
            self.side, self.first, self.pick, self.buffers = side, first, pick, buffers
            self.up, self.down, self.me, self.far, self.to_up, self.to_down = way
            self.top = pl.ds(side * 2 * SUF, SUF)
            self.bottom = pl.ds(side * 2 * SUF + SUF, SUF)

        def send(self, index, ref, to):
            sem = self.first + index
            copy = remote(
                ref,
                self.buffers.at[self.side, index],
                ring_send.at[sem],
                ring_recv.at[sem],
                group,
                to,
            )
            copy.start()
            pending.append(copy)
            return copy

        def start_far(self):
            pick = self.pick
            self.c0 = self.send(0, pick(self.far, self.top), self.to_up)
            self.c1 = self.send(1, pick(self.far, self.bottom), self.to_down)

        def start_near(self):
            pick = self.pick
            self.c2 = self.send(2, pick(self.up, self.bottom), self.to_up)
            self.c3 = self.send(3, pick(self.down, self.top), self.to_down)

        def add(self, ref, *indices):
            total = ref[...].astype(F32)
            for index in indices:
                total = total + self.buffers[self.side, index].astype(F32)
            ref[...] = total.astype(BF16)

        def relay(self):
            pick = self.pick
            self.c0.wait_recv()
            self.add(pick(self.up, self.top), 0)
            self.c4 = self.send(4, pick(self.up, self.top), self.to_up)
            self.c1.wait_recv()
            self.add(pick(self.down, self.bottom), 1)
            self.c5 = self.send(5, pick(self.down, self.bottom), self.to_down)

        def finish(self):
            pick = self.pick
            self.c3.wait_recv()
            self.c4.wait_recv()
            self.add(pick(self.me, self.top), 3, 4)
            self.c2.wait_recv()
            self.c5.wait_recv()
            self.add(pick(self.me, self.bottom), 2, 5)

    along_x = (x_up, x_down, x, x_far, to_x_up, to_x_down)
    along_z = (z_up, z_down, z, z_far, to_z_up, to_z_down)
    firsts = (
        Ring(0, 0, lambda j, rows: part.at[j, :, rows], big, along_x),
        Ring(1, 6, lambda j, rows: part.at[:, j, rows], big, along_z),
    )
    seconds = (
        Ring(0, 12, lambda j, rows: part.at[x, j, rows], small, along_z),
        Ring(1, 18, lambda j, rows: part.at[j, z, rows], small, along_x),
    )

    def project(bx, bz):
        columns = pl.ds(pl.multiple_of((bx * 4 + bz) * PART, PART), PART)
        part[bx, bz] = jnp.dot(
            mixed[...], weights[:, columns], preferred_element_type=F32
        ).astype(BF16)

    def project_many(pairs):
        for bx, bz in pairs:
            project(bx, bz)

    for i in range(CONVS):
        combine(i)
    load.wait()
    project_many([(x_far, bz) for bz in (z_far, z_up, z_down, z)])
    firsts[0].start_far()
    project_many([(bx, z_far) for bx in (x_up, x_down, x)])
    firsts[1].start_far()
    project_many([(x_up, z_up), (x_up, z_down), (x_up, z)])
    project_many([(x_down, z_up), (x_down, z_down), (x_down, z)])
    firsts[0].start_near()
    project_many([(x, z_up), (x, z_down), (x, z)])
    firsts[1].start_near()
    firsts[0].relay()
    firsts[1].relay()
    for first, second in zip(firsts, seconds):
        first.finish()
        second.start_far()
        second.start_near()
    seconds[0].relay()
    seconds[1].relay()
    seconds[0].finish()
    seconds[1].finish()
    out_ref[...] = part[x, z]
    for copy in exchanged + pending:
        copy.wait_send()


def any_spec():
    return pl.BlockSpec(memory_space=pl.ANY)


def vmem_spec():
    return pl.BlockSpec(memory_space=pltpu.VMEM)


def smem_spec():
    return pl.BlockSpec(memory_space=pltpu.SMEM)


def shards(
    hidden_states,
    norm_gain,
    w_query,
    b_query,
    w_key,
    b_key,
    w_value,
    b_value,
    w_out,
    pool_keys,
    pool_values,
    conv_slots,
    page_table,
    prefix_len,
    suffix_len,
    new_dest,
):
    dma = pltpu.SemaphoreType.DMA
    freq = THETA ** (-(np.arange(HD // 2, dtype=np.float64) * 2.0 / HD))
    freq = jnp.asarray(np.concatenate([freq, freq])[None, :], F32)
    shape = jax.ShapeDtypeStruct
    got_k, got_v, queries, key_new, value_new, lists, new_pages = pl.pallas_call(
        gather_kernel,
        out_shape=[
            shape((4, GROUPS, 2, 2, PAGE, HD), BF16),
            shape((4, GROUPS, 2, 2, PAGE, HD), BF16),
            shape((4, CONVS, HEADS * SUF, HD), BF16),
            shape((ROWS, HD), BF16),
            shape((ROWS, HD), BF16),
            shape((LIST, HD), I32),
            shape((TENSOR, SUF, HD), BF16),
        ],
        in_specs=[smem_spec()] * 4
        + [vmem_spec()]
        + [any_spec()] * 6
        + [vmem_spec()] * 5,
        out_specs=[any_spec()] * 3 + [vmem_spec()] * 3 + [any_spec()],
        scratch_shapes=[
            pltpu.VMEM((4, 4, ROWS, PART), BF16),
            pltpu.VMEM((WIDTH, HEADS * HD), BF16),
            pltpu.VMEM((HD, WIDTH), BF16),
            pltpu.VMEM((ROWS, HEADS * HD), F32),
            pltpu.VMEM((ROWS, HD), F32),
            pltpu.VMEM((ROWS, HD), F32),
            pltpu.VMEM((GROUPS, 2, 8, PAGE, HD), BF16),
            pltpu.VMEM((4, 2 * GROUPS, 2, PAGE, HD), BF16),
            pltpu.VMEM((CONVS, HEADS * SUF, HD), BF16),
            pltpu.VMEM((ROWS, HD), BF16),
            pltpu.VMEM((ROWS, HD), BF16),
            pltpu.VMEM((GROUPS * CONVS, SUF, HD), BF16),
            pltpu.VMEM((TENSOR, SUF, HD), BF16),
            pltpu.SMEM((2, TENSOR), I32),
            pltpu.VMEM((1, WIDTH), F32),
            dma((8,)),
            dma((2, GROUPS)),
            dma((20,)),
            dma((20,)),
            dma((2, GROUPS)),
            dma((2, GROUPS)),
            dma((2, GROUPS, 4)),
            dma((2, GROUPS, 4)),
            dma((4,)),
            dma((4,)),
            dma((4,)),
            dma((4,)),
            dma((GROUPS,)),
            dma((GROUPS,)),
            dma((TENSOR,)),
            dma((TENSOR,)),
        ],
        compiler_params=pltpu.CompilerParams(
            collective_id=0, has_side_effects=True, vmem_limit_bytes=60 * 1024 * 1024
        ),
        name="gather",
    )(
        conv_slots,
        prefix_len,
        suffix_len,
        new_dest,
        page_table,
        hidden_states,
        pool_keys,
        pool_values,
        w_query,
        w_key.T,
        w_value.T,
        norm_gain,
        b_query,
        b_key,
        b_value,
        freq,
    )
    attn_out = pl.pallas_call(
        attend_kernel,
        out_shape=shape((ROWS, PART), BF16),
        in_specs=[smem_spec()] * 3 + [vmem_spec()] * 2 + [any_spec()] * 4,
        out_specs=vmem_spec(),
        scratch_shapes=[
            pltpu.VMEM((4, CONVS, HEADS * SUF, HD), BF16),
            pltpu.VMEM((PAGES, 2, PAGE, HD), BF16),
            pltpu.VMEM((PAGES, 2, PAGE, HD), BF16),
            pltpu.VMEM((HEADS * HD, WIDTH), BF16),
            pltpu.VMEM((4, BLOCKS, HD, HEADS * SUF), F32),
            pltpu.VMEM((4, BLOCKS, 8, HEADS * SUF), F32),
            pltpu.VMEM((CONVS, HD, HEADS * SUF), F32),
            pltpu.VMEM((CONVS, 8, HEADS * SUF), F32),
            pltpu.VMEM((4, CONVS, HD, HEADS * SUF), BF16),
            pltpu.VMEM((4, CONVS, 8, HEADS * SUF), F32),
            pltpu.VMEM((4, CONVS, HD, HEADS * SUF), BF16),
            pltpu.VMEM((4, CONVS, 8, HEADS * SUF), F32),
            pltpu.VMEM((ROWS, HEADS * HD), BF16),
            pltpu.VMEM((4, 4, ROWS, PART), BF16),
            pltpu.VMEM((2, 6, 4, SUF, PART), BF16),
            pltpu.VMEM((2, 6, SUF, PART), BF16),
            dma((4,)),
            dma((4,)),
            dma((4,)),
            dma((4,)),
            dma((4,)),
            dma((24,)),
            dma((24,)),
        ],
        compiler_params=pltpu.CompilerParams(
            collective_id=1, has_side_effects=True, vmem_limit_bytes=60 * 1024 * 1024
        ),
        name="attend",
    )(
        lists,
        conv_slots,
        suffix_len,
        key_new,
        value_new,
        queries,
        got_k.reshape(PAGES, 2, PAGE, HD),
        got_v.reshape(PAGES, 2, PAGE, HD),
        w_out,
    )
    pages = new_pages.reshape(TENSOR // 2, 2, SUF, HD)
    return (attn_out, pages[None, :, 0], pages[None, :, 1])


def solution(mesh):
    in_specs = (
        P("group", "tensor"),
        P(),
        P(None, "tensor"),
        P("tensor"),
        P(None, "tensor"),
        P("tensor"),
        P(None, "tensor"),
        P("tensor"),
        P("tensor", None),
        P(("group", "tensor"), None, None, None),
        P(("group", "tensor"), None, None, None),
        P(),
        P(),
        P(),
        P(),
        P(),
    )
    out_specs = (
        P("group", "tensor"),
        P(("group", "tensor"), None, None, None),
        P(("group", "tensor"), None, None, None),
    )
    return jax.shard_map(shards, mesh=mesh, in_specs=in_specs, out_specs=out_specs, check_vma=False)
```

```python
import jax
import jax.numpy as jnp
import numpy as np
from jax import lax
from jax.experimental import pallas as pl
from jax.experimental.pallas import tpu as pltpu
from jax.sharding import PartitionSpec as P

HD = 128
SUF = 64
CONVS = 4
ROWS = CONVS * SUF
GROUPS = 8
TENSOR = 16
WIDTH = 8192
PART = WIDTH // TENSOR
PAGES = 64
PAGE = 64
HEADS = 4
THETA = 1000000.0
EPSILON = 1e-06
NEGATIVE = -1e30
SCALE = HD**-0.5 * 1.4426950408889634
STEP = 4
BLOCKS = 20
LIST = 80
LN2 = 0.6931471805599453
MESH = pl.DeviceIdType.MESH
BF16 = jnp.bfloat16
F32 = jnp.float32
I32 = jnp.int32


def remote(src, dst, send_sem, recv_sem, group, tensor):
    return pltpu.make_async_remote_copy(
        src_ref=src,
        dst_ref=dst,
        send_sem=send_sem,
        recv_sem=recv_sem,
        device_id=(group, tensor),
        device_id_type=MESH,
    )


def place():
    group = lax.axis_index("group")
    tensor = lax.axis_index("tensor")
    return (
        group,
        tensor,
        lax.div(group, 2),
        lax.rem(group, 2),
        lax.div(tensor, 4),
        lax.rem(tensor, 4),
    )


def lane_iota(shape):
    return lax.broadcasted_iota(I32, shape, len(shape) - 1)


def row_iota(shape):
    return lax.broadcasted_iota(I32, shape, len(shape) - 2)


def layer_kernel(
    conv_ref,
    prefix_ref,
    suffix_ref,
    dest_ref,
    table_ref,
    hidden,
    pool_k,
    pool_v,
    w_query,
    w_key,
    w_value,
    w_out,
    gain_ref,
    b_query,
    b_key,
    b_value,
    freq_ref,
    out_ref,
    new_pages,
    feat,
    wq,
    wkv,
    acc_q,
    acc_kv,
    squares,
    stage_k,
    stage_v,
    got_k,
    got_v,
    queries,
    key_new,
    value_new,
    kv_own,
    kv_other,
    new_all,
    table_out,
    lists,
    chosen,
    gain,
    weights,
    accums,
    stats,
    own_accum,
    own_stats,
    mixed_out,
    lse_out,
    mixed_got,
    lse_got,
    mixed,
    part,
    big,
    small,
    new_send,
    load_sem,
    keep_sem,
    feat_send,
    feat_recv,
    y_send,
    y_recv,
    x_send,
    x_recv,
    v_send,
    v_recv,
    pair_send,
    pair_recv,
    group_send,
    group_recv,
    mixed_send,
    mixed_recv,
    lse_send,
    lse_recv,
    ring_send,
    ring_recv,
    page_send,
    page_recv,
):
    group, tensor, y, core, x, z = place()
    parity = lax.rem(z, 2)
    partner_z = [z, z + 1 - 2 * parity, lax.rem(z + 2, 4), 3 - z]
    own = pltpu.make_async_copy(hidden, feat.at[x, z], load_sem.at[0])
    own.start()
    loads = [
        pltpu.make_async_copy(w_query, wq, load_sem.at[1]),
        pltpu.make_async_copy(w_key, wkv.at[pl.ds(0, HD // 2)], load_sem.at[2]),
        pltpu.make_async_copy(w_value, wkv.at[pl.ds(HD // 2, HD // 2)], load_sem.at[3]),
    ]
    for load in loads:
        load.start()

    def group_at(shift):
        to_y = lax.rem(y + shift // 2, 4)
        to_core = lax.rem(core + shift % 2, 2)
        return to_y * 2 + to_core

    barrier = pltpu.get_barrier_semaphore()
    for shift in range(1, GROUPS):
        pl.semaphore_signal(
            barrier, inc=1, device_id=(group_at(shift), tensor), device_id_type=MESH
        )

    def greet(off, carry):
        to = lax.rem(tensor + off, TENSOR)
        pl.semaphore_signal(barrier, inc=1, device_id=(group, to), device_id_type=MESH)
        return carry

    lax.fori_loop(1, TENSOR, greet, 0)
    pl.semaphore_wait(barrier, GROUPS - 1 + TENSOR - 1)

    own.wait()
    x_at = [lax.rem(x + shift, 4) for shift in range(4)]
    x_up, x_far, x_down = x_at[1:]
    z_up, z_far, z_down = (lax.rem(z + shift, 4) for shift in (1, 2, 3))
    to_x_up, to_x_down = x_at[1] * 4 + z, x_at[3] * 4 + z
    to_z_up, to_z_down = x * 4 + z_up, x * 4 + z_down
    half_rows = ROWS // 2
    low_rows, high_rows = pl.ds(0, half_rows), pl.ds(half_rows, half_rows)
    sent, kept = [], []

    def pass_on(index, ref, to):
        copy = remote(ref, ref, feat_send.at[index], feat_recv.at[index], group, to)
        copy.start()
        sent.append(copy)
        return copy

    def spread(block, shift):
        ref = feat.at[x_at[shift], z]
        return (
            pass_on(4 + 4 * block, ref, to_z_up),
            pass_on(5 + 4 * block, ref, to_z_down),
        )

    def spread_on(block, shift, copies):
        copies[0].wait_recv()
        first = pass_on(6 + 4 * block, feat.at[x_at[shift], z_down, low_rows], to_z_up)
        copies[1].wait_recv()
        second = pass_on(7 + 4 * block, feat.at[x_at[shift], z_up, high_rows], to_z_down)
        return first, second

    pages_out = []

    def push(source, target, send_sem, recv_sem, to_group, to):
        copy = remote(source, target, send_sem, recv_sem, to_group, to)
        copy.start()
        pages_out.append(copy)
        return copy

    def keep(source, target, sem):
        copy = pltpu.make_async_copy(source, target, sem)
        copy.start()
        kept.append(copy)

    def slots(shift):
        return pl.ds(2 * group_at(shift), 2)

    def heads(step):
        return pl.ds(2 * x_at[step], 2)

    def keys_first(shift):
        return push(
            pool_k.at[slots(shift)],
            stage_k.at[shift],
            y_send.at[0, shift],
            y_recv.at[0, shift],
            group_at(shift),
            tensor,
        )

    def keys_second(shift):
        for step in (1, 3, 2, 0):
            if shift == 0:
                source = pool_k.at[slots(0), heads(step)]
            else:
                source = stage_k.at[shift, :, heads(step)]
            target = got_k.at[pl.ds(2 * (step * GROUPS + shift), 2)]
            if step == 0:
                keep(source, target, keep_sem.at[0, shift])
            else:
                keys_last.append(
                    push(
                        source,
                        target,
                        x_send.at[0, shift, step],
                        x_recv.at[0, shift, step],
                        group,
                        x_at[step] * 4 + z,
                    )
                )

    def values_first(step):
        return push(
            pool_v.at[:, heads(step)],
            stage_v.at[step],
            v_send.at[step],
            v_recv.at[step],
            group,
            x_at[step] * 4 + z,
        )

    def values_second(step):
        for shift in (1, 2, 6, 3, 7, 4, 5, 0):
            if step == 0:
                source = pool_v.at[slots(shift), heads(0)]
            else:
                source = stage_v.at[step, slots(shift)]
            target = got_v.at[pl.ds(2 * (step * GROUPS + shift), 2)]
            if shift == 0:
                keep(source, target, keep_sem.at[1, step])
            else:
                keys_last.append(
                    push(
                        source,
                        target,
                        x_send.at[1, shift, step],
                        x_recv.at[1, shift, step],
                        group_at(shift),
                        tensor,
                    )
                )

    keys_last = []
    f0 = pass_on(0, feat.at[x, z], to_x_up)
    f1 = pass_on(1, feat.at[x, z], to_x_down)
    s0 = spread(0, 0)
    key_first = {shift: keys_first(shift) for shift in (1, 2, 6, 3, 7, 4, 5)}
    f0.wait_recv()
    f2 = pass_on(2, feat.at[x_at[3], z, low_rows], to_x_up)
    s1 = spread(1, 3)
    f1.wait_recv()
    f3 = pass_on(3, feat.at[x_at[1], z, high_rows], to_x_down)
    s2 = spread(2, 1)
    prefix = [prefix_ref[conv_ref[group * CONVS + i]] for i in range(CONVS)]
    suffix = [suffix_ref[conv_ref[group * CONVS + i]] for i in range(CONVS)]

    offsets = row_iota((SUF, HD))
    positions = jnp.concatenate([offsets + prefix[i] for i in range(CONVS)], axis=0)
    angle = positions.astype(F32) * freq_ref[...]
    cosine = jnp.cos(angle)
    sine = jnp.sin(angle)
    sine = jnp.where(lane_iota((ROWS, HD)) < HD // 2, -sine, sine)

    f2.wait_recv()
    f3.wait_recv()
    s3 = spread(3, 2)
    value_first = {step: values_first(step) for step in (1, 3, 2)}
    keys_second(0)
    values_second(0)
    key_first[1].wait_recv()
    keys_second(1)
    r0 = spread_on(0, 0, s0)

    page_ids = lane_iota((1, PAGES))
    below = (row_iota((PAGES, PAGES)) < lane_iota((PAGES, PAGES))).astype(F32)
    lane = lane_iota((LIST, HD))
    place_id = row_iota((LIST, PAGES)).astype(F32)
    row_id = row_iota((LIST, 1)).astype(F32)
    codes = jnp.zeros((LIST, 1), F32)
    block_conv = jnp.zeros((LIST, 1), F32)
    block_first = jnp.zeros((LIST, 1), F32)
    last_block = jnp.zeros((LIST, 1), F32)
    has_block = jnp.zeros((LIST, 1), F32)
    begin = jnp.zeros((1, 1), F32)
    for i in range(CONVS):
        entry = table_ref[pl.ds(conv_ref[group * CONVS + i], 1), :]
        source = entry >> 4
        source_y, source_core = source >> 5, (source >> 4) & 1
        source_x, source_z = (source >> 2) & 3, source & 3
        live = jnp.clip(prefix[i] - page_ids * PAGE, 0, PAGE)
        here = (source_z == z) & (live > 0)
        where = ((x - source_x) & 3) * GROUPS
        where = where + ((y - source_y) & 3) * 2 + ((core - source_core) & 1)
        value = ((where * 2 + (entry & 1)) * 128 + live).astype(F32)
        here_f = here.astype(F32)
        order = jnp.dot(
            jnp.broadcast_to(here_f, (8, PAGES)), below, preferred_element_type=F32
        )[0:1, :]
        count = jnp.sum(here_f, axis=1, keepdims=True)
        blocks = jnp.floor((count + (STEP - 1)) * (1.0 / STEP))
        match = (order + begin * STEP == place_id) & (
            jnp.broadcast_to(here_f, (LIST, PAGES)) > 0.5
        )
        codes = codes + jnp.sum(jnp.where(match, value, 0.0), axis=1, keepdims=True)
        block_first = jnp.where(row_id == begin, 1.0, block_first)
        begin = begin + blocks
        if i < CONVS - 1:
            block_conv = block_conv + jnp.where(row_id >= begin, 1.0, 0.0)
        last_block = jnp.where(row_id == i, jnp.maximum(begin - 1.0, 0.0), last_block)
        has_block = jnp.where(row_id == i, jnp.minimum(count, 1.0), has_block)
    table = jnp.zeros((LIST, HD), F32)
    for column, data in enumerate((codes, block_conv, block_first, last_block, has_block)):
        table = jnp.where(lane == column, data, table)
    table_out[...] = table.astype(I32)
    list_copy = pltpu.make_async_copy(table_out, lists, load_sem.at[4])
    list_copy.start()

    def find(to, carry):
        target = group * TENSOR + to
        index = jnp.int32(0)
        found = jnp.int32(0)
        for slot in range(GROUPS * CONVS):
            hit = dest_ref[conv_ref[slot]] == target
            index = jnp.where(hit, slot, index)
            found = jnp.where(hit, 1, found)
        chosen[0, to] = index
        chosen[1, to] = found
        return carry

    for load in loads:
        load.wait()
    load_out = pltpu.make_async_copy(w_out, weights, load_sem.at[5])
    load_out.start()
    gain[...] = gain_ref[...].astype(F32).reshape(1, WIDTH)
    query_bias = b_query[...].astype(F32).reshape(1, HEADS * HD)
    acc_q[...] = jnp.zeros_like(acc_q)
    acc_kv[...] = jnp.zeros_like(acc_kv)
    squares[...] = jnp.zeros_like(squares)

    def project(bz):
        def one(bx, carry):
            block = bx * 4 + bz
            rows = pl.ds(pl.multiple_of(block * PART, PART), PART)
            wide = feat[bx, bz].astype(F32)
            scaled = (wide * gain[:, rows]).astype(BF16)
            acc_q[...] += jnp.dot(scaled, wq[rows, :], preferred_element_type=F32)
            acc_kv[...] += lax.dot_general(
                scaled,
                wkv[:, rows],
                (((1,), (1,)), ((), ())),
                preferred_element_type=F32,
            )
            wide = wide * wide
            total = squares[...]
            for part in range(PART // HD):
                total = total + wide[:, part * HD : (part + 1) * HD]
            squares[...] = total
            return carry

        lax.fori_loop(0, 4, one, 0)

    project(z)
    lax.fori_loop(0, TENSOR, find, 0)
    r1 = spread_on(1, 3, s1)
    r2 = spread_on(2, 1, s2)
    for shift in (2, 6, 3, 7, 4, 5):
        key_first[shift].wait_recv()
        keys_second(shift)
    r3 = spread_on(3, 2, s3)
    project(z_up)
    project(z_down)
    for step in (1, 3, 2):
        value_first[step].wait_recv()
        values_second(step)
    for copies in (r0, r1, r2, r3):
        for copy in copies:
            copy.wait_recv()
    project(z_far)
    mean = jnp.sum(squares[...], axis=1, keepdims=True) * (1.0 / WIDTH)
    factor = lax.rsqrt(mean + EPSILON)
    bias = jnp.concatenate(
        [ref[...].astype(F32).reshape(1, HD // 2) for ref in (b_key, b_value)], axis=1
    )
    kv_own[...] = (acc_kv[...] * factor + bias).astype(BF16)
    kv_copy = remote(
        kv_own,
        kv_other,
        pair_send.at[0],
        pair_recv.at[0],
        group,
        x * 4 + partner_z[1],
    )
    kv_copy.start()

    def rotate(values):
        return values * cosine + pltpu.roll(values, HD // 2, 1) * sine

    for head in range(HEADS):
        columns = slice(head * HD, (head + 1) * HD)
        values = acc_q[:, columns] * factor + query_bias[:, columns]
        values = rotate(values).astype(BF16)
        for i in range(CONVS):
            queries[0, i, head * SUF : (head + 1) * SUF, :] = values[i * SUF : (i + 1) * SUF, :]
    query_out = [
        remote(
            queries.at[0],
            queries.at[r],
            pair_send.at[r],
            pair_recv.at[r],
            group,
            x * 4 + partner_z[r],
        )
        for r in (1, 2, 3)
    ]
    for copy in query_out:
        copy.start()

    kv_copy.wait_recv()
    mine = kv_own[...].astype(F32)
    theirs = kv_other[...].astype(F32)
    even = jnp.where(parity == 0, mine, theirs)
    odd = jnp.where(parity == 0, theirs, mine)
    low = lane_iota((ROWS, HD)) < HD // 2
    keys = jnp.where(low, even, pltpu.roll(odd, HD // 2, 1))
    keys = rotate(keys)
    values = jnp.where(low, pltpu.roll(even, HD // 2, 1), odd)
    key_new[...] = keys.astype(BF16)
    value_new[...] = values.astype(BF16)

    page = jnp.where(parity == 0, keys.astype(BF16).astype(F32), values)
    live_row = jnp.concatenate([offsets < suffix[i] for i in range(CONVS)], axis=0)
    page = jnp.where(live_row, page, 0.0).astype(BF16)
    new_ref = new_all.at[pl.ds(group * CONVS, CONVS)]
    new_ref[...] = page.reshape(CONVS, SUF, HD)
    group_out = [
        remote(
            new_ref,
            new_ref,
            group_send.at[shift],
            group_recv.at[shift],
            group_at(shift),
            tensor,
        )
        for shift in range(1, GROUPS)
    ]
    for copy in group_out:
        copy.start()

    half = HEADS * SUF
    own_head = lax.div(z, 2)

    def score(keys, query):
        return lax.dot_general(
            keys, query, (((1,), (1,)), ((), ())), preferred_element_type=F32
        )

    def mix(values, shares):
        return lax.dot_general(
            values,
            shares.astype(BF16),
            (((0,), (0,)), ((), ())),
            preferred_element_type=F32,
        )

    causal = row_iota((SUF, half)) <= (lane_iota((SUF, half)) & (SUF - 1))
    for i in range(CONVS):
        rows = slice(i * SUF, (i + 1) * SUF)
        scores = score(key_new[rows], queries[0, i])
        scores = jnp.where(causal, scores * SCALE, NEGATIVE)
        peak = jnp.max(scores, axis=0, keepdims=True)
        shares = jnp.exp2(scores - peak)
        own_accum[i] = mix(value_new[rows], shares)
        own_stats[i, 0:1, :] = peak
        own_stats[i, 1:2, :] = jnp.sum(shares, axis=0, keepdims=True)
    list_copy.wait()
    for copy in query_out + keys_last:
        copy.wait_recv()
    for copy in kept:
        copy.wait()

    token = row_iota((PAGE, half))

    def attend(head, sides, width):
        def pack(index, state):
            blocks = [index * width + k for k in range(width)]
            codes = [[lists[b * STEP + p, 0] for p in range(STEP)] for b in blocks]
            convs = [jnp.clip(lists[b, 1], 0, CONVS - 1) for b in blocks]
            spots = [[jnp.clip(code >> 7, 0, PAGES - 1) for code in row] for row in codes]
            firsts = [lists[b, 2] == 1 for b in blocks]
            keys = [
                jnp.concatenate([got_k[spot, head] for spot in row], axis=0)
                for row in spots
            ]
            values = [
                jnp.concatenate([got_v[spot, head] for spot in row], axis=0)
                for row in spots
            ]
            pairs = [(k, s) for k in range(width) for s in range(len(sides))]
            scores = {
                (k, s): score(keys[k], queries[sides[s], convs[k]]) for k, s in pairs
            }
            for k, s in pairs:
                scores[k, s] = jnp.concatenate(
                    [
                        jnp.where(
                            token < (codes[k][p] & 127),
                            scores[k, s][p * PAGE : (p + 1) * PAGE] * SCALE,
                            NEGATIVE,
                        )
                        for p in range(STEP)
                    ],
                    axis=0,
                )
            tops = {
                key: jnp.max(value, axis=0, keepdims=True) for key, value in scores.items()
            }
            state = list(state)
            fresh, shrink = {}, {}
            for s in range(len(sides)):
                peak = state[s][0]
                for k in range(width):
                    peak = jnp.where(firsts[k], NEGATIVE, peak)
                    fresh[k, s] = jnp.maximum(peak, tops[k, s])
                    shrink[k, s] = jnp.exp2(peak - fresh[k, s])
                    peak = fresh[k, s]
            shares = {key: jnp.exp2(scores[key] - fresh[key]) for key in pairs}
            sums = {key: jnp.sum(shares[key], axis=0, keepdims=True) for key in pairs}
            mixes = {(k, s): mix(values[k], shares[k, s]) for k, s in pairs}
            for s, side in enumerate(sides):
                peak, total, accum = state[s]
                for k in range(width):
                    total = total * shrink[k, s] + sums[k, s]
                    accum = accum * shrink[k, s] + mixes[k, s]
                    accums[side, blocks[k]] = accum
                    stats[side, blocks[k], 0:1, :] = fresh[k, s]
                    stats[side, blocks[k], 1:2, :] = total
                state[s] = (fresh[width - 1, s], total, accum)
            return tuple(state)

        empty = (
            jnp.full((1, half), NEGATIVE, F32),
            jnp.zeros((1, half), F32),
            jnp.zeros((HD, half), F32),
        )
        lax.fori_loop(0, BLOCKS // width, pack, tuple(empty for _ in sides))

    def result(side, i):
        last = jnp.clip(lists[i, 3], 0, BLOCKS - 1)
        some = lists[i, 4] == 1
        peak = jnp.where(some, stats[side, last, 0:1, :], NEGATIVE)
        total = jnp.where(some, stats[side, last, 1:2, :], 0.0)
        accum = accums[side, last] * jnp.where(some, 1.0, 0.0)
        return peak, total, accum

    def send(side):
        for i in range(CONVS):
            peak, total, accum = result(side, i)
            safe = jnp.where(total > 0.0, total, 1.0)
            mixed_out[side, i] = (accum * (1.0 / safe)).astype(BF16)
            lse = jnp.where(total > 0.0, peak + jnp.log(safe) * (1.0 / LN2), NEGATIVE)
            lse_out[side, i] = jnp.broadcast_to(lse, (8, half))
        copies = [
            remote(
                source.at[side],
                target.at[side],
                send_sem.at[side],
                recv_sem.at[side],
                group,
                x * 4 + partner_z[side],
            )
            for source, target, send_sem, recv_sem in (
                (mixed_out, mixed_got, mixed_send, mixed_recv),
                (lse_out, lse_got, lse_send, lse_recv),
            )
        ]
        for copy in copies:
            copy.start()
        return copies

    attend(1 - own_head, (2,), 10)
    exchanged = send(2)
    attend(1 - own_head, (3,), 10)
    exchanged = exchanged + send(3)

    attend(own_head, (1,), 10)
    exchanged = exchanged + send(1)

    for copy in group_out:
        copy.wait_recv()

    def choose(to, carry):
        page = new_all[jnp.clip(chosen[0, to], 0, GROUPS * CONVS - 1)].astype(F32)
        new_send[to] = (page * chosen[1, to].astype(F32)).astype(BF16)
        return carry

    lax.fori_loop(0, TENSOR, choose, 0)
    mine_copy = pltpu.make_async_copy(
        new_send.at[tensor], new_pages.at[tensor], load_sem.at[6]
    )
    mine_copy.start()

    def page_copy(off):
        to = lax.rem(tensor + off, TENSOR)
        return remote(
            new_send.at[to],
            new_pages.at[tensor],
            page_send.at[off],
            page_recv.at[off],
            group,
            to,
        )

    def page_start(off, carry):
        page_copy(off).start()
        return carry

    lax.fori_loop(1, TENSOR, page_start, 0)
    attend(own_head, (0,), 10)
    for copy in exchanged:
        copy.wait_recv()
    row_of = lane_iota((1, half)) & (SUF - 1)

    def combine(i):
        peak, total, accum = result(0, i)
        own_peak = own_stats[i, 0:1, :]
        logs = [lse_got[r, i, 0:1, :] for r in (1, 2, 3)]
        top = jnp.maximum(
            jnp.maximum(peak, own_peak), jnp.maximum(jnp.maximum(logs[0], logs[1]), logs[2])
        )
        shares = [jnp.exp2(log - top) for log in logs]
        first, second = jnp.exp2(peak - top), jnp.exp2(own_peak - top)
        total = total * first + own_stats[i, 1:2, :] * second
        total = total + shares[0] + shares[1] + shares[2]
        scale = jnp.where(row_of < suffix_ref[conv_ref[group * CONVS + i]], 1.0, 0.0) / total
        joined = accum * (first * scale) + own_accum[i] * (second * scale)
        for r in (1, 2, 3):
            joined = joined + mixed_got[r, i].astype(F32) * (shares[r - 1] * scale)
        turned = jnp.transpose(joined).astype(BF16)
        for head in range(HEADS):
            mixed[i * SUF : (i + 1) * SUF, head * HD : (head + 1) * HD] = turned[
                head * SUF : (head + 1) * SUF, :
            ]

    pending = []

    class Ring:
        def __init__(self, side, first, pick, buffers, way):
            self.side, self.first, self.pick, self.buffers = side, first, pick, buffers
            self.up, self.down, self.me, self.far, self.to_up, self.to_down = way
            self.top = pl.ds(side * 2 * SUF, SUF)
            self.bottom = pl.ds(side * 2 * SUF + SUF, SUF)

        def send(self, index, ref, to):
            sem = self.first + index
            copy = remote(
                ref,
                self.buffers.at[self.side, index],
                ring_send.at[sem],
                ring_recv.at[sem],
                group,
                to,
            )
            copy.start()
            pending.append(copy)
            return copy

        def start_far(self):
            pick = self.pick
            self.c0 = self.send(0, pick(self.far, self.top), self.to_up)
            self.c1 = self.send(1, pick(self.far, self.bottom), self.to_down)

        def start_near(self):
            pick = self.pick
            self.c2 = self.send(2, pick(self.up, self.bottom), self.to_up)
            self.c3 = self.send(3, pick(self.down, self.top), self.to_down)

        def add(self, ref, *indices):
            total = ref[...].astype(F32)
            for index in indices:
                total = total + self.buffers[self.side, index].astype(F32)
            ref[...] = total.astype(BF16)

        def relay(self):
            pick = self.pick
            self.c0.wait_recv()
            self.add(pick(self.up, self.top), 0)
            self.c4 = self.send(4, pick(self.up, self.top), self.to_up)
            self.c1.wait_recv()
            self.add(pick(self.down, self.bottom), 1)
            self.c5 = self.send(5, pick(self.down, self.bottom), self.to_down)

        def finish(self):
            pick = self.pick
            self.c3.wait_recv()
            self.c4.wait_recv()
            self.add(pick(self.me, self.top), 3, 4)
            self.c2.wait_recv()
            self.c5.wait_recv()
            self.add(pick(self.me, self.bottom), 2, 5)

    along_x = (x_up, x_down, x, x_far, to_x_up, to_x_down)
    along_z = (z_up, z_down, z, z_far, to_z_up, to_z_down)
    firsts = (
        Ring(0, 0, lambda j, rows: part.at[j, :, rows], big, along_x),
        Ring(1, 6, lambda j, rows: part.at[:, j, rows], big, along_z),
    )
    seconds = (
        Ring(0, 12, lambda j, rows: part.at[x, j, rows], small, along_z),
        Ring(1, 18, lambda j, rows: part.at[j, z, rows], small, along_x),
    )

    def out_block(bx, bz):
        columns = pl.ds(pl.multiple_of((bx * 4 + bz) * PART, PART), PART)
        part[bx, bz] = jnp.dot(
            mixed[...], weights[:, columns], preferred_element_type=F32
        ).astype(BF16)

    def project_many(pairs):
        for bx, bz in pairs:
            out_block(bx, bz)

    for i in range(CONVS):
        combine(i)
    load_out.wait()
    project_many([(x_far, bz) for bz in (z_far, z_up, z_down, z)])
    firsts[0].start_far()
    project_many([(bx, z_far) for bx in (x_up, x_down, x)])
    firsts[1].start_far()
    project_many([(x_up, z_up), (x_up, z_down), (x_up, z)])
    project_many([(x_down, z_up), (x_down, z_down), (x_down, z)])
    firsts[0].start_near()
    project_many([(x, z_up), (x, z_down), (x, z)])
    firsts[1].start_near()
    firsts[0].relay()
    firsts[1].relay()
    for first, second in zip(firsts, seconds):
        first.finish()
        second.start_far()
        second.start_near()
    seconds[0].relay()
    seconds[1].relay()
    seconds[0].finish()
    seconds[1].finish()
    out_ref[...] = part[x, z]
    for copy in exchanged + pending + sent + pages_out + group_out + query_out + [kv_copy]:
        copy.wait_send()
    mine_copy.wait()

    def page_end(off, carry):
        page_copy(off).wait()
        return carry

    lax.fori_loop(1, TENSOR, page_end, 0)


def any_spec():
    return pl.BlockSpec(memory_space=pl.ANY)


def vmem_spec():
    return pl.BlockSpec(memory_space=pltpu.VMEM)


def smem_spec():
    return pl.BlockSpec(memory_space=pltpu.SMEM)


def shards(
    hidden_states,
    norm_gain,
    w_query,
    b_query,
    w_key,
    b_key,
    w_value,
    b_value,
    w_out,
    pool_keys,
    pool_values,
    conv_slots,
    page_table,
    prefix_len,
    suffix_len,
    new_dest,
):
    dma = pltpu.SemaphoreType.DMA
    freq = THETA ** (-(np.arange(HD // 2, dtype=np.float64) * 2.0 / HD))
    freq = jnp.asarray(np.concatenate([freq, freq])[None, :], F32)
    shape = jax.ShapeDtypeStruct
    attn_out, new_pages = pl.pallas_call(
        layer_kernel,
        out_shape=[shape((ROWS, PART), BF16), shape((TENSOR, SUF, HD), BF16)],
        in_specs=[smem_spec()] * 4
        + [vmem_spec()]
        + [any_spec()] * 7
        + [vmem_spec()] * 5,
        out_specs=[vmem_spec(), any_spec()],
        scratch_shapes=[
            pltpu.VMEM((4, 4, ROWS, PART), BF16),
            pltpu.VMEM((WIDTH, HEADS * HD), BF16),
            pltpu.VMEM((HD, WIDTH), BF16),
            pltpu.VMEM((ROWS, HEADS * HD), F32),
            pltpu.VMEM((ROWS, HD), F32),
            pltpu.VMEM((ROWS, HD), F32),
            pltpu.VMEM((GROUPS, 2, 8, PAGE, HD), BF16),
            pltpu.VMEM((4, 2 * GROUPS, 2, PAGE, HD), BF16),
            pltpu.VMEM((PAGES, 2, PAGE, HD), BF16),
            pltpu.VMEM((PAGES, 2, PAGE, HD), BF16),
            pltpu.VMEM((4, CONVS, HEADS * SUF, HD), BF16),
            pltpu.VMEM((ROWS, HD), BF16),
            pltpu.VMEM((ROWS, HD), BF16),
            pltpu.VMEM((ROWS, HD), BF16),
            pltpu.VMEM((ROWS, HD), BF16),
            pltpu.VMEM((GROUPS * CONVS, SUF, HD), BF16),
            pltpu.VMEM((LIST, HD), I32),
            pltpu.SMEM((LIST, HD), I32),
            pltpu.SMEM((2, TENSOR), I32),
            pltpu.VMEM((1, WIDTH), F32),
            pltpu.VMEM((HEADS * HD, WIDTH), BF16),
            pltpu.VMEM((4, BLOCKS, HD, HEADS * SUF), F32),
            pltpu.VMEM((4, BLOCKS, 8, HEADS * SUF), F32),
            pltpu.VMEM((CONVS, HD, HEADS * SUF), F32),
            pltpu.VMEM((CONVS, 8, HEADS * SUF), F32),
            pltpu.VMEM((4, CONVS, HD, HEADS * SUF), BF16),
            pltpu.VMEM((4, CONVS, 8, HEADS * SUF), F32),
            pltpu.VMEM((4, CONVS, HD, HEADS * SUF), BF16),
            pltpu.VMEM((4, CONVS, 8, HEADS * SUF), F32),
            pltpu.VMEM((ROWS, HEADS * HD), BF16),
            pltpu.VMEM((4, 4, ROWS, PART), BF16),
            pltpu.VMEM((2, 6, 4, SUF, PART), BF16),
            pltpu.VMEM((2, 6, SUF, PART), BF16),
            pltpu.VMEM((TENSOR, SUF, HD), BF16),
            dma((8,)),
            dma((2, GROUPS)),
            dma((20,)),
            dma((20,)),
            dma((2, GROUPS)),
            dma((2, GROUPS)),
            dma((2, GROUPS, 4)),
            dma((2, GROUPS, 4)),
            dma((4,)),
            dma((4,)),
            dma((4,)),
            dma((4,)),
            dma((GROUPS,)),
            dma((GROUPS,)),
            dma((4,)),
            dma((4,)),
            dma((4,)),
            dma((4,)),
            dma((24,)),
            dma((24,)),
            dma((TENSOR,)),
            dma((TENSOR,)),
        ],
        compiler_params=pltpu.CompilerParams(
            collective_id=0, has_side_effects=True, vmem_limit_bytes=62 * 1024 * 1024
        ),
        name="layer",
    )(
        conv_slots,
        prefix_len,
        suffix_len,
        new_dest,
        page_table,
        hidden_states,
        pool_keys,
        pool_values,
        w_query,
        w_key.T,
        w_value.T,
        w_out,
        norm_gain,
        b_query,
        b_key,
        b_value,
        freq,
    )
    pages = new_pages.reshape(TENSOR // 2, 2, SUF, HD)
    return (attn_out, pages[None, :, 0], pages[None, :, 1])


def solution(mesh):
    in_specs = (
        P("group", "tensor"),
        P(),
        P(None, "tensor"),
        P("tensor"),
        P(None, "tensor"),
        P("tensor"),
        P(None, "tensor"),
        P("tensor"),
        P("tensor", None),
        P(("group", "tensor"), None, None, None),
        P(("group", "tensor"), None, None, None),
        P(),
        P(),
        P(),
        P(),
        P(),
    )
    out_specs = (
        P("group", "tensor"),
        P(("group", "tensor"), None, None, None),
        P(("group", "tensor"), None, None, None),
    )
    return jax.shard_map(shards, mesh=mesh, in_specs=in_specs, out_specs=out_specs, check_vma=False)
```

```python
import jax
import jax.numpy as jnp
import numpy as np
from jax import lax
from jax.experimental import pallas as pl
from jax.experimental.pallas import tpu as pltpu
from jax.sharding import PartitionSpec as P

HD = 128
SUF = 64
CONVS = 4
ROWS = CONVS * SUF
GROUPS = 8
TENSOR = 16
WIDTH = 8192
PART = WIDTH // TENSOR
PAGES = 64
PAGE = 64
HEADS = 4
THETA = 1000000.0
EPSILON = 1e-06
NEGATIVE = -1e30
SCALE = HD**-0.5 * 1.4426950408889634
STEP = 4
BLOCKS = 20
LIST = 80
LN2 = 0.6931471805599453
MESH = pl.DeviceIdType.MESH
BF16 = jnp.bfloat16
F32 = jnp.float32
I32 = jnp.int32


def remote(src, dst, send_sem, recv_sem, group, tensor):
    return pltpu.make_async_remote_copy(
        src_ref=src,
        dst_ref=dst,
        send_sem=send_sem,
        recv_sem=recv_sem,
        device_id=(group, tensor),
        device_id_type=MESH,
    )


def place():
    group = lax.axis_index("group")
    tensor = lax.axis_index("tensor")
    return (
        group,
        tensor,
        lax.div(group, 2),
        lax.rem(group, 2),
        lax.div(tensor, 4),
        lax.rem(tensor, 4),
    )


def lane_iota(shape):
    return lax.broadcasted_iota(I32, shape, len(shape) - 1)


def row_iota(shape):
    return lax.broadcasted_iota(I32, shape, len(shape) - 2)


def layer_kernel(
    conv_ref,
    prefix_ref,
    suffix_ref,
    dest_ref,
    table_ref,
    hidden,
    pool_k,
    pool_v,
    w_query,
    w_key,
    w_value,
    w_out,
    gain_ref,
    b_query,
    b_key,
    b_value,
    freq_ref,
    out_ref,
    new_pages,
    feat,
    wq,
    wkv,
    acc_q,
    acc_kv,
    squares,
    stage_k,
    stage_v,
    got_k,
    got_v,
    queries,
    key_new,
    value_new,
    kv_own,
    kv_other,
    new_all,
    table_out,
    lists,
    chosen,
    gain,
    weights,
    accums,
    stats,
    own_accum,
    own_stats,
    mixed_out,
    lse_out,
    mixed_got,
    lse_got,
    mixed,
    part,
    big,
    small,
    new_send,
    load_sem,
    keep_sem,
    feat_send,
    feat_recv,
    y_send,
    y_recv,
    x_send,
    x_recv,
    v_send,
    v_recv,
    pair_send,
    pair_recv,
    group_send,
    group_recv,
    mixed_send,
    mixed_recv,
    lse_send,
    lse_recv,
    ring_send,
    ring_recv,
    page_send,
    page_recv,
):
    group, tensor, y, core, x, z = place()
    parity = lax.rem(z, 2)
    partner_z = [z, z + 1 - 2 * parity, lax.rem(z + 2, 4), 3 - z]
    own = pltpu.make_async_copy(hidden, feat.at[x, z], load_sem.at[0])
    own.start()
    loads = [
        pltpu.make_async_copy(w_query, wq, load_sem.at[1]),
        pltpu.make_async_copy(w_key, wkv.at[pl.ds(0, HD // 2)], load_sem.at[2]),
        pltpu.make_async_copy(w_value, wkv.at[pl.ds(HD // 2, HD // 2)], load_sem.at[3]),
    ]
    for load in loads:
        load.start()

    def group_at(shift):
        to_y = lax.rem(y + shift // 2, 4)
        to_core = lax.rem(core + shift % 2, 2)
        return to_y * 2 + to_core

    barrier = pltpu.get_barrier_semaphore()
    for shift in range(1, GROUPS):
        pl.semaphore_signal(
            barrier, inc=1, device_id=(group_at(shift), tensor), device_id_type=MESH
        )

    def greet(off, carry):
        to = lax.rem(tensor + off, TENSOR)
        pl.semaphore_signal(barrier, inc=1, device_id=(group, to), device_id_type=MESH)
        return carry

    lax.fori_loop(1, TENSOR, greet, 0)
    pl.semaphore_wait(barrier, GROUPS - 1 + TENSOR - 1)

    own.wait()
    x_at = [lax.rem(x + shift, 4) for shift in range(4)]
    x_up, x_far, x_down = x_at[1:]
    z_up, z_far, z_down = (lax.rem(z + shift, 4) for shift in (1, 2, 3))
    to_x_up, to_x_down = x_at[1] * 4 + z, x_at[3] * 4 + z
    to_z_up, to_z_down = x * 4 + z_up, x * 4 + z_down
    half_rows = ROWS // 2
    low_rows, high_rows = pl.ds(0, half_rows), pl.ds(half_rows, half_rows)
    sent, kept = [], []

    def pass_on(index, ref, to):
        copy = remote(ref, ref, feat_send.at[index], feat_recv.at[index], group, to)
        copy.start()
        sent.append(copy)
        return copy

    def spread(block, shift):
        ref = feat.at[x_at[shift], z]
        return (
            pass_on(4 + 4 * block, ref, to_z_up),
            pass_on(5 + 4 * block, ref, to_z_down),
        )

    def spread_on(block, shift, copies):
        copies[0].wait_recv()
        first = pass_on(6 + 4 * block, feat.at[x_at[shift], z_down, low_rows], to_z_up)
        copies[1].wait_recv()
        second = pass_on(7 + 4 * block, feat.at[x_at[shift], z_up, high_rows], to_z_down)
        return first, second

    pages_out = []

    def push(source, target, send_sem, recv_sem, to_group, to):
        copy = remote(source, target, send_sem, recv_sem, to_group, to)
        copy.start()
        pages_out.append(copy)
        return copy

    def keep(source, target, sem):
        copy = pltpu.make_async_copy(source, target, sem)
        copy.start()
        kept.append(copy)

    def slots(shift):
        return pl.ds(2 * group_at(shift), 2)

    def heads(step):
        return pl.ds(2 * x_at[step], 2)

    def keys_first(shift):
        return push(
            pool_k.at[slots(shift)],
            stage_k.at[shift],
            y_send.at[0, shift],
            y_recv.at[0, shift],
            group_at(shift),
            tensor,
        )

    def keys_second(shift):
        for step in (1, 3, 2, 0):
            if shift == 0:
                source = pool_k.at[slots(0), heads(step)]
            else:
                source = stage_k.at[shift, :, heads(step)]
            target = got_k.at[pl.ds(2 * (step * GROUPS + shift), 2)]
            if step == 0:
                keep(source, target, keep_sem.at[0, shift])
            else:
                keys_last.append(
                    push(
                        source,
                        target,
                        x_send.at[0, shift, step],
                        x_recv.at[0, shift, step],
                        group,
                        x_at[step] * 4 + z,
                    )
                )

    def values_first(step):
        return push(
            pool_v.at[:, heads(step)],
            stage_v.at[step],
            v_send.at[step],
            v_recv.at[step],
            group,
            x_at[step] * 4 + z,
        )

    def values_second(step):
        for shift in (1, 2, 6, 3, 7, 4, 5, 0):
            if step == 0:
                source = pool_v.at[slots(shift), heads(0)]
            else:
                source = stage_v.at[step, slots(shift)]
            target = got_v.at[pl.ds(2 * (step * GROUPS + shift), 2)]
            if shift == 0:
                keep(source, target, keep_sem.at[1, step])
            else:
                keys_last.append(
                    push(
                        source,
                        target,
                        x_send.at[1, shift, step],
                        x_recv.at[1, shift, step],
                        group_at(shift),
                        tensor,
                    )
                )

    keys_last = []
    f0 = pass_on(0, feat.at[x, z], to_x_up)
    f1 = pass_on(1, feat.at[x, z], to_x_down)
    s0 = spread(0, 0)
    key_first = {shift: keys_first(shift) for shift in (1, 2, 6, 3, 7, 4, 5)}
    f0.wait_recv()
    f2 = pass_on(2, feat.at[x_at[3], z, low_rows], to_x_up)
    s1 = spread(1, 3)
    f1.wait_recv()
    f3 = pass_on(3, feat.at[x_at[1], z, high_rows], to_x_down)
    s2 = spread(2, 1)
    value_first = {step: values_first(step) for step in (1, 3, 2)}
    prefix = [prefix_ref[conv_ref[group * CONVS + i]] for i in range(CONVS)]
    suffix = [suffix_ref[conv_ref[group * CONVS + i]] for i in range(CONVS)]

    offsets = row_iota((SUF, HD))
    positions = jnp.concatenate([offsets + prefix[i] for i in range(CONVS)], axis=0)
    angle = positions.astype(F32) * freq_ref[...]
    cosine = jnp.cos(angle)
    sine = jnp.sin(angle)
    sine = jnp.where(lane_iota((ROWS, HD)) < HD // 2, -sine, sine)

    f2.wait_recv()
    f3.wait_recv()
    s3 = spread(3, 2)
    r0 = spread_on(0, 0, s0)

    for load in loads:
        load.wait()
    load_out = pltpu.make_async_copy(w_out, weights, load_sem.at[5])
    load_out.start()
    gain[...] = gain_ref[...].astype(F32).reshape(1, WIDTH)
    query_bias = b_query[...].astype(F32).reshape(1, HEADS * HD)
    acc_q[...] = jnp.zeros_like(acc_q)
    acc_kv[...] = jnp.zeros_like(acc_kv)
    squares[...] = jnp.zeros_like(squares)

    def project(bz, first, end):
        def one(bx, carry):
            block = bx * 4 + bz
            rows = pl.ds(pl.multiple_of(block * PART, PART), PART)
            wide = feat[bx, bz].astype(F32)
            scaled = (wide * gain[:, rows]).astype(BF16)
            acc_q[...] += jnp.dot(scaled, wq[rows, :], preferred_element_type=F32)
            acc_kv[...] += lax.dot_general(
                scaled,
                wkv[:, rows],
                (((1,), (1,)), ((), ())),
                preferred_element_type=F32,
            )
            wide = wide * wide
            total = squares[...]
            for part in range(PART // HD):
                total = total + wide[:, part * HD : (part + 1) * HD]
            squares[...] = total
            return carry

        lax.fori_loop(first, end, one, 0)

    project(z, 0, 4)
    r1 = spread_on(1, 3, s1)
    r2 = spread_on(2, 1, s2)
    r3 = spread_on(3, 2, s3)
    for shift in (1, 2, 6, 3, 7, 4, 5):
        key_first[shift].wait_recv()
    values_second(0)
    for shift in (0, 1, 2, 6, 3, 7, 4, 5):
        keys_second(shift)
    project(z_up, 0, 4)
    project(z_down, 0, 4)
    for step in (1, 3, 2):
        value_first[step].wait_recv()
        values_second(step)
    for shift, copies in ((0, r0), (3, r1), (1, r2), (2, r3)):
        for copy in copies:
            copy.wait_recv()
        project(z_far, x_at[shift], x_at[shift] + 1)
    mean = jnp.sum(squares[...], axis=1, keepdims=True) * (1.0 / WIDTH)
    factor = lax.rsqrt(mean + EPSILON)
    bias = jnp.concatenate(
        [ref[...].astype(F32).reshape(1, HD // 2) for ref in (b_key, b_value)], axis=1
    )
    kv_own[...] = (acc_kv[...] * factor + bias).astype(BF16)
    kv_copy = remote(
        kv_own,
        kv_other,
        pair_send.at[0],
        pair_recv.at[0],
        group,
        x * 4 + partner_z[1],
    )
    kv_copy.start()

    def rotate(values):
        return values * cosine + pltpu.roll(values, HD // 2, 1) * sine

    for head in range(HEADS):
        columns = slice(head * HD, (head + 1) * HD)
        values = acc_q[:, columns] * factor + query_bias[:, columns]
        values = rotate(values).astype(BF16)
        for i in range(CONVS):
            queries[0, i, head * SUF : (head + 1) * SUF, :] = values[i * SUF : (i + 1) * SUF, :]
    query_out = [
        remote(
            queries.at[0],
            queries.at[r],
            pair_send.at[r],
            pair_recv.at[r],
            group,
            x * 4 + partner_z[r],
        )
        for r in (1, 2, 3)
    ]
    for copy in query_out:
        copy.start()

    kv_copy.wait_recv()
    mine = kv_own[...].astype(F32)
    theirs = kv_other[...].astype(F32)
    even = jnp.where(parity == 0, mine, theirs)
    odd = jnp.where(parity == 0, theirs, mine)
    low = lane_iota((ROWS, HD)) < HD // 2
    keys = jnp.where(low, even, pltpu.roll(odd, HD // 2, 1))
    keys = rotate(keys)
    values = jnp.where(low, pltpu.roll(even, HD // 2, 1), odd)
    key_new[...] = keys.astype(BF16)
    value_new[...] = values.astype(BF16)

    page = jnp.where(parity == 0, keys.astype(BF16).astype(F32), values)
    live_row = jnp.concatenate([offsets < suffix[i] for i in range(CONVS)], axis=0)
    page = jnp.where(live_row, page, 0.0).astype(BF16)
    new_ref = new_all.at[pl.ds(group * CONVS, CONVS)]
    new_ref[...] = page.reshape(CONVS, SUF, HD)
    group_out = [
        remote(
            new_ref,
            new_ref,
            group_send.at[shift],
            group_recv.at[shift],
            group_at(shift),
            tensor,
        )
        for shift in range(1, GROUPS)
    ]
    for copy in group_out:
        copy.start()

    page_ids = lane_iota((1, PAGES))
    below = (row_iota((PAGES, PAGES)) < lane_iota((PAGES, PAGES))).astype(F32)
    lane = lane_iota((LIST, HD))
    place_id = row_iota((LIST, PAGES)).astype(F32)
    row_id = row_iota((LIST, 1)).astype(F32)
    codes = jnp.zeros((LIST, 1), F32)
    block_conv = jnp.zeros((LIST, 1), F32)
    block_first = jnp.zeros((LIST, 1), F32)
    last_block = jnp.zeros((LIST, 1), F32)
    has_block = jnp.zeros((LIST, 1), F32)
    begin = jnp.zeros((1, 1), F32)
    for i in range(CONVS):
        entry = table_ref[pl.ds(conv_ref[group * CONVS + i], 1), :]
        source = entry >> 4
        source_y, source_core = source >> 5, (source >> 4) & 1
        source_x, source_z = (source >> 2) & 3, source & 3
        live = jnp.clip(prefix[i] - page_ids * PAGE, 0, PAGE)
        here = (source_z == z) & (live > 0)
        where = ((x - source_x) & 3) * GROUPS
        where = where + ((y - source_y) & 3) * 2 + ((core - source_core) & 1)
        value = ((where * 2 + (entry & 1)) * 128 + live).astype(F32)
        here_f = here.astype(F32)
        order = jnp.dot(
            jnp.broadcast_to(here_f, (8, PAGES)), below, preferred_element_type=F32
        )[0:1, :]
        count = jnp.sum(here_f, axis=1, keepdims=True)
        blocks = jnp.floor((count + (STEP - 1)) * (1.0 / STEP))
        match = (order + begin * STEP == place_id) & (
            jnp.broadcast_to(here_f, (LIST, PAGES)) > 0.5
        )
        codes = codes + jnp.sum(jnp.where(match, value, 0.0), axis=1, keepdims=True)
        block_first = jnp.where(row_id == begin, 1.0, block_first)
        begin = begin + blocks
        if i < CONVS - 1:
            block_conv = block_conv + jnp.where(row_id >= begin, 1.0, 0.0)
        last_block = jnp.where(row_id == i, jnp.maximum(begin - 1.0, 0.0), last_block)
        has_block = jnp.where(row_id == i, jnp.minimum(count, 1.0), has_block)
    table = jnp.zeros((LIST, HD), F32)
    for column, data in enumerate((codes, block_conv, block_first, last_block, has_block)):
        table = jnp.where(lane == column, data, table)
    table_out[...] = table.astype(I32)
    list_copy = pltpu.make_async_copy(table_out, lists, load_sem.at[4])
    list_copy.start()

    def find(to, carry):
        target = group * TENSOR + to
        index = jnp.int32(0)
        found = jnp.int32(0)
        for slot in range(GROUPS * CONVS):
            hit = dest_ref[conv_ref[slot]] == target
            index = jnp.where(hit, slot, index)
            found = jnp.where(hit, 1, found)
        chosen[0, to] = index
        chosen[1, to] = found
        return carry

    lax.fori_loop(0, TENSOR, find, 0)

    half = HEADS * SUF
    own_head = lax.div(z, 2)

    def score(keys, query):
        return lax.dot_general(
            keys, query, (((1,), (1,)), ((), ())), preferred_element_type=F32
        )

    def mix(values, shares):
        return lax.dot_general(
            values,
            shares.astype(BF16),
            (((0,), (0,)), ((), ())),
            preferred_element_type=F32,
        )

    causal = row_iota((SUF, half)) <= (lane_iota((SUF, half)) & (SUF - 1))
    for i in range(CONVS):
        rows = slice(i * SUF, (i + 1) * SUF)
        scores = score(key_new[rows], queries[0, i])
        scores = jnp.where(causal, scores * SCALE, NEGATIVE)
        peak = jnp.max(scores, axis=0, keepdims=True)
        shares = jnp.exp2(scores - peak)
        own_accum[i] = mix(value_new[rows], shares)
        own_stats[i, 0:1, :] = peak
        own_stats[i, 1:2, :] = jnp.sum(shares, axis=0, keepdims=True)
    list_copy.wait()
    for copy in query_out + keys_last:
        copy.wait_recv()
    for copy in kept:
        copy.wait()

    token = row_iota((PAGE, half))

    def attend(head, sides, width):
        def pack(index, state):
            blocks = [index * width + k for k in range(width)]
            codes = [[lists[b * STEP + p, 0] for p in range(STEP)] for b in blocks]
            convs = [jnp.clip(lists[b, 1], 0, CONVS - 1) for b in blocks]
            spots = [[jnp.clip(code >> 7, 0, PAGES - 1) for code in row] for row in codes]
            firsts = [lists[b, 2] == 1 for b in blocks]
            keys = [
                jnp.concatenate([got_k[spot, head] for spot in row], axis=0)
                for row in spots
            ]
            values = [
                jnp.concatenate([got_v[spot, head] for spot in row], axis=0)
                for row in spots
            ]
            pairs = [(k, s) for k in range(width) for s in range(len(sides))]
            scores = {
                (k, s): score(keys[k], queries[sides[s], convs[k]]) for k, s in pairs
            }
            for k, s in pairs:
                scores[k, s] = jnp.concatenate(
                    [
                        jnp.where(
                            token < (codes[k][p] & 127),
                            scores[k, s][p * PAGE : (p + 1) * PAGE] * SCALE,
                            NEGATIVE,
                        )
                        for p in range(STEP)
                    ],
                    axis=0,
                )
            tops = {
                key: jnp.max(value, axis=0, keepdims=True) for key, value in scores.items()
            }
            state = list(state)
            fresh, shrink = {}, {}
            for s in range(len(sides)):
                peak = state[s][0]
                for k in range(width):
                    peak = jnp.where(firsts[k], NEGATIVE, peak)
                    fresh[k, s] = jnp.maximum(peak, tops[k, s])
                    shrink[k, s] = jnp.exp2(peak - fresh[k, s])
                    peak = fresh[k, s]
            shares = {key: jnp.exp2(scores[key] - fresh[key]) for key in pairs}
            sums = {key: jnp.sum(shares[key], axis=0, keepdims=True) for key in pairs}
            mixes = {(k, s): mix(values[k], shares[k, s]) for k, s in pairs}
            for s, side in enumerate(sides):
                peak, total, accum = state[s]
                for k in range(width):
                    total = total * shrink[k, s] + sums[k, s]
                    accum = accum * shrink[k, s] + mixes[k, s]
                    accums[side, blocks[k]] = accum
                    stats[side, blocks[k], 0:1, :] = fresh[k, s]
                    stats[side, blocks[k], 1:2, :] = total
                state[s] = (fresh[width - 1, s], total, accum)
            return tuple(state)

        empty = (
            jnp.full((1, half), NEGATIVE, F32),
            jnp.zeros((1, half), F32),
            jnp.zeros((HD, half), F32),
        )
        lax.fori_loop(0, BLOCKS // width, pack, tuple(empty for _ in sides))

    def result(side, i):
        last = jnp.clip(lists[i, 3], 0, BLOCKS - 1)
        some = lists[i, 4] == 1
        peak = jnp.where(some, stats[side, last, 0:1, :], NEGATIVE)
        total = jnp.where(some, stats[side, last, 1:2, :], 0.0)
        accum = accums[side, last] * jnp.where(some, 1.0, 0.0)
        return peak, total, accum

    def send(side):
        for i in range(CONVS):
            peak, total, accum = result(side, i)
            safe = jnp.where(total > 0.0, total, 1.0)
            mixed_out[side, i] = (accum * (1.0 / safe)).astype(BF16)
            lse = jnp.where(total > 0.0, peak + jnp.log(safe) * (1.0 / LN2), NEGATIVE)
            lse_out[side, i] = jnp.broadcast_to(lse, (8, half))
        copies = [
            remote(
                source.at[side],
                target.at[side],
                send_sem.at[side],
                recv_sem.at[side],
                group,
                x * 4 + partner_z[side],
            )
            for source, target, send_sem, recv_sem in (
                (mixed_out, mixed_got, mixed_send, mixed_recv),
                (lse_out, lse_got, lse_send, lse_recv),
            )
        ]
        for copy in copies:
            copy.start()
        return copies

    attend(1 - own_head, (2,), 10)
    exchanged = send(2)
    attend(1 - own_head, (3,), 10)
    exchanged = exchanged + send(3)

    attend(own_head, (1,), 10)
    exchanged = exchanged + send(1)

    for copy in group_out:
        copy.wait_recv()

    def choose(to, carry):
        page = new_all[jnp.clip(chosen[0, to], 0, GROUPS * CONVS - 1)].astype(F32)
        new_send[to] = (page * chosen[1, to].astype(F32)).astype(BF16)
        return carry

    lax.fori_loop(0, TENSOR, choose, 0)
    mine_copy = pltpu.make_async_copy(
        new_send.at[tensor], new_pages.at[tensor], load_sem.at[6]
    )
    mine_copy.start()

    def page_copy(off):
        to = lax.rem(tensor + off, TENSOR)
        return remote(
            new_send.at[to],
            new_pages.at[tensor],
            page_send.at[off],
            page_recv.at[off],
            group,
            to,
        )

    def page_start(off, carry):
        page_copy(off).start()
        return carry

    lax.fori_loop(1, TENSOR, page_start, 0)
    attend(own_head, (0,), 10)
    for copy in exchanged:
        copy.wait_recv()
    row_of = lane_iota((1, half)) & (SUF - 1)

    def combine(i):
        peak, total, accum = result(0, i)
        own_peak = own_stats[i, 0:1, :]
        logs = [lse_got[r, i, 0:1, :] for r in (1, 2, 3)]
        top = jnp.maximum(
            jnp.maximum(peak, own_peak), jnp.maximum(jnp.maximum(logs[0], logs[1]), logs[2])
        )
        shares = [jnp.exp2(log - top) for log in logs]
        first, second = jnp.exp2(peak - top), jnp.exp2(own_peak - top)
        total = total * first + own_stats[i, 1:2, :] * second
        total = total + shares[0] + shares[1] + shares[2]
        scale = jnp.where(row_of < suffix_ref[conv_ref[group * CONVS + i]], 1.0, 0.0) / total
        joined = accum * (first * scale) + own_accum[i] * (second * scale)
        for r in (1, 2, 3):
            joined = joined + mixed_got[r, i].astype(F32) * (shares[r - 1] * scale)
        turned = jnp.transpose(joined).astype(BF16)
        for head in range(HEADS):
            mixed[i * SUF : (i + 1) * SUF, head * HD : (head + 1) * HD] = turned[
                head * SUF : (head + 1) * SUF, :
            ]

    pending = []

    class Ring:
        def __init__(self, side, first, pick, buffers, way):
            self.side, self.first, self.pick, self.buffers = side, first, pick, buffers
            self.up, self.down, self.me, self.far, self.to_up, self.to_down = way
            self.top = pl.ds(side * 2 * SUF, SUF)
            self.bottom = pl.ds(side * 2 * SUF + SUF, SUF)

        def send(self, index, ref, to):
            sem = self.first + index
            copy = remote(
                ref,
                self.buffers.at[self.side, index],
                ring_send.at[sem],
                ring_recv.at[sem],
                group,
                to,
            )
            copy.start()
            pending.append(copy)
            return copy

        def start_far(self):
            pick = self.pick
            self.c0 = self.send(0, pick(self.far, self.top), self.to_up)
            self.c1 = self.send(1, pick(self.far, self.bottom), self.to_down)

        def start_near(self):
            pick = self.pick
            self.c2 = self.send(2, pick(self.up, self.bottom), self.to_up)
            self.c3 = self.send(3, pick(self.down, self.top), self.to_down)

        def add(self, ref, *indices):
            total = ref[...].astype(F32)
            for index in indices:
                total = total + self.buffers[self.side, index].astype(F32)
            ref[...] = total.astype(BF16)

        def relay(self):
            pick = self.pick
            self.c0.wait_recv()
            self.add(pick(self.up, self.top), 0)
            self.c4 = self.send(4, pick(self.up, self.top), self.to_up)
            self.c1.wait_recv()
            self.add(pick(self.down, self.bottom), 1)
            self.c5 = self.send(5, pick(self.down, self.bottom), self.to_down)

        def finish(self):
            pick = self.pick
            self.c3.wait_recv()
            self.c4.wait_recv()
            self.add(pick(self.me, self.top), 3, 4)
            self.c2.wait_recv()
            self.c5.wait_recv()
            self.add(pick(self.me, self.bottom), 2, 5)

    along_x = (x_up, x_down, x, x_far, to_x_up, to_x_down)
    along_z = (z_up, z_down, z, z_far, to_z_up, to_z_down)
    firsts = (
        Ring(0, 0, lambda j, rows: part.at[j, :, rows], big, along_x),
        Ring(1, 6, lambda j, rows: part.at[:, j, rows], big, along_z),
    )
    seconds = (
        Ring(0, 12, lambda j, rows: part.at[x, j, rows], small, along_z),
        Ring(1, 18, lambda j, rows: part.at[j, z, rows], small, along_x),
    )

    def out_block(bx, bz):
        columns = pl.ds(pl.multiple_of((bx * 4 + bz) * PART, PART), PART)
        part[bx, bz] = jnp.dot(
            mixed[...], weights[:, columns], preferred_element_type=F32
        ).astype(BF16)

    def project_many(pairs):
        for bx, bz in pairs:
            out_block(bx, bz)

    for i in range(CONVS):
        combine(i)
    load_out.wait()
    project_many([(x_far, bz) for bz in (z_far, z_up, z_down, z)])
    firsts[0].start_far()
    project_many([(bx, z_far) for bx in (x_up, x_down, x)])
    firsts[1].start_far()
    project_many([(x_up, z_up), (x_up, z_down), (x_up, z)])
    project_many([(x_down, z_up), (x_down, z_down), (x_down, z)])
    firsts[0].start_near()
    project_many([(x, z_up), (x, z_down), (x, z)])
    firsts[1].start_near()
    firsts[0].relay()
    firsts[1].relay()
    for first, second in zip(firsts, seconds):
        first.finish()
        second.start_far()
        second.start_near()
    seconds[0].relay()
    seconds[1].relay()
    seconds[0].finish()
    seconds[1].finish()
    out_ref[...] = part[x, z]
    for copy in exchanged + pending + sent + pages_out + group_out + query_out + [kv_copy]:
        copy.wait_send()
    mine_copy.wait()

    def page_end(off, carry):
        page_copy(off).wait()
        return carry

    lax.fori_loop(1, TENSOR, page_end, 0)


def place_kernel(part_out, pages, attn_out, new_keys, new_values, sems):
    copies = [
        pltpu.make_async_copy(part_out, attn_out, sems.at[0]),
        pltpu.make_async_copy(pages.at[:, 0], new_keys.at[0], sems.at[1]),
        pltpu.make_async_copy(pages.at[:, 1], new_values.at[0], sems.at[2]),
    ]
    for copy in copies:
        copy.start()
    for copy in copies:
        copy.wait()


def any_spec():
    return pl.BlockSpec(memory_space=pl.ANY)


def vmem_spec():
    return pl.BlockSpec(memory_space=pltpu.VMEM)


def smem_spec():
    return pl.BlockSpec(memory_space=pltpu.SMEM)


def shards(
    hidden_states,
    norm_gain,
    w_query,
    b_query,
    w_key,
    b_key,
    w_value,
    b_value,
    w_out,
    pool_keys,
    pool_values,
    conv_slots,
    page_table,
    prefix_len,
    suffix_len,
    new_dest,
):
    dma = pltpu.SemaphoreType.DMA
    freq = THETA ** (-(np.arange(HD // 2, dtype=np.float64) * 2.0 / HD))
    freq = jnp.asarray(np.concatenate([freq, freq])[None, :], F32)
    shape = jax.ShapeDtypeStruct
    attn_out, new_pages = pl.pallas_call(
        layer_kernel,
        out_shape=[shape((ROWS, PART), BF16), shape((TENSOR, SUF, HD), BF16)],
        in_specs=[smem_spec()] * 4
        + [vmem_spec()]
        + [any_spec()] * 7
        + [vmem_spec()] * 5,
        out_specs=[vmem_spec(), any_spec()],
        scratch_shapes=[
            pltpu.VMEM((4, 4, ROWS, PART), BF16),
            pltpu.VMEM((WIDTH, HEADS * HD), BF16),
            pltpu.VMEM((HD, WIDTH), BF16),
            pltpu.VMEM((ROWS, HEADS * HD), F32),
            pltpu.VMEM((ROWS, HD), F32),
            pltpu.VMEM((ROWS, HD), F32),
            pltpu.VMEM((GROUPS, 2, 8, PAGE, HD), BF16),
            pltpu.VMEM((4, 2 * GROUPS, 2, PAGE, HD), BF16),
            pltpu.VMEM((PAGES, 2, PAGE, HD), BF16),
            pltpu.VMEM((PAGES, 2, PAGE, HD), BF16),
            pltpu.VMEM((4, CONVS, HEADS * SUF, HD), BF16),
            pltpu.VMEM((ROWS, HD), BF16),
            pltpu.VMEM((ROWS, HD), BF16),
            pltpu.VMEM((ROWS, HD), BF16),
            pltpu.VMEM((ROWS, HD), BF16),
            pltpu.VMEM((GROUPS * CONVS, SUF, HD), BF16),
            pltpu.VMEM((LIST, HD), I32),
            pltpu.SMEM((LIST, HD), I32),
            pltpu.SMEM((2, TENSOR), I32),
            pltpu.VMEM((1, WIDTH), F32),
            pltpu.VMEM((HEADS * HD, WIDTH), BF16),
            pltpu.VMEM((4, BLOCKS, HD, HEADS * SUF), F32),
            pltpu.VMEM((4, BLOCKS, 8, HEADS * SUF), F32),
            pltpu.VMEM((CONVS, HD, HEADS * SUF), F32),
            pltpu.VMEM((CONVS, 8, HEADS * SUF), F32),
            pltpu.VMEM((4, CONVS, HD, HEADS * SUF), BF16),
            pltpu.VMEM((4, CONVS, 8, HEADS * SUF), F32),
            pltpu.VMEM((4, CONVS, HD, HEADS * SUF), BF16),
            pltpu.VMEM((4, CONVS, 8, HEADS * SUF), F32),
            pltpu.VMEM((ROWS, HEADS * HD), BF16),
            pltpu.VMEM((4, 4, ROWS, PART), BF16),
            pltpu.VMEM((2, 6, 4, SUF, PART), BF16),
            pltpu.VMEM((2, 6, SUF, PART), BF16),
            pltpu.VMEM((TENSOR, SUF, HD), BF16),
            dma((8,)),
            dma((2, GROUPS)),
            dma((20,)),
            dma((20,)),
            dma((2, GROUPS)),
            dma((2, GROUPS)),
            dma((2, GROUPS, 4)),
            dma((2, GROUPS, 4)),
            dma((4,)),
            dma((4,)),
            dma((4,)),
            dma((4,)),
            dma((GROUPS,)),
            dma((GROUPS,)),
            dma((4,)),
            dma((4,)),
            dma((4,)),
            dma((4,)),
            dma((24,)),
            dma((24,)),
            dma((TENSOR,)),
            dma((TENSOR,)),
        ],
        compiler_params=pltpu.CompilerParams(
            collective_id=0, has_side_effects=True, vmem_limit_bytes=62 * 1024 * 1024
        ),
        name="layer",
    )(
        conv_slots,
        prefix_len,
        suffix_len,
        new_dest,
        page_table,
        hidden_states,
        pool_keys,
        pool_values,
        w_query,
        w_key.T,
        w_value.T,
        w_out,
        norm_gain,
        b_query,
        b_key,
        b_value,
        freq,
    )
    page_shape = shape((1, TENSOR // 2, SUF, HD), BF16)
    return pl.pallas_call(
        place_kernel,
        out_shape=[shape((ROWS, PART), BF16), page_shape, page_shape],
        in_specs=[any_spec()] * 2,
        out_specs=[any_spec()] * 3,
        scratch_shapes=[dma((3,))],
        compiler_params=pltpu.CompilerParams(vmem_limit_bytes=62 * 1024 * 1024),
        name="place",
    )(attn_out, new_pages.reshape(TENSOR // 2, 2, SUF, HD))


def solution(mesh):
    in_specs = (
        P("group", "tensor"),
        P(),
        P(None, "tensor"),
        P("tensor"),
        P(None, "tensor"),
        P("tensor"),
        P(None, "tensor"),
        P("tensor"),
        P("tensor", None),
        P(("group", "tensor"), None, None, None),
        P(("group", "tensor"), None, None, None),
        P(),
        P(),
        P(),
        P(),
        P(),
    )
    out_specs = (
        P("group", "tensor"),
        P(("group", "tensor"), None, None, None),
        P(("group", "tensor"), None, None, None),
    )
    return jax.shard_map(shards, mesh=mesh, in_specs=in_specs, out_specs=out_specs, check_vma=False)
```

```python
import jax
import jax.numpy as jnp
import numpy as np
from jax import lax
from jax.experimental import pallas as pl
from jax.experimental.pallas import tpu as pltpu
from jax.sharding import PartitionSpec as P

HD = 128
SUF = 64
CONVS = 4
ROWS = CONVS * SUF
GROUPS = 8
TENSOR = 16
WIDTH = 8192
PART = WIDTH // TENSOR
PAGES = 64
PAGE = 64
HEADS = 4
THETA = 1000000.0
EPSILON = 1e-06
NEGATIVE = -1e30
SCALE = HD**-0.5 * 1.4426950408889634
STEP = 4
BLOCKS = 20
LIST = 80
LN2 = 0.6931471805599453
MESH = pl.DeviceIdType.MESH
BF16 = jnp.bfloat16
F32 = jnp.float32
I32 = jnp.int32


def remote(src, dst, send_sem, recv_sem, group, tensor):
    return pltpu.make_async_remote_copy(
        src_ref=src,
        dst_ref=dst,
        send_sem=send_sem,
        recv_sem=recv_sem,
        device_id=(group, tensor),
        device_id_type=MESH,
    )


def place():
    group = lax.axis_index("group")
    tensor = lax.axis_index("tensor")
    return (
        group,
        tensor,
        lax.div(group, 2),
        lax.rem(group, 2),
        lax.div(tensor, 4),
        lax.rem(tensor, 4),
    )


def lane_iota(shape):
    return lax.broadcasted_iota(I32, shape, len(shape) - 1)


def row_iota(shape):
    return lax.broadcasted_iota(I32, shape, len(shape) - 2)


def layer_kernel(
    conv_ref,
    prefix_ref,
    suffix_ref,
    dest_ref,
    table_ref,
    hidden,
    pool_k,
    pool_v,
    w_query,
    w_key,
    w_value,
    w_out,
    gain_ref,
    b_query,
    b_key,
    b_value,
    freq_ref,
    out_ref,
    new_pages,
    feat,
    wq,
    wkv,
    acc_q,
    acc_kv,
    squares,
    stage_k,
    stage_v,
    got_k,
    got_v,
    queries,
    key_new,
    value_new,
    kv_own,
    kv_other,
    new_all,
    table_out,
    lists,
    chosen,
    gain,
    weights,
    accums,
    stats,
    own_accum,
    own_stats,
    mixed_out,
    lse_out,
    mixed_got,
    lse_got,
    mixed,
    part,
    big,
    small,
    new_send,
    load_sem,
    keep_sem,
    feat_send,
    feat_recv,
    y_send,
    y_recv,
    x_send,
    x_recv,
    v_send,
    v_recv,
    pair_send,
    pair_recv,
    group_send,
    group_recv,
    mixed_send,
    mixed_recv,
    lse_send,
    lse_recv,
    ring_send,
    ring_recv,
    page_send,
    page_recv,
):
    group, tensor, y, core, x, z = place()
    parity = lax.rem(z, 2)
    partner_z = [z, z + 1 - 2 * parity, lax.rem(z + 2, 4), 3 - z]
    own = pltpu.make_async_copy(hidden, feat.at[x, z], load_sem.at[0])
    own.start()
    loads = [
        pltpu.make_async_copy(w_query, wq, load_sem.at[1]),
        pltpu.make_async_copy(w_key, wkv.at[pl.ds(0, HD // 2)], load_sem.at[2]),
        pltpu.make_async_copy(w_value, wkv.at[pl.ds(HD // 2, HD // 2)], load_sem.at[3]),
    ]
    for load in loads:
        load.start()

    def group_at(shift):
        to_y = lax.rem(y + shift // 2, 4)
        to_core = lax.rem(core + shift % 2, 2)
        return to_y * 2 + to_core

    barrier = pltpu.get_barrier_semaphore()
    for shift in range(1, GROUPS):
        pl.semaphore_signal(
            barrier, inc=1, device_id=(group_at(shift), tensor), device_id_type=MESH
        )

    def greet(off, carry):
        to = lax.rem(tensor + off, TENSOR)
        pl.semaphore_signal(barrier, inc=1, device_id=(group, to), device_id_type=MESH)
        return carry

    lax.fori_loop(1, TENSOR, greet, 0)
    pl.semaphore_wait(barrier, GROUPS - 1 + TENSOR - 1)

    own.wait()
    x_at = [lax.rem(x + shift, 4) for shift in range(4)]
    x_up, x_far, x_down = x_at[1:]
    z_up, z_far, z_down = (lax.rem(z + shift, 4) for shift in (1, 2, 3))
    to_x_up, to_x_down = x_at[1] * 4 + z, x_at[3] * 4 + z
    to_z_up, to_z_down = x * 4 + z_up, x * 4 + z_down
    half_rows = ROWS // 2
    low_rows, high_rows = pl.ds(0, half_rows), pl.ds(half_rows, half_rows)
    sent, kept = [], []

    def pass_on(index, ref, to):
        copy = remote(ref, ref, feat_send.at[index], feat_recv.at[index], group, to)
        copy.start()
        sent.append(copy)
        return copy

    def spread(block, shift):
        ref = feat.at[x_at[shift], z]
        return (
            pass_on(4 + 4 * block, ref, to_z_up),
            pass_on(5 + 4 * block, ref, to_z_down),
        )

    def spread_on(block, shift, copies):
        copies[0].wait_recv()
        first = pass_on(6 + 4 * block, feat.at[x_at[shift], z_down, low_rows], to_z_up)
        copies[1].wait_recv()
        second = pass_on(7 + 4 * block, feat.at[x_at[shift], z_up, high_rows], to_z_down)
        return first, second

    pages_out = []

    def push(source, target, send_sem, recv_sem, to_group, to):
        copy = remote(source, target, send_sem, recv_sem, to_group, to)
        copy.start()
        pages_out.append(copy)
        return copy

    def keep(source, target, sem):
        copy = pltpu.make_async_copy(source, target, sem)
        copy.start()
        kept.append(copy)

    def slots(shift):
        return pl.ds(2 * group_at(shift), 2)

    def heads(step):
        return pl.ds(2 * x_at[step], 2)

    def keys_first(shift):
        return push(
            pool_k.at[slots(shift)],
            stage_k.at[shift],
            y_send.at[0, shift],
            y_recv.at[0, shift],
            group_at(shift),
            tensor,
        )

    def keys_second(shift):
        for step in (1, 3, 2, 0):
            if shift == 0:
                source = pool_k.at[slots(0), heads(step)]
            else:
                source = stage_k.at[shift, :, heads(step)]
            target = got_k.at[pl.ds(2 * (step * GROUPS + shift), 2)]
            if step == 0:
                keep(source, target, keep_sem.at[0, shift])
            else:
                keys_last.append(
                    push(
                        source,
                        target,
                        x_send.at[0, shift, step],
                        x_recv.at[0, shift, step],
                        group,
                        x_at[step] * 4 + z,
                    )
                )

    def values_first(step):
        return push(
            pool_v.at[:, heads(step)],
            stage_v.at[step],
            v_send.at[step],
            v_recv.at[step],
            group,
            x_at[step] * 4 + z,
        )

    def values_second(step):
        for shift in (1, 2, 6, 3, 7, 4, 5, 0):
            if step == 0:
                source = pool_v.at[slots(shift), heads(0)]
            else:
                source = stage_v.at[step, slots(shift)]
            target = got_v.at[pl.ds(2 * (step * GROUPS + shift), 2)]
            if shift == 0:
                keep(source, target, keep_sem.at[1, step])
            else:
                keys_last.append(
                    push(
                        source,
                        target,
                        x_send.at[1, shift, step],
                        x_recv.at[1, shift, step],
                        group_at(shift),
                        tensor,
                    )
                )

    keys_last = []
    f0 = pass_on(0, feat.at[x, z], to_x_up)
    f1 = pass_on(1, feat.at[x, z], to_x_down)
    s0 = spread(0, 0)
    key_first = {shift: keys_first(shift) for shift in (1, 2, 6, 3, 7, 4, 5)}
    f0.wait_recv()
    f2 = pass_on(2, feat.at[x_at[3], z, low_rows], to_x_up)
    s1 = spread(1, 3)
    f1.wait_recv()
    f3 = pass_on(3, feat.at[x_at[1], z, high_rows], to_x_down)
    s2 = spread(2, 1)
    prefix = [prefix_ref[conv_ref[group * CONVS + i]] for i in range(CONVS)]
    suffix = [suffix_ref[conv_ref[group * CONVS + i]] for i in range(CONVS)]

    offsets = row_iota((SUF, HD))
    positions = jnp.concatenate([offsets + prefix[i] for i in range(CONVS)], axis=0)
    angle = positions.astype(F32) * freq_ref[...]
    cosine = jnp.cos(angle)
    sine = jnp.sin(angle)
    sine = jnp.where(lane_iota((ROWS, HD)) < HD // 2, -sine, sine)

    f2.wait_recv()
    f3.wait_recv()
    s3 = spread(3, 2)
    value_first = {step: values_first(step) for step in (1, 3, 2)}
    keys_second(0)
    values_second(0)
    key_first[1].wait_recv()
    keys_second(1)
    r0 = spread_on(0, 0, s0)

    page_ids = lane_iota((1, PAGES))
    below = (row_iota((PAGES, PAGES)) < lane_iota((PAGES, PAGES))).astype(F32)
    lane = lane_iota((LIST, HD))
    place_id = row_iota((LIST, PAGES)).astype(F32)
    row_id = row_iota((LIST, 1)).astype(F32)
    codes = jnp.zeros((LIST, 1), F32)
    block_conv = jnp.zeros((LIST, 1), F32)
    block_first = jnp.zeros((LIST, 1), F32)
    last_block = jnp.zeros((LIST, 1), F32)
    has_block = jnp.zeros((LIST, 1), F32)
    begin = jnp.zeros((1, 1), F32)
    for i in range(CONVS):
        entry = table_ref[pl.ds(conv_ref[group * CONVS + i], 1), :]
        source = entry >> 4
        source_y, source_core = source >> 5, (source >> 4) & 1
        source_x, source_z = (source >> 2) & 3, source & 3
        live = jnp.clip(prefix[i] - page_ids * PAGE, 0, PAGE)
        here = (source_z == z) & (live > 0)
        where = ((x - source_x) & 3) * GROUPS
        where = where + ((y - source_y) & 3) * 2 + ((core - source_core) & 1)
        value = ((where * 2 + (entry & 1)) * 128 + live).astype(F32)
        here_f = here.astype(F32)
        order = jnp.dot(
            jnp.broadcast_to(here_f, (8, PAGES)), below, preferred_element_type=F32
        )[0:1, :]
        count = jnp.sum(here_f, axis=1, keepdims=True)
        blocks = jnp.floor((count + (STEP - 1)) * (1.0 / STEP))
        match = (order + begin * STEP == place_id) & (
            jnp.broadcast_to(here_f, (LIST, PAGES)) > 0.5
        )
        codes = codes + jnp.sum(jnp.where(match, value, 0.0), axis=1, keepdims=True)
        block_first = jnp.where(row_id == begin, 1.0, block_first)
        begin = begin + blocks
        if i < CONVS - 1:
            block_conv = block_conv + jnp.where(row_id >= begin, 1.0, 0.0)
        last_block = jnp.where(row_id == i, jnp.maximum(begin - 1.0, 0.0), last_block)
        has_block = jnp.where(row_id == i, jnp.minimum(count, 1.0), has_block)
    table = jnp.zeros((LIST, HD), F32)
    for column, data in enumerate((codes, block_conv, block_first, last_block, has_block)):
        table = jnp.where(lane == column, data, table)
    table_out[...] = table.astype(I32)
    list_copy = pltpu.make_async_copy(table_out, lists, load_sem.at[4])
    list_copy.start()

    def find(to, carry):
        target = group * TENSOR + to
        index = jnp.int32(0)
        found = jnp.int32(0)
        for slot in range(GROUPS * CONVS):
            hit = dest_ref[conv_ref[slot]] == target
            index = jnp.where(hit, slot, index)
            found = jnp.where(hit, 1, found)
        chosen[0, to] = index
        chosen[1, to] = found
        return carry

    for load in loads:
        load.wait()
    load_out = pltpu.make_async_copy(w_out, weights, load_sem.at[5])
    load_out.start()
    gain[...] = gain_ref[...].astype(F32).reshape(1, WIDTH)
    query_bias = b_query[...].astype(F32).reshape(1, HEADS * HD)
    acc_q[...] = jnp.zeros_like(acc_q)
    acc_kv[...] = jnp.zeros_like(acc_kv)
    squares[...] = jnp.zeros_like(squares)

    def project(bz):
        def one(bx, carry):
            block = bx * 4 + bz
            rows = pl.ds(pl.multiple_of(block * PART, PART), PART)
            wide = feat[bx, bz].astype(F32)
            scaled = (wide * gain[:, rows]).astype(BF16)
            acc_q[...] += jnp.dot(scaled, wq[rows, :], preferred_element_type=F32)
            acc_kv[...] += lax.dot_general(
                scaled,
                wkv[:, rows],
                (((1,), (1,)), ((), ())),
                preferred_element_type=F32,
            )
            wide = wide * wide
            total = squares[...]
            for part in range(PART // HD):
                total = total + wide[:, part * HD : (part + 1) * HD]
            squares[...] = total
            return carry

        lax.fori_loop(0, 4, one, 0)

    project(z)
    lax.fori_loop(0, TENSOR, find, 0)
    r1 = spread_on(1, 3, s1)
    r2 = spread_on(2, 1, s2)
    for shift in (2, 6, 3, 7, 4, 5):
        key_first[shift].wait_recv()
        keys_second(shift)
    r3 = spread_on(3, 2, s3)
    project(z_up)
    project(z_down)
    for step in (1, 3, 2):
        value_first[step].wait_recv()
        values_second(step)
    for copies in (r0, r1, r2, r3):
        for copy in copies:
            copy.wait_recv()
    project(z_far)
    mean = jnp.sum(squares[...], axis=1, keepdims=True) * (1.0 / WIDTH)
    factor = lax.rsqrt(mean + EPSILON)
    bias = jnp.concatenate(
        [ref[...].astype(F32).reshape(1, HD // 2) for ref in (b_key, b_value)], axis=1
    )
    kv_own[...] = (acc_kv[...] * factor + bias).astype(BF16)
    kv_copy = remote(
        kv_own,
        kv_other,
        pair_send.at[0],
        pair_recv.at[0],
        group,
        x * 4 + partner_z[1],
    )
    kv_copy.start()

    def rotate(values):
        return values * cosine + pltpu.roll(values, HD // 2, 1) * sine

    for head in range(HEADS):
        columns = slice(head * HD, (head + 1) * HD)
        values = acc_q[:, columns] * factor + query_bias[:, columns]
        values = rotate(values).astype(BF16)
        for i in range(CONVS):
            queries[0, i, head * SUF : (head + 1) * SUF, :] = values[i * SUF : (i + 1) * SUF, :]
    query_out = [
        remote(
            queries.at[0],
            queries.at[r],
            pair_send.at[r],
            pair_recv.at[r],
            group,
            x * 4 + partner_z[r],
        )
        for r in (1, 2, 3)
    ]
    for copy in query_out:
        copy.start()

    kv_copy.wait_recv()
    mine = kv_own[...].astype(F32)
    theirs = kv_other[...].astype(F32)
    even = jnp.where(parity == 0, mine, theirs)
    odd = jnp.where(parity == 0, theirs, mine)
    low = lane_iota((ROWS, HD)) < HD // 2
    keys = jnp.where(low, even, pltpu.roll(odd, HD // 2, 1))
    keys = rotate(keys)
    values = jnp.where(low, pltpu.roll(even, HD // 2, 1), odd)
    key_new[...] = keys.astype(BF16)
    value_new[...] = values.astype(BF16)

    page = jnp.where(parity == 0, keys.astype(BF16).astype(F32), values)
    live_row = jnp.concatenate([offsets < suffix[i] for i in range(CONVS)], axis=0)
    page = jnp.where(live_row, page, 0.0).astype(BF16)
    new_ref = new_all.at[pl.ds(group * CONVS, CONVS)]
    new_ref[...] = page.reshape(CONVS, SUF, HD)
    group_out = [
        remote(
            new_ref,
            new_ref,
            group_send.at[shift],
            group_recv.at[shift],
            group_at(shift),
            tensor,
        )
        for shift in range(1, GROUPS)
    ]
    for copy in group_out:
        copy.start()

    half = HEADS * SUF
    own_head = lax.div(z, 2)

    def score(keys, query):
        return lax.dot_general(
            keys, query, (((1,), (1,)), ((), ())), preferred_element_type=F32
        )

    def mix(values, shares):
        return lax.dot_general(
            values,
            shares.astype(BF16),
            (((0,), (0,)), ((), ())),
            preferred_element_type=F32,
        )

    causal = row_iota((SUF, half)) <= (lane_iota((SUF, half)) & (SUF - 1))
    for i in range(CONVS):
        rows = slice(i * SUF, (i + 1) * SUF)
        scores = score(key_new[rows], queries[0, i])
        scores = jnp.where(causal, scores * SCALE, NEGATIVE)
        peak = jnp.max(scores, axis=0, keepdims=True)
        shares = jnp.exp2(scores - peak)
        own_accum[i] = mix(value_new[rows], shares)
        own_stats[i, 0:1, :] = peak
        own_stats[i, 1:2, :] = jnp.sum(shares, axis=0, keepdims=True)
    list_copy.wait()
    for copy in query_out + keys_last:
        copy.wait_recv()
    for copy in kept:
        copy.wait()

    token = row_iota((PAGE, half))

    def attend(head, sides, width):
        def pack(index, state):
            blocks = [index * width + k for k in range(width)]
            codes = [[lists[b * STEP + p, 0] for p in range(STEP)] for b in blocks]
            convs = [jnp.clip(lists[b, 1], 0, CONVS - 1) for b in blocks]
            spots = [[jnp.clip(code >> 7, 0, PAGES - 1) for code in row] for row in codes]
            firsts = [lists[b, 2] == 1 for b in blocks]
            keys = [
                jnp.concatenate([got_k[spot, head] for spot in row], axis=0)
                for row in spots
            ]
            values = [
                jnp.concatenate([got_v[spot, head] for spot in row], axis=0)
                for row in spots
            ]
            pairs = [(k, s) for k in range(width) for s in range(len(sides))]
            scores = {
                (k, s): score(keys[k], queries[sides[s], convs[k]]) for k, s in pairs
            }
            for k, s in pairs:
                scores[k, s] = jnp.concatenate(
                    [
                        jnp.where(
                            token < (codes[k][p] & 127),
                            scores[k, s][p * PAGE : (p + 1) * PAGE] * SCALE,
                            NEGATIVE,
                        )
                        for p in range(STEP)
                    ],
                    axis=0,
                )
            tops = {
                key: jnp.max(value, axis=0, keepdims=True) for key, value in scores.items()
            }
            state = list(state)
            fresh, shrink = {}, {}
            for s in range(len(sides)):
                peak = state[s][0]
                for k in range(width):
                    peak = jnp.where(firsts[k], NEGATIVE, peak)
                    fresh[k, s] = jnp.maximum(peak, tops[k, s])
                    shrink[k, s] = jnp.exp2(peak - fresh[k, s])
                    peak = fresh[k, s]
            shares = {key: jnp.exp2(scores[key] - fresh[key]) for key in pairs}
            sums = {key: jnp.sum(shares[key], axis=0, keepdims=True) for key in pairs}
            mixes = {(k, s): mix(values[k], shares[k, s]) for k, s in pairs}
            for s, side in enumerate(sides):
                peak, total, accum = state[s]
                for k in range(width):
                    total = total * shrink[k, s] + sums[k, s]
                    accum = accum * shrink[k, s] + mixes[k, s]
                    accums[side, blocks[k]] = accum
                    stats[side, blocks[k], 0:1, :] = fresh[k, s]
                    stats[side, blocks[k], 1:2, :] = total
                state[s] = (fresh[width - 1, s], total, accum)
            return tuple(state)

        empty = (
            jnp.full((1, half), NEGATIVE, F32),
            jnp.zeros((1, half), F32),
            jnp.zeros((HD, half), F32),
        )
        lax.fori_loop(0, BLOCKS // width, pack, tuple(empty for _ in sides))

    def result(side, i):
        last = jnp.clip(lists[i, 3], 0, BLOCKS - 1)
        some = lists[i, 4] == 1
        peak = jnp.where(some, stats[side, last, 0:1, :], NEGATIVE)
        total = jnp.where(some, stats[side, last, 1:2, :], 0.0)
        accum = accums[side, last] * jnp.where(some, 1.0, 0.0)
        return peak, total, accum

    def send(side):
        for i in range(CONVS):
            peak, total, accum = result(side, i)
            safe = jnp.where(total > 0.0, total, 1.0)
            mixed_out[side, i] = (accum * (1.0 / safe)).astype(BF16)
            lse = jnp.where(total > 0.0, peak + jnp.log(safe) * (1.0 / LN2), NEGATIVE)
            lse_out[side, i] = jnp.broadcast_to(lse, (8, half))
        copies = [
            remote(
                source.at[side],
                target.at[side],
                send_sem.at[side],
                recv_sem.at[side],
                group,
                x * 4 + partner_z[side],
            )
            for source, target, send_sem, recv_sem in (
                (mixed_out, mixed_got, mixed_send, mixed_recv),
                (lse_out, lse_got, lse_send, lse_recv),
            )
        ]
        for copy in copies:
            copy.start()
        return copies

    attend(1 - own_head, (2,), 10)
    exchanged = send(2)
    attend(1 - own_head, (3,), 10)
    exchanged = exchanged + send(3)

    attend(own_head, (1,), 10)
    exchanged = exchanged + send(1)

    for copy in group_out:
        copy.wait_recv()

    def choose(to, carry):
        page = new_all[jnp.clip(chosen[0, to], 0, GROUPS * CONVS - 1)].astype(F32)
        new_send[to] = (page * chosen[1, to].astype(F32)).astype(BF16)
        return carry

    lax.fori_loop(0, TENSOR, choose, 0)
    mine_copy = pltpu.make_async_copy(
        new_send.at[tensor], new_pages.at[tensor], load_sem.at[6]
    )
    mine_copy.start()

    def page_copy(off):
        to = lax.rem(tensor + off, TENSOR)
        return remote(
            new_send.at[to],
            new_pages.at[tensor],
            page_send.at[off],
            page_recv.at[off],
            group,
            to,
        )

    def page_start(off, carry):
        page_copy(off).start()
        return carry

    lax.fori_loop(1, TENSOR, page_start, 0)
    attend(own_head, (0,), 10)
    for copy in exchanged:
        copy.wait_recv()
    row_of = lane_iota((1, half)) & (SUF - 1)

    def combine(i):
        peak, total, accum = result(0, i)
        own_peak = own_stats[i, 0:1, :]
        logs = [lse_got[r, i, 0:1, :] for r in (1, 2, 3)]
        top = jnp.maximum(
            jnp.maximum(peak, own_peak), jnp.maximum(jnp.maximum(logs[0], logs[1]), logs[2])
        )
        shares = [jnp.exp2(log - top) for log in logs]
        first, second = jnp.exp2(peak - top), jnp.exp2(own_peak - top)
        total = total * first + own_stats[i, 1:2, :] * second
        total = total + shares[0] + shares[1] + shares[2]
        scale = jnp.where(row_of < suffix_ref[conv_ref[group * CONVS + i]], 1.0, 0.0) / total
        joined = accum * (first * scale) + own_accum[i] * (second * scale)
        for r in (1, 2, 3):
            joined = joined + mixed_got[r, i].astype(F32) * (shares[r - 1] * scale)
        turned = jnp.transpose(joined).astype(BF16)
        for head in range(HEADS):
            mixed[i * SUF : (i + 1) * SUF, head * HD : (head + 1) * HD] = turned[
                head * SUF : (head + 1) * SUF, :
            ]

    pending = []

    class Ring:
        def __init__(self, side, first, pick, buffers, way):
            self.side, self.first, self.pick, self.buffers = side, first, pick, buffers
            self.up, self.down, self.me, self.far, self.to_up, self.to_down = way
            self.top = pl.ds(side * 2 * SUF, SUF)
            self.bottom = pl.ds(side * 2 * SUF + SUF, SUF)

        def send(self, index, ref, to):
            sem = self.first + index
            copy = remote(
                ref,
                self.buffers.at[self.side, index],
                ring_send.at[sem],
                ring_recv.at[sem],
                group,
                to,
            )
            copy.start()
            pending.append(copy)
            return copy

        def start_far(self):
            pick = self.pick
            self.c0 = self.send(0, pick(self.far, self.top), self.to_up)
            self.c1 = self.send(1, pick(self.far, self.bottom), self.to_down)

        def start_near(self):
            pick = self.pick
            self.c2 = self.send(2, pick(self.up, self.bottom), self.to_up)
            self.c3 = self.send(3, pick(self.down, self.top), self.to_down)

        def add(self, ref, *indices):
            total = ref[...].astype(F32)
            for index in indices:
                total = total + self.buffers[self.side, index].astype(F32)
            ref[...] = total.astype(BF16)

        def relay(self):
            pick = self.pick
            self.c0.wait_recv()
            self.add(pick(self.up, self.top), 0)
            self.c4 = self.send(4, pick(self.up, self.top), self.to_up)
            self.c1.wait_recv()
            self.add(pick(self.down, self.bottom), 1)
            self.c5 = self.send(5, pick(self.down, self.bottom), self.to_down)

        def finish(self):
            pick = self.pick
            self.c3.wait_recv()
            self.c4.wait_recv()
            self.add(pick(self.me, self.top), 3, 4)
            self.c2.wait_recv()
            self.c5.wait_recv()
            self.add(pick(self.me, self.bottom), 2, 5)

    along_x = (x_up, x_down, x, x_far, to_x_up, to_x_down)
    along_z = (z_up, z_down, z, z_far, to_z_up, to_z_down)
    firsts = (
        Ring(0, 0, lambda j, rows: part.at[j, :, rows], big, along_x),
        Ring(1, 6, lambda j, rows: part.at[:, j, rows], big, along_z),
    )
    seconds = (
        Ring(0, 12, lambda j, rows: part.at[x, j, rows], small, along_z),
        Ring(1, 18, lambda j, rows: part.at[j, z, rows], small, along_x),
    )

    def out_block(bx, bz):
        columns = pl.ds(pl.multiple_of((bx * 4 + bz) * PART, PART), PART)
        part[bx, bz] = jnp.dot(
            mixed[...], weights[:, columns], preferred_element_type=F32
        ).astype(BF16)

    def project_many(pairs):
        for bx, bz in pairs:
            out_block(bx, bz)

    for i in range(CONVS):
        combine(i)
    load_out.wait()
    project_many([(x_far, bz) for bz in (z_far, z_up, z_down, z)])
    firsts[0].start_far()
    project_many([(bx, z_far) for bx in (x_up, x_down, x)])
    firsts[1].start_far()
    project_many([(x_up, z_up), (x_up, z_down), (x_up, z)])
    project_many([(x_down, z_up), (x_down, z_down), (x_down, z)])
    firsts[0].start_near()
    project_many([(x, z_up), (x, z_down), (x, z)])
    firsts[1].start_near()
    firsts[0].relay()
    firsts[1].relay()
    for first, second in zip(firsts, seconds):
        first.finish()
        second.start_far()
        second.start_near()
    seconds[0].relay()
    seconds[1].relay()
    seconds[0].finish()
    seconds[1].finish()
    out_ref[...] = part[x, z]
    for copy in exchanged + pending + sent + pages_out + group_out + query_out + [kv_copy]:
        copy.wait_send()
    mine_copy.wait()

    def page_end(off, carry):
        page_copy(off).wait()
        return carry

    lax.fori_loop(1, TENSOR, page_end, 0)


def place_kernel(part_out, pages, attn_out, new_keys, new_values):
    attn_out[...] = part_out[...]
    new_keys[0] = pages[:, 0]
    new_values[0] = pages[:, 1]


def any_spec():
    return pl.BlockSpec(memory_space=pl.ANY)


def vmem_spec():
    return pl.BlockSpec(memory_space=pltpu.VMEM)


def smem_spec():
    return pl.BlockSpec(memory_space=pltpu.SMEM)


def shards(
    hidden_states,
    norm_gain,
    w_query,
    b_query,
    w_key,
    b_key,
    w_value,
    b_value,
    w_out,
    pool_keys,
    pool_values,
    conv_slots,
    page_table,
    prefix_len,
    suffix_len,
    new_dest,
):
    dma = pltpu.SemaphoreType.DMA
    freq = THETA ** (-(np.arange(HD // 2, dtype=np.float64) * 2.0 / HD))
    freq = jnp.asarray(np.concatenate([freq, freq])[None, :], F32)
    shape = jax.ShapeDtypeStruct
    attn_out, new_pages = pl.pallas_call(
        layer_kernel,
        out_shape=[shape((ROWS, PART), BF16), shape((TENSOR, SUF, HD), BF16)],
        in_specs=[smem_spec()] * 4
        + [vmem_spec()]
        + [any_spec()] * 7
        + [vmem_spec()] * 5,
        out_specs=[vmem_spec(), any_spec()],
        scratch_shapes=[
            pltpu.VMEM((4, 4, ROWS, PART), BF16),
            pltpu.VMEM((WIDTH, HEADS * HD), BF16),
            pltpu.VMEM((HD, WIDTH), BF16),
            pltpu.VMEM((ROWS, HEADS * HD), F32),
            pltpu.VMEM((ROWS, HD), F32),
            pltpu.VMEM((ROWS, HD), F32),
            pltpu.VMEM((GROUPS, 2, 8, PAGE, HD), BF16),
            pltpu.VMEM((4, 2 * GROUPS, 2, PAGE, HD), BF16),
            pltpu.VMEM((PAGES, 2, PAGE, HD), BF16),
            pltpu.VMEM((PAGES, 2, PAGE, HD), BF16),
            pltpu.VMEM((4, CONVS, HEADS * SUF, HD), BF16),
            pltpu.VMEM((ROWS, HD), BF16),
            pltpu.VMEM((ROWS, HD), BF16),
            pltpu.VMEM((ROWS, HD), BF16),
            pltpu.VMEM((ROWS, HD), BF16),
            pltpu.VMEM((GROUPS * CONVS, SUF, HD), BF16),
            pltpu.VMEM((LIST, HD), I32),
            pltpu.SMEM((LIST, HD), I32),
            pltpu.SMEM((2, TENSOR), I32),
            pltpu.VMEM((1, WIDTH), F32),
            pltpu.VMEM((HEADS * HD, WIDTH), BF16),
            pltpu.VMEM((4, BLOCKS, HD, HEADS * SUF), F32),
            pltpu.VMEM((4, BLOCKS, 8, HEADS * SUF), F32),
            pltpu.VMEM((CONVS, HD, HEADS * SUF), F32),
            pltpu.VMEM((CONVS, 8, HEADS * SUF), F32),
            pltpu.VMEM((4, CONVS, HD, HEADS * SUF), BF16),
            pltpu.VMEM((4, CONVS, 8, HEADS * SUF), F32),
            pltpu.VMEM((4, CONVS, HD, HEADS * SUF), BF16),
            pltpu.VMEM((4, CONVS, 8, HEADS * SUF), F32),
            pltpu.VMEM((ROWS, HEADS * HD), BF16),
            pltpu.VMEM((4, 4, ROWS, PART), BF16),
            pltpu.VMEM((2, 6, 4, SUF, PART), BF16),
            pltpu.VMEM((2, 6, SUF, PART), BF16),
            pltpu.VMEM((TENSOR, SUF, HD), BF16),
            dma((8,)),
            dma((2, GROUPS)),
            dma((20,)),
            dma((20,)),
            dma((2, GROUPS)),
            dma((2, GROUPS)),
            dma((2, GROUPS, 4)),
            dma((2, GROUPS, 4)),
            dma((4,)),
            dma((4,)),
            dma((4,)),
            dma((4,)),
            dma((GROUPS,)),
            dma((GROUPS,)),
            dma((4,)),
            dma((4,)),
            dma((4,)),
            dma((4,)),
            dma((24,)),
            dma((24,)),
            dma((TENSOR,)),
            dma((TENSOR,)),
        ],
        compiler_params=pltpu.CompilerParams(
            collective_id=0, has_side_effects=True, vmem_limit_bytes=62 * 1024 * 1024
        ),
        name="layer",
    )(
        conv_slots,
        prefix_len,
        suffix_len,
        new_dest,
        page_table,
        hidden_states,
        pool_keys,
        pool_values,
        w_query,
        w_key.T,
        w_value.T,
        w_out,
        norm_gain,
        b_query,
        b_key,
        b_value,
        freq,
    )
    page_shape = shape((1, TENSOR // 2, SUF, HD), BF16)
    return pl.pallas_call(
        place_kernel,
        out_shape=[shape((ROWS, PART), BF16), page_shape, page_shape],
        in_specs=[vmem_spec()] * 2,
        out_specs=[vmem_spec()] * 3,
        compiler_params=pltpu.CompilerParams(vmem_limit_bytes=62 * 1024 * 1024),
        name="place",
    )(attn_out, new_pages.reshape(TENSOR // 2, 2, SUF, HD))


def solution(mesh):
    in_specs = (
        P("group", "tensor"),
        P(),
        P(None, "tensor"),
        P("tensor"),
        P(None, "tensor"),
        P("tensor"),
        P(None, "tensor"),
        P("tensor"),
        P("tensor", None),
        P(("group", "tensor"), None, None, None),
        P(("group", "tensor"), None, None, None),
        P(),
        P(),
        P(),
        P(),
        P(),
    )
    out_specs = (
        P("group", "tensor"),
        P(("group", "tensor"), None, None, None),
        P(("group", "tensor"), None, None, None),
    )
    return jax.shard_map(shards, mesh=mesh, in_specs=in_specs, out_specs=out_specs, check_vma=False)
```

```python
import jax
import jax.numpy as jnp
import numpy as np
from jax import lax
from jax.experimental import pallas as pl
from jax.experimental.pallas import tpu as pltpu
from jax.sharding import PartitionSpec as P

HD = 128
SUF = 64
CONVS = 4
ROWS = CONVS * SUF
GROUPS = 8
TENSOR = 16
WIDTH = 8192
PART = WIDTH // TENSOR
PAGES = 64
PAGE = 64
HEADS = 4
THETA = 1000000.0
EPSILON = 1e-06
NEGATIVE = -1e30
SCALE = HD**-0.5 * 1.4426950408889634
STEP = 4
BLOCKS = 20
LIST = 80
LN2 = 0.6931471805599453
MESH = pl.DeviceIdType.MESH
BF16 = jnp.bfloat16
F32 = jnp.float32
I32 = jnp.int32


def remote(src, dst, send_sem, recv_sem, group, tensor):
    return pltpu.make_async_remote_copy(
        src_ref=src,
        dst_ref=dst,
        send_sem=send_sem,
        recv_sem=recv_sem,
        device_id=(group, tensor),
        device_id_type=MESH,
    )


def place():
    group = lax.axis_index("group")
    tensor = lax.axis_index("tensor")
    return (
        group,
        tensor,
        lax.div(group, 2),
        lax.rem(group, 2),
        lax.div(tensor, 4),
        lax.rem(tensor, 4),
    )


def lane_iota(shape):
    return lax.broadcasted_iota(I32, shape, len(shape) - 1)


def row_iota(shape):
    return lax.broadcasted_iota(I32, shape, len(shape) - 2)


def layer_kernel(
    conv_ref,
    prefix_ref,
    suffix_ref,
    dest_ref,
    table_ref,
    hidden,
    pool_k,
    pool_v,
    w_query,
    w_key,
    w_value,
    w_out,
    gain_ref,
    b_query,
    b_key,
    b_value,
    freq_ref,
    out_ref,
    new_pages,
    feat,
    wq,
    wkv,
    acc_q,
    acc_kv,
    squares,
    stage_k,
    stage_v,
    got_k,
    got_v,
    queries,
    key_new,
    value_new,
    kv_own,
    kv_other,
    new_all,
    table_out,
    lists,
    chosen,
    gain,
    weights,
    accums,
    stats,
    own_accum,
    own_stats,
    mixed_out,
    lse_out,
    mixed_got,
    lse_got,
    mixed,
    part,
    big,
    small,
    new_send,
    load_sem,
    keep_sem,
    feat_send,
    feat_recv,
    y_send,
    y_recv,
    x_send,
    x_recv,
    v_send,
    v_recv,
    pair_send,
    pair_recv,
    group_send,
    group_recv,
    mixed_send,
    mixed_recv,
    lse_send,
    lse_recv,
    ring_send,
    ring_recv,
    page_send,
    page_recv,
):
    group, tensor, y, core, x, z = place()
    parity = lax.rem(z, 2)
    partner_z = [z, z + 1 - 2 * parity, lax.rem(z + 2, 4), 3 - z]
    own = pltpu.make_async_copy(hidden, feat.at[x, z], load_sem.at[0])
    own.start()
    loads = [
        pltpu.make_async_copy(w_query, wq, load_sem.at[1]),
        pltpu.make_async_copy(w_key, wkv.at[pl.ds(0, HD // 2)], load_sem.at[2]),
        pltpu.make_async_copy(w_value, wkv.at[pl.ds(HD // 2, HD // 2)], load_sem.at[3]),
    ]
    for load in loads:
        load.start()

    def group_at(shift):
        to_y = lax.rem(y + shift // 2, 4)
        to_core = lax.rem(core + shift % 2, 2)
        return to_y * 2 + to_core

    barrier = pltpu.get_barrier_semaphore()
    for shift in range(1, GROUPS):
        pl.semaphore_signal(
            barrier, inc=1, device_id=(group_at(shift), tensor), device_id_type=MESH
        )

    def greet(off, carry):
        to = lax.rem(tensor + off, TENSOR)
        pl.semaphore_signal(barrier, inc=1, device_id=(group, to), device_id_type=MESH)
        return carry

    lax.fori_loop(1, TENSOR, greet, 0)
    pl.semaphore_wait(barrier, GROUPS - 1 + TENSOR - 1)

    own.wait()
    x_at = [lax.rem(x + shift, 4) for shift in range(4)]
    x_up, x_far, x_down = x_at[1:]
    z_up, z_far, z_down = (lax.rem(z + shift, 4) for shift in (1, 2, 3))
    to_x_up, to_x_down = x_at[1] * 4 + z, x_at[3] * 4 + z
    to_z_up, to_z_down = x * 4 + z_up, x * 4 + z_down
    half_rows = ROWS // 2
    low_rows, high_rows = pl.ds(0, half_rows), pl.ds(half_rows, half_rows)
    sent, kept = [], []

    def pass_on(index, ref, to):
        copy = remote(ref, ref, feat_send.at[index], feat_recv.at[index], group, to)
        copy.start()
        sent.append(copy)
        return copy

    def spread(block, shift):
        ref = feat.at[x_at[shift], z]
        return (
            pass_on(4 + 4 * block, ref, to_z_up),
            pass_on(5 + 4 * block, ref, to_z_down),
        )

    def spread_on(block, shift, copies):
        copies[0].wait_recv()
        first = pass_on(6 + 4 * block, feat.at[x_at[shift], z_down, low_rows], to_z_up)
        copies[1].wait_recv()
        second = pass_on(7 + 4 * block, feat.at[x_at[shift], z_up, high_rows], to_z_down)
        return first, second

    pages_out = []

    def push(source, target, send_sem, recv_sem, to_group, to):
        copy = remote(source, target, send_sem, recv_sem, to_group, to)
        copy.start()
        pages_out.append(copy)
        return copy

    def keep(source, target, sem):
        copy = pltpu.make_async_copy(source, target, sem)
        copy.start()
        kept.append(copy)

    def slots(shift):
        return pl.ds(2 * group_at(shift), 2)

    def heads(step):
        return pl.ds(2 * x_at[step], 2)

    def keys_first(shift):
        return push(
            pool_k.at[slots(shift)],
            stage_k.at[shift],
            y_send.at[0, shift],
            y_recv.at[0, shift],
            group_at(shift),
            tensor,
        )

    def keys_second(shift):
        for step in (1, 3, 2, 0):
            if shift == 0:
                source = pool_k.at[slots(0), heads(step)]
            else:
                source = stage_k.at[shift, :, heads(step)]
            target = got_k.at[pl.ds(2 * (step * GROUPS + shift), 2)]
            if step == 0:
                keep(source, target, keep_sem.at[0, shift])
            else:
                keys_last.append(
                    push(
                        source,
                        target,
                        x_send.at[0, shift, step],
                        x_recv.at[0, shift, step],
                        group,
                        x_at[step] * 4 + z,
                    )
                )

    def values_first(step):
        return push(
            pool_v.at[:, heads(step)],
            stage_v.at[step],
            v_send.at[step],
            v_recv.at[step],
            group,
            x_at[step] * 4 + z,
        )

    def values_second(step):
        for shift in (1, 2, 6, 3, 7, 4, 5, 0):
            if step == 0:
                source = pool_v.at[slots(shift), heads(0)]
            else:
                source = stage_v.at[step, slots(shift)]
            target = got_v.at[pl.ds(2 * (step * GROUPS + shift), 2)]
            if shift == 0:
                keep(source, target, keep_sem.at[1, step])
            else:
                keys_last.append(
                    push(
                        source,
                        target,
                        x_send.at[1, shift, step],
                        x_recv.at[1, shift, step],
                        group_at(shift),
                        tensor,
                    )
                )

    keys_last = []
    f0 = pass_on(0, feat.at[x, z], to_x_up)
    f1 = pass_on(1, feat.at[x, z], to_x_down)
    s0 = spread(0, 0)
    key_first = {shift: keys_first(shift) for shift in (1, 2, 6, 3, 7, 4, 5)}
    f0.wait_recv()
    f2 = pass_on(2, feat.at[x_at[3], z, low_rows], to_x_up)
    s1 = spread(1, 3)
    f1.wait_recv()
    f3 = pass_on(3, feat.at[x_at[1], z, high_rows], to_x_down)
    s2 = spread(2, 1)
    value_first = {step: values_first(step) for step in (1, 3, 2)}
    prefix = [prefix_ref[conv_ref[group * CONVS + i]] for i in range(CONVS)]
    suffix = [suffix_ref[conv_ref[group * CONVS + i]] for i in range(CONVS)]

    offsets = row_iota((SUF, HD))
    positions = jnp.concatenate([offsets + prefix[i] for i in range(CONVS)], axis=0)
    angle = positions.astype(F32) * freq_ref[...]
    cosine = jnp.cos(angle)
    sine = jnp.sin(angle)
    sine = jnp.where(lane_iota((ROWS, HD)) < HD // 2, -sine, sine)

    f2.wait_recv()
    f3.wait_recv()
    s3 = spread(3, 2)
    r0 = spread_on(0, 0, s0)

    page_ids = lane_iota((1, PAGES))
    below = (row_iota((PAGES, PAGES)) < lane_iota((PAGES, PAGES))).astype(F32)
    lane = lane_iota((LIST, HD))
    place_id = row_iota((LIST, PAGES)).astype(F32)
    row_id = row_iota((LIST, 1)).astype(F32)
    codes = jnp.zeros((LIST, 1), F32)
    block_conv = jnp.zeros((LIST, 1), F32)
    block_first = jnp.zeros((LIST, 1), F32)
    last_block = jnp.zeros((LIST, 1), F32)
    has_block = jnp.zeros((LIST, 1), F32)
    begin = jnp.zeros((1, 1), F32)
    for i in range(CONVS):
        entry = table_ref[pl.ds(conv_ref[group * CONVS + i], 1), :]
        source = entry >> 4
        source_y, source_core = source >> 5, (source >> 4) & 1
        source_x, source_z = (source >> 2) & 3, source & 3
        live = jnp.clip(prefix[i] - page_ids * PAGE, 0, PAGE)
        here = (source_z == z) & (live > 0)
        where = ((x - source_x) & 3) * GROUPS
        where = where + ((y - source_y) & 3) * 2 + ((core - source_core) & 1)
        value = ((where * 2 + (entry & 1)) * 128 + live).astype(F32)
        here_f = here.astype(F32)
        order = jnp.dot(
            jnp.broadcast_to(here_f, (8, PAGES)), below, preferred_element_type=F32
        )[0:1, :]
        count = jnp.sum(here_f, axis=1, keepdims=True)
        blocks = jnp.floor((count + (STEP - 1)) * (1.0 / STEP))
        match = (order + begin * STEP == place_id) & (
            jnp.broadcast_to(here_f, (LIST, PAGES)) > 0.5
        )
        codes = codes + jnp.sum(jnp.where(match, value, 0.0), axis=1, keepdims=True)
        block_first = jnp.where(row_id == begin, 1.0, block_first)
        begin = begin + blocks
        if i < CONVS - 1:
            block_conv = block_conv + jnp.where(row_id >= begin, 1.0, 0.0)
        last_block = jnp.where(row_id == i, jnp.maximum(begin - 1.0, 0.0), last_block)
        has_block = jnp.where(row_id == i, jnp.minimum(count, 1.0), has_block)
    table = jnp.zeros((LIST, HD), F32)
    for column, data in enumerate((codes, block_conv, block_first, last_block, has_block)):
        table = jnp.where(lane == column, data, table)
    table_out[...] = table.astype(I32)
    list_copy = pltpu.make_async_copy(table_out, lists, load_sem.at[4])
    list_copy.start()

    def find(to, carry):
        target = group * TENSOR + to
        index = jnp.int32(0)
        found = jnp.int32(0)
        for slot in range(GROUPS * CONVS):
            hit = dest_ref[conv_ref[slot]] == target
            index = jnp.where(hit, slot, index)
            found = jnp.where(hit, 1, found)
        chosen[0, to] = index
        chosen[1, to] = found
        return carry

    for load in loads:
        load.wait()
    load_out = pltpu.make_async_copy(w_out, weights, load_sem.at[5])
    load_out.start()
    gain[...] = gain_ref[...].astype(F32).reshape(1, WIDTH)
    query_bias = b_query[...].astype(F32).reshape(1, HEADS * HD)
    acc_q[...] = jnp.zeros_like(acc_q)
    acc_kv[...] = jnp.zeros_like(acc_kv)
    squares[...] = jnp.zeros_like(squares)

    def project(bz):
        def one(bx, carry):
            block = bx * 4 + bz
            rows = pl.ds(pl.multiple_of(block * PART, PART), PART)
            wide = feat[bx, bz].astype(F32)
            scaled = (wide * gain[:, rows]).astype(BF16)
            acc_q[...] += jnp.dot(scaled, wq[rows, :], preferred_element_type=F32)
            acc_kv[...] += lax.dot_general(
                scaled,
                wkv[:, rows],
                (((1,), (1,)), ((), ())),
                preferred_element_type=F32,
            )
            wide = wide * wide
            total = squares[...]
            for part in range(PART // HD):
                total = total + wide[:, part * HD : (part + 1) * HD]
            squares[...] = total
            return carry

        lax.fori_loop(0, 4, one, 0)

    project(z)
    lax.fori_loop(0, TENSOR, find, 0)
    r1 = spread_on(1, 3, s1)
    r2 = spread_on(2, 1, s2)
    r3 = spread_on(3, 2, s3)
    for shift in (1, 2, 6, 3, 7, 4, 5):
        key_first[shift].wait_recv()
    values_second(0)
    project(z_up)
    for step in (1, 3, 2):
        value_first[step].wait_recv()
        values_second(step)
    for shift in (0, 1, 2, 6, 3, 7, 4, 5):
        keys_second(shift)
    project(z_down)
    for copies in (r0, r1, r2, r3):
        for copy in copies:
            copy.wait_recv()
    project(z_far)
    mean = jnp.sum(squares[...], axis=1, keepdims=True) * (1.0 / WIDTH)
    factor = lax.rsqrt(mean + EPSILON)
    bias = jnp.concatenate(
        [ref[...].astype(F32).reshape(1, HD // 2) for ref in (b_key, b_value)], axis=1
    )
    kv_own[...] = (acc_kv[...] * factor + bias).astype(BF16)
    kv_copy = remote(
        kv_own,
        kv_other,
        pair_send.at[0],
        pair_recv.at[0],
        group,
        x * 4 + partner_z[1],
    )
    kv_copy.start()

    def rotate(values):
        return values * cosine + pltpu.roll(values, HD // 2, 1) * sine

    for head in range(HEADS):
        columns = slice(head * HD, (head + 1) * HD)
        values = acc_q[:, columns] * factor + query_bias[:, columns]
        values = rotate(values).astype(BF16)
        for i in range(CONVS):
            queries[0, i, head * SUF : (head + 1) * SUF, :] = values[i * SUF : (i + 1) * SUF, :]
    query_out = [
        remote(
            queries.at[0],
            queries.at[r],
            pair_send.at[r],
            pair_recv.at[r],
            group,
            x * 4 + partner_z[r],
        )
        for r in (1, 2, 3)
    ]
    for copy in query_out:
        copy.start()

    kv_copy.wait_recv()
    mine = kv_own[...].astype(F32)
    theirs = kv_other[...].astype(F32)
    even = jnp.where(parity == 0, mine, theirs)
    odd = jnp.where(parity == 0, theirs, mine)
    low = lane_iota((ROWS, HD)) < HD // 2
    keys = jnp.where(low, even, pltpu.roll(odd, HD // 2, 1))
    keys = rotate(keys)
    values = jnp.where(low, pltpu.roll(even, HD // 2, 1), odd)
    key_new[...] = keys.astype(BF16)
    value_new[...] = values.astype(BF16)

    page = jnp.where(parity == 0, keys.astype(BF16).astype(F32), values)
    live_row = jnp.concatenate([offsets < suffix[i] for i in range(CONVS)], axis=0)
    page = jnp.where(live_row, page, 0.0).astype(BF16)
    new_ref = new_all.at[pl.ds(group * CONVS, CONVS)]
    new_ref[...] = page.reshape(CONVS, SUF, HD)
    group_out = [
        remote(
            new_ref,
            new_ref,
            group_send.at[shift],
            group_recv.at[shift],
            group_at(shift),
            tensor,
        )
        for shift in range(1, GROUPS)
    ]
    for copy in group_out:
        copy.start()

    half = HEADS * SUF
    own_head = lax.div(z, 2)

    def score(keys, query):
        return lax.dot_general(
            keys, query, (((1,), (1,)), ((), ())), preferred_element_type=F32
        )

    def mix(values, shares):
        return lax.dot_general(
            values,
            shares.astype(BF16),
            (((0,), (0,)), ((), ())),
            preferred_element_type=F32,
        )

    causal = row_iota((SUF, half)) <= (lane_iota((SUF, half)) & (SUF - 1))
    for i in range(CONVS):
        rows = slice(i * SUF, (i + 1) * SUF)
        scores = score(key_new[rows], queries[0, i])
        scores = jnp.where(causal, scores * SCALE, NEGATIVE)
        peak = jnp.max(scores, axis=0, keepdims=True)
        shares = jnp.exp2(scores - peak)
        own_accum[i] = mix(value_new[rows], shares)
        own_stats[i, 0:1, :] = peak
        own_stats[i, 1:2, :] = jnp.sum(shares, axis=0, keepdims=True)
    list_copy.wait()
    for copy in query_out + keys_last:
        copy.wait_recv()
    for copy in kept:
        copy.wait()

    token = row_iota((PAGE, half))

    def attend(head, sides, width):
        def pack(index, state):
            blocks = [index * width + k for k in range(width)]
            codes = [[lists[b * STEP + p, 0] for p in range(STEP)] for b in blocks]
            convs = [jnp.clip(lists[b, 1], 0, CONVS - 1) for b in blocks]
            spots = [[jnp.clip(code >> 7, 0, PAGES - 1) for code in row] for row in codes]
            firsts = [lists[b, 2] == 1 for b in blocks]
            keys = [
                jnp.concatenate([got_k[spot, head] for spot in row], axis=0)
                for row in spots
            ]
            values = [
                jnp.concatenate([got_v[spot, head] for spot in row], axis=0)
                for row in spots
            ]
            pairs = [(k, s) for k in range(width) for s in range(len(sides))]
            scores = {
                (k, s): score(keys[k], queries[sides[s], convs[k]]) for k, s in pairs
            }
            for k, s in pairs:
                scores[k, s] = jnp.concatenate(
                    [
                        jnp.where(
                            token < (codes[k][p] & 127),
                            scores[k, s][p * PAGE : (p + 1) * PAGE] * SCALE,
                            NEGATIVE,
                        )
                        for p in range(STEP)
                    ],
                    axis=0,
                )
            tops = {
                key: jnp.max(value, axis=0, keepdims=True) for key, value in scores.items()
            }
            state = list(state)
            fresh, shrink = {}, {}
            for s in range(len(sides)):
                peak = state[s][0]
                for k in range(width):
                    peak = jnp.where(firsts[k], NEGATIVE, peak)
                    fresh[k, s] = jnp.maximum(peak, tops[k, s])
                    shrink[k, s] = jnp.exp2(peak - fresh[k, s])
                    peak = fresh[k, s]
            shares = {key: jnp.exp2(scores[key] - fresh[key]) for key in pairs}
            sums = {key: jnp.sum(shares[key], axis=0, keepdims=True) for key in pairs}
            mixes = {(k, s): mix(values[k], shares[k, s]) for k, s in pairs}
            for s, side in enumerate(sides):
                peak, total, accum = state[s]
                for k in range(width):
                    total = total * shrink[k, s] + sums[k, s]
                    accum = accum * shrink[k, s] + mixes[k, s]
                    accums[side, blocks[k]] = accum
                    stats[side, blocks[k], 0:1, :] = fresh[k, s]
                    stats[side, blocks[k], 1:2, :] = total
                state[s] = (fresh[width - 1, s], total, accum)
            return tuple(state)

        empty = (
            jnp.full((1, half), NEGATIVE, F32),
            jnp.zeros((1, half), F32),
            jnp.zeros((HD, half), F32),
        )
        lax.fori_loop(0, BLOCKS // width, pack, tuple(empty for _ in sides))

    def result(side, i):
        last = jnp.clip(lists[i, 3], 0, BLOCKS - 1)
        some = lists[i, 4] == 1
        peak = jnp.where(some, stats[side, last, 0:1, :], NEGATIVE)
        total = jnp.where(some, stats[side, last, 1:2, :], 0.0)
        accum = accums[side, last] * jnp.where(some, 1.0, 0.0)
        return peak, total, accum

    def send(side):
        for i in range(CONVS):
            peak, total, accum = result(side, i)
            safe = jnp.where(total > 0.0, total, 1.0)
            mixed_out[side, i] = (accum * (1.0 / safe)).astype(BF16)
            lse = jnp.where(total > 0.0, peak + jnp.log(safe) * (1.0 / LN2), NEGATIVE)
            lse_out[side, i] = jnp.broadcast_to(lse, (8, half))
        copies = [
            remote(
                source.at[side],
                target.at[side],
                send_sem.at[side],
                recv_sem.at[side],
                group,
                x * 4 + partner_z[side],
            )
            for source, target, send_sem, recv_sem in (
                (mixed_out, mixed_got, mixed_send, mixed_recv),
                (lse_out, lse_got, lse_send, lse_recv),
            )
        ]
        for copy in copies:
            copy.start()
        return copies

    attend(1 - own_head, (2,), 10)
    exchanged = send(2)
    attend(1 - own_head, (3,), 10)
    exchanged = exchanged + send(3)

    attend(own_head, (1,), 10)
    exchanged = exchanged + send(1)

    for copy in group_out:
        copy.wait_recv()

    def choose(to, carry):
        page = new_all[jnp.clip(chosen[0, to], 0, GROUPS * CONVS - 1)].astype(F32)
        new_send[to] = (page * chosen[1, to].astype(F32)).astype(BF16)
        return carry

    lax.fori_loop(0, TENSOR, choose, 0)
    mine_copy = pltpu.make_async_copy(
        new_send.at[tensor], new_pages.at[tensor], load_sem.at[6]
    )
    mine_copy.start()

    def page_copy(off):
        to = lax.rem(tensor + off, TENSOR)
        return remote(
            new_send.at[to],
            new_pages.at[tensor],
            page_send.at[off],
            page_recv.at[off],
            group,
            to,
        )

    def page_start(off, carry):
        page_copy(off).start()
        return carry

    lax.fori_loop(1, TENSOR, page_start, 0)
    attend(own_head, (0,), 10)
    for copy in exchanged:
        copy.wait_recv()
    row_of = lane_iota((1, half)) & (SUF - 1)

    def combine(i):
        peak, total, accum = result(0, i)
        own_peak = own_stats[i, 0:1, :]
        logs = [lse_got[r, i, 0:1, :] for r in (1, 2, 3)]
        top = jnp.maximum(
            jnp.maximum(peak, own_peak), jnp.maximum(jnp.maximum(logs[0], logs[1]), logs[2])
        )
        shares = [jnp.exp2(log - top) for log in logs]
        first, second = jnp.exp2(peak - top), jnp.exp2(own_peak - top)
        total = total * first + own_stats[i, 1:2, :] * second
        total = total + shares[0] + shares[1] + shares[2]
        scale = jnp.where(row_of < suffix_ref[conv_ref[group * CONVS + i]], 1.0, 0.0) / total
        joined = accum * (first * scale) + own_accum[i] * (second * scale)
        for r in (1, 2, 3):
            joined = joined + mixed_got[r, i].astype(F32) * (shares[r - 1] * scale)
        turned = jnp.transpose(joined).astype(BF16)
        for head in range(HEADS):
            mixed[i * SUF : (i + 1) * SUF, head * HD : (head + 1) * HD] = turned[
                head * SUF : (head + 1) * SUF, :
            ]

    pending = []

    class Ring:
        def __init__(self, side, first, pick, buffers, way):
            self.side, self.first, self.pick, self.buffers = side, first, pick, buffers
            self.up, self.down, self.me, self.far, self.to_up, self.to_down = way
            self.top = pl.ds(side * 2 * SUF, SUF)
            self.bottom = pl.ds(side * 2 * SUF + SUF, SUF)

        def send(self, index, ref, to):
            sem = self.first + index
            copy = remote(
                ref,
                self.buffers.at[self.side, index],
                ring_send.at[sem],
                ring_recv.at[sem],
                group,
                to,
            )
            copy.start()
            pending.append(copy)
            return copy

        def start_far(self):
            pick = self.pick
            self.c0 = self.send(0, pick(self.far, self.top), self.to_up)
            self.c1 = self.send(1, pick(self.far, self.bottom), self.to_down)

        def start_near(self):
            pick = self.pick
            self.c2 = self.send(2, pick(self.up, self.bottom), self.to_up)
            self.c3 = self.send(3, pick(self.down, self.top), self.to_down)

        def add(self, ref, *indices):
            total = ref[...].astype(F32)
            for index in indices:
                total = total + self.buffers[self.side, index].astype(F32)
            ref[...] = total.astype(BF16)

        def relay(self):
            pick = self.pick
            self.c0.wait_recv()
            self.add(pick(self.up, self.top), 0)
            self.c4 = self.send(4, pick(self.up, self.top), self.to_up)
            self.c1.wait_recv()
            self.add(pick(self.down, self.bottom), 1)
            self.c5 = self.send(5, pick(self.down, self.bottom), self.to_down)

        def finish(self):
            pick = self.pick
            self.c3.wait_recv()
            self.c4.wait_recv()
            self.add(pick(self.me, self.top), 3, 4)
            self.c2.wait_recv()
            self.c5.wait_recv()
            self.add(pick(self.me, self.bottom), 2, 5)

    along_x = (x_up, x_down, x, x_far, to_x_up, to_x_down)
    along_z = (z_up, z_down, z, z_far, to_z_up, to_z_down)
    firsts = (
        Ring(0, 0, lambda j, rows: part.at[j, :, rows], big, along_x),
        Ring(1, 6, lambda j, rows: part.at[:, j, rows], big, along_z),
    )
    seconds = (
        Ring(0, 12, lambda j, rows: part.at[x, j, rows], small, along_z),
        Ring(1, 18, lambda j, rows: part.at[j, z, rows], small, along_x),
    )

    def out_block(bx, bz):
        columns = pl.ds(pl.multiple_of((bx * 4 + bz) * PART, PART), PART)
        part[bx, bz] = jnp.dot(
            mixed[...], weights[:, columns], preferred_element_type=F32
        ).astype(BF16)

    def project_many(pairs):
        for bx, bz in pairs:
            out_block(bx, bz)

    for i in range(CONVS):
        combine(i)
    load_out.wait()
    project_many([(x_far, bz) for bz in (z_far, z_up, z_down, z)])
    firsts[0].start_far()
    project_many([(bx, z_far) for bx in (x_up, x_down, x)])
    firsts[1].start_far()
    project_many([(x_up, z_up), (x_up, z_down), (x_up, z)])
    project_many([(x_down, z_up), (x_down, z_down), (x_down, z)])
    firsts[0].start_near()
    project_many([(x, z_up), (x, z_down), (x, z)])
    firsts[1].start_near()
    firsts[0].relay()
    firsts[1].relay()
    for first, second in zip(firsts, seconds):
        first.finish()
        second.start_far()
        second.start_near()
    seconds[0].relay()
    seconds[1].relay()
    seconds[0].finish()
    seconds[1].finish()
    out_ref[...] = part[x, z]
    for copy in exchanged + pending + sent + pages_out + group_out + query_out + [kv_copy]:
        copy.wait_send()
    mine_copy.wait()

    def page_end(off, carry):
        page_copy(off).wait()
        return carry

    lax.fori_loop(1, TENSOR, page_end, 0)


def place_kernel(part_out, pages, attn_out, new_keys, new_values):
    attn_out[...] = part_out[...]
    new_keys[0] = pages[:, 0]
    new_values[0] = pages[:, 1]


def any_spec():
    return pl.BlockSpec(memory_space=pl.ANY)


def vmem_spec():
    return pl.BlockSpec(memory_space=pltpu.VMEM)


def smem_spec():
    return pl.BlockSpec(memory_space=pltpu.SMEM)


def shards(
    hidden_states,
    norm_gain,
    w_query,
    b_query,
    w_key,
    b_key,
    w_value,
    b_value,
    w_out,
    pool_keys,
    pool_values,
    conv_slots,
    page_table,
    prefix_len,
    suffix_len,
    new_dest,
):
    dma = pltpu.SemaphoreType.DMA
    freq = THETA ** (-(np.arange(HD // 2, dtype=np.float64) * 2.0 / HD))
    freq = jnp.asarray(np.concatenate([freq, freq])[None, :], F32)
    shape = jax.ShapeDtypeStruct
    attn_out, new_pages = pl.pallas_call(
        layer_kernel,
        out_shape=[shape((ROWS, PART), BF16), shape((TENSOR, SUF, HD), BF16)],
        in_specs=[smem_spec()] * 4
        + [vmem_spec()]
        + [any_spec()] * 7
        + [vmem_spec()] * 5,
        out_specs=[vmem_spec(), any_spec()],
        scratch_shapes=[
            pltpu.VMEM((4, 4, ROWS, PART), BF16),
            pltpu.VMEM((WIDTH, HEADS * HD), BF16),
            pltpu.VMEM((HD, WIDTH), BF16),
            pltpu.VMEM((ROWS, HEADS * HD), F32),
            pltpu.VMEM((ROWS, HD), F32),
            pltpu.VMEM((ROWS, HD), F32),
            pltpu.VMEM((GROUPS, 2, 8, PAGE, HD), BF16),
            pltpu.VMEM((4, 2 * GROUPS, 2, PAGE, HD), BF16),
            pltpu.VMEM((PAGES, 2, PAGE, HD), BF16),
            pltpu.VMEM((PAGES, 2, PAGE, HD), BF16),
            pltpu.VMEM((4, CONVS, HEADS * SUF, HD), BF16),
            pltpu.VMEM((ROWS, HD), BF16),
            pltpu.VMEM((ROWS, HD), BF16),
            pltpu.VMEM((ROWS, HD), BF16),
            pltpu.VMEM((ROWS, HD), BF16),
            pltpu.VMEM((GROUPS * CONVS, SUF, HD), BF16),
            pltpu.VMEM((LIST, HD), I32),
            pltpu.SMEM((LIST, HD), I32),
            pltpu.SMEM((2, TENSOR), I32),
            pltpu.VMEM((1, WIDTH), F32),
            pltpu.VMEM((HEADS * HD, WIDTH), BF16),
            pltpu.VMEM((4, BLOCKS, HD, HEADS * SUF), F32),
            pltpu.VMEM((4, BLOCKS, 8, HEADS * SUF), F32),
            pltpu.VMEM((CONVS, HD, HEADS * SUF), F32),
            pltpu.VMEM((CONVS, 8, HEADS * SUF), F32),
            pltpu.VMEM((4, CONVS, HD, HEADS * SUF), BF16),
            pltpu.VMEM((4, CONVS, 8, HEADS * SUF), F32),
            pltpu.VMEM((4, CONVS, HD, HEADS * SUF), BF16),
            pltpu.VMEM((4, CONVS, 8, HEADS * SUF), F32),
            pltpu.VMEM((ROWS, HEADS * HD), BF16),
            pltpu.VMEM((4, 4, ROWS, PART), BF16),
            pltpu.VMEM((2, 6, 4, SUF, PART), BF16),
            pltpu.VMEM((2, 6, SUF, PART), BF16),
            pltpu.VMEM((TENSOR, SUF, HD), BF16),
            dma((8,)),
            dma((2, GROUPS)),
            dma((20,)),
            dma((20,)),
            dma((2, GROUPS)),
            dma((2, GROUPS)),
            dma((2, GROUPS, 4)),
            dma((2, GROUPS, 4)),
            dma((4,)),
            dma((4,)),
            dma((4,)),
            dma((4,)),
            dma((GROUPS,)),
            dma((GROUPS,)),
            dma((4,)),
            dma((4,)),
            dma((4,)),
            dma((4,)),
            dma((24,)),
            dma((24,)),
            dma((TENSOR,)),
            dma((TENSOR,)),
        ],
        compiler_params=pltpu.CompilerParams(
            collective_id=0, has_side_effects=True, vmem_limit_bytes=62 * 1024 * 1024
        ),
        name="layer",
    )(
        conv_slots,
        prefix_len,
        suffix_len,
        new_dest,
        page_table,
        hidden_states,
        pool_keys,
        pool_values,
        w_query,
        w_key.T,
        w_value.T,
        w_out,
        norm_gain,
        b_query,
        b_key,
        b_value,
        freq,
    )
    page_shape = shape((1, TENSOR // 2, SUF, HD), BF16)
    return pl.pallas_call(
        place_kernel,
        out_shape=[shape((ROWS, PART), BF16), page_shape, page_shape],
        in_specs=[vmem_spec()] * 2,
        out_specs=[vmem_spec()] * 3,
        compiler_params=pltpu.CompilerParams(vmem_limit_bytes=62 * 1024 * 1024),
        name="place",
    )(attn_out, new_pages.reshape(TENSOR // 2, 2, SUF, HD))


def solution(mesh):
    in_specs = (
        P("group", "tensor"),
        P(),
        P(None, "tensor"),
        P("tensor"),
        P(None, "tensor"),
        P("tensor"),
        P(None, "tensor"),
        P("tensor"),
        P("tensor", None),
        P(("group", "tensor"), None, None, None),
        P(("group", "tensor"), None, None, None),
        P(),
        P(),
        P(),
        P(),
        P(),
    )
    out_specs = (
        P("group", "tensor"),
        P(("group", "tensor"), None, None, None),
        P(("group", "tensor"), None, None, None),
    )
    return jax.shard_map(shards, mesh=mesh, in_specs=in_specs, out_specs=out_specs, check_vma=False)
```
